32 devices in a mesh: row: 2 (over x), col: 16 (over z, y, core).
Axes of the slice: x: 2, y: 2, z: 4, core: 2. Of those that a mesh axis runs over, the one named last changes fastest.
Arguments:
- image_tokens: bfloat16 [4096, 50, 384], P(('row', 'col')), may hold values from -6 to 6
- text_tokens: bfloat16 [4096, 16, 384], P(('row', 'col')), may hold values from -6 to 6
- lengths: int32 [4096], P(('row', 'col')), may hold values from 1 to 16, as said below
- pair_count: int32 [2, 16], replicated, may hold values from 24 to 128, as said below
- img_qkv: bfloat16 [384, 1152], replicated, may hold values from -0.3125 to 0.3125
- img_out: bfloat16 [384, 384], replicated, may hold values from -0.875 to 0.875
- img_up: bfloat16 [384, 1536], replicated, may hold values from -0.3125 to 0.3125
- img_down: bfloat16 [1536, 384], replicated, may hold values from -0.15625 to 0.15625
- img_proj: bfloat16 [384, 384], replicated, may hold values from -0.3125 to 0.3125
- gain_one: float32 [384], replicated, may hold values from 0.5 to 1.5
- txt_qkv: bfloat16 [384, 1152], replicated, may hold values from -0.3125 to 0.3125
- txt_out: bfloat16 [384, 384], replicated, may hold values from -0.625 to 0.625
- gain_two: float32 [384], replicated, may hold values from 0.5 to 1.5
- txt_up: bfloat16 [384, 1536], replicated, may hold values from -0.3125 to 0.3125
- txt_down: bfloat16 [1536, 384], replicated, may hold values from -0.15625 to 0.15625
- txt_proj: bfloat16 [384, 384], replicated, may hold values from -0.3125 to 0.3125
- log_scale: float32 [1], replicated, may hold values from 3.2 to 3.8
Outputs:
- loss: float32 [1], replicated
- text_grad: bfloat16 [4096, 16, 384], P(('row', 'col'))
- grad_gain_one: float32 [384], replicated
- grad_qkv: float32 [384, 1152], replicated
- grad_out: float32 [384, 384], replicated
- grad_gain_two: float32 [384], replicated
- grad_up: float32 [384, 1536], replicated
- grad_down: float32 [1536, 384], replicated
- grad_proj: float32 [384, 384], replicated
- grad_scale: float32 [1], replicated
The draws below stay inside these ranges and needn't reach their ends.
Inputs may be any that keep to these rules, and one draw needn't show every extreme that they name: `lengths`: every caption has 1 to 16 live tokens; some caption has 16. `pair_count`: A block's live pairs grow with its row index r, from about a quarter of 128 at r = 0 to nearly 128 at the last row index; some block is full.
All inputs are finite; a program needn't handle non-finite values.
Results may differ from the reference program's by a relative error of at most 0.017.
The reference program's roundings to bfloat16 on the way count: a program that leaves them out, or rounds other values in their place, can miss the bound.
Values may be sent and summed in bfloat16 or wider, within the bound.
No kernel may reach another device: no remote copies, remote signals or barrier semaphores. Data moves between devices by JAX's collectives and lax.ppermute only.
A program may use at most 192 MiB of HBM per device.

```python
import math
import jax
import jax.numpy as jnp
from jax import lax

D = 384
HEADS = 6
HEAD = 64
FF = 1536
E = 384
LI = 50
LT = 16
P_DEV = 128
PAIRS = 4096
N_ROW = 2
N_COL = 16


def draw_lengths(key, part):
    key = jax.random.fold_in(key, 11)
    first, second = jax.random.split(key)
    values = jax.random.randint(first, (PAIRS,), 1, LT + 1)
    chosen = jax.random.randint(second, (), 0, PAIRS)
    return jnp.where(jnp.arange(PAIRS) == chosen, LT, values).astype(jnp.int32)


def draw_pair_count(key, part):
    key = jax.random.fold_in(key, 23)
    first, second, third = jax.random.split(key, 3)
    rows = jnp.arange(N_ROW)[:, None]
    cols = jnp.arange(N_COL)[None, :]
    base = P_DEV // 4 + (P_DEV - P_DEV // 4) * rows // (N_ROW - 1)
    jitter = jax.random.randint(first, (N_ROW, N_COL), 0, max(1, P_DEV // 16) + 1)
    lowest = max(1, P_DEV // 4 - P_DEV // 16)
    values = jnp.clip(base - jitter, lowest, P_DEV)
    top_col = jax.random.randint(second, (), 0, N_COL)
    low_col = jax.random.randint(third, (), 0, N_COL)
    values = jnp.where((rows == N_ROW - 1) & (cols == top_col), P_DEV, values)
    values = jnp.where((rows == 0) & (cols == low_col), lowest, values)
    return values.astype(jnp.int32)


def level_of(own_key, extent, cuts, smallest, high):
    loudness = 1.0
    for axis_at, parts in cuts:
        draws = jax.random.uniform(jax.random.fold_in(jax.random.fold_in(own_key, 6), axis_at), (parts,), jnp.float32, smallest / len(cuts), high / len(cuts))
        loudness = loudness * jnp.repeat(jnp.exp(draws), extent[axis_at] // parts).reshape((-1,) + (1,) * (len(extent) - 1 - axis_at))
    return loudness


def gaussian(own_key, dims, spread, most, cuts=(), held_as=jnp.bfloat16):
    array = jax.random.normal(own_key, dims, jnp.float32) * spread
    if len(cuts) > 0:
        array = level_of(own_key, dims, cuts, -0.22, 0.18) * array
    return jnp.clip(array, min=-most, max=most).astype(held_as)


def setup_inputs(seed: int = 0) -> dict:
    seeds = jax.random.split(jax.random.key(seed), 18)
    image_tokens = gaussian(seeds[0], (PAIRS, LI, D), 1.0, 6.0, ((0, 32),))
    text_tokens = gaussian(seeds[1], (PAIRS, LT, D), 1.0, 6.0, ((0, 32),))
    lengths = draw_lengths(jax.random.fold_in(seeds[17], 71), 0)
    pair_count = draw_pair_count(jax.random.fold_in(seeds[17], 71), 0)
    img_qkv = gaussian(seeds[4], (D, 3 * D), D ** -0.5, 0.3125)
    img_out = gaussian(seeds[5], (D, D), (D // 8) ** -0.5, 0.875)
    img_up = gaussian(seeds[6], (D, FF), D ** -0.5, 0.3125)
    img_down = gaussian(seeds[7], (FF, D), FF ** -0.5, 0.15625)
    img_proj = gaussian(seeds[8], (D, E), D ** -0.5, 0.3125)
    gain_one = jnp.clip(1.0 + 0.1 * jax.random.normal(seeds[9], (D,), jnp.float32), 0.5, 1.5)
    txt_qkv = gaussian(seeds[10], (D, 3 * D), D ** -0.5, 0.3125)
    txt_out = gaussian(seeds[11], (D, D), (D // 4) ** -0.5, 0.625)
    gain_two = jnp.clip(1.0 + 0.1 * jax.random.normal(seeds[12], (D,), jnp.float32), 0.5, 1.5)
    txt_up = gaussian(seeds[13], (D, FF), D ** -0.5, 0.3125)
    txt_down = gaussian(seeds[14], (FF, D), FF ** -0.5, 0.15625)
    txt_proj = gaussian(seeds[15], (D, E), D ** -0.5, 0.3125)
    log_scale = jnp.clip(jax.random.uniform(seeds[16], (1,), jnp.float32, 3.2, 3.8), 3.2, 3.8)
    return {"image_tokens": image_tokens, "text_tokens": text_tokens, "lengths": lengths, "pair_count": pair_count, "img_qkv": img_qkv, "img_out": img_out, "img_up": img_up, "img_down": img_down, "img_proj": img_proj, "gain_one": gain_one, "txt_qkv": txt_qkv, "txt_out": txt_out, "gain_two": gain_two, "txt_up": txt_up, "txt_down": txt_down, "txt_proj": txt_proj, "log_scale": log_scale}


epsilon = 1e-06
floor_value = -1e+30
highest = lax.Precision.HIGHEST

@jax.custom_vjp
def low(v):
    return lax.optimization_barrier(v.astype(jnp.bfloat16)).astype(jnp.float32)

@jax.custom_vjp
def low_back(v):
    return v

def low_keep(v):
    return (low(v), None)

def low_pass(kept, grad):
    return (grad,)

def back_keep(v):
    return (v, None)

def back_low(kept, grad):
    return (low(grad),)
low.defvjp(low_keep, low_pass)
low_back.defvjp(back_keep, back_low)

def layer_norm(values):
    centred = values - lax.optimization_barrier(jnp.mean(values, axis=-1, keepdims=True))
    return centred * lax.rsqrt(lax.optimization_barrier(jnp.mean(centred * centred, axis=-1, keepdims=True)) + epsilon)

def matmul(left, right):
    return jnp.einsum('...d,de->...e', left, right, precision=highest)

def unit_vector(values):
    return values * lax.rsqrt(lax.optimization_barrier(jnp.sum(values * values, axis=-1, keepdims=True)) + epsilon)

def attention(mixed, key_mask):
    count, length, _ = mixed.shape
    split = mixed.reshape(count, length, 3, HEADS, HEAD)
    query, keys, values = (split[:, :, 0], split[:, :, 1], split[:, :, 2])
    scores = low_back(jnp.einsum('nqhd,nkhd->nhqk', query, keys, precision=highest) * HEAD ** (-0.5))
    scores = jnp.where(key_mask[:, None, None, :], scores, floor_value)
    peak = lax.optimization_barrier(jnp.max(scores, axis=-1, keepdims=True))
    expo = jnp.exp(scores - peak)
    probs = low(expo / lax.optimization_barrier(jnp.sum(expo, axis=-1, keepdims=True)))
    result = jnp.einsum('nhqk,nkhd->nqhd', probs, values, precision=highest)
    return result.reshape(count, length, HEADS * HEAD)

def image_tower(tokens, w_qkv, w_out, w_up, w_down, w_proj):
    key_mask = jnp.ones(tokens.shape[:2], dtype=bool)
    normed = low(layer_norm(tokens))
    mixed = low(matmul(normed, w_qkv))
    attended = low(attention(mixed, key_mask))
    after = tokens + matmul(attended, w_out)
    hidden = low(jax.nn.gelu(matmul(low(layer_norm(after)), w_up)))
    output = after + matmul(hidden, w_down)
    pooled = low(lax.optimization_barrier(jnp.mean(output, axis=1)))
    return low(unit_vector(matmul(pooled, w_proj)))

def text_tower(tokens, lens, gain_a, w_qkv, w_out, gain_b, w_up, w_down, w_proj):
    length = tokens.shape[1]
    key_mask = jnp.arange(length)[None, :] < lens[:, None]
    normed = low(layer_norm(tokens) * gain_a)
    mixed = low(low_back(matmul(normed, w_qkv)))
    attended = low(low_back(attention(mixed, key_mask)))
    after = tokens + low_back(matmul(attended, w_out))
    normed_two = low(layer_norm(after) * gain_b)
    hidden_pre = low_back(matmul(normed_two, w_up))
    hidden = low(jax.nn.gelu(hidden_pre))
    output = after + low_back(matmul(hidden, w_down))
    weights = key_mask.astype(jnp.float32) / lens[:, None].astype(jnp.float32)
    pooled = low(lax.optimization_barrier(jnp.sum(output * weights[:, :, None], axis=1)))
    embedded = low_back(matmul(pooled, w_proj))
    return low(unit_vector(embedded))

def contrast(image_units, text_units, scale_log, valid, pair_total, row_group):
    scale = jnp.exp(scale_log[0])
    valid_float = valid.astype(jnp.float32)
    blocks = image_units.reshape(PAIRS // row_group, row_group, E)
    block_valid = valid.reshape(PAIRS // row_group, row_group)

    def step(carry, inputs):
        peak_col, total_col = carry
        rows, row_ok = inputs
        sims = scale * low_back(jnp.einsum('ie,je->ij', rows, text_units, precision=highest))
        by_row = jnp.where(valid[None, :], sims, floor_value)
        row_peak = lax.optimization_barrier(jnp.max(by_row, axis=1, keepdims=True))
        row_lse = row_peak[:, 0] + jnp.log(lax.optimization_barrier(jnp.sum(jnp.exp(by_row - row_peak), axis=1)))
        by_col = jnp.where(row_ok[:, None], sims, floor_value)
        new_peak = jnp.maximum(peak_col, lax.optimization_barrier(jnp.max(by_col, axis=0)))
        new_total = total_col * jnp.exp(peak_col - new_peak) + lax.optimization_barrier(jnp.sum(jnp.exp(by_col - new_peak[None, :]), axis=0))
        return ((new_peak, new_total), jnp.sum(jnp.where(row_ok, row_lse, 0.0)))
    start = (jnp.full((PAIRS,), floor_value, jnp.float32), jnp.zeros((PAIRS,), jnp.float32))
    (peak_col, total_col), row_sums = lax.scan(jax.checkpoint(step), start, (blocks, block_valid))
    col_lse = peak_col + jnp.log(total_col)
    diagonal = scale * low_back(lax.optimization_barrier(jnp.sum(image_units * text_units, axis=1)))
    summed = jnp.sum(row_sums) + jnp.sum(valid_float * col_lse) - 2.0 * jnp.sum(valid_float * diagonal)
    return summed / (2.0 * pair_total)

def reference(image_tokens, text_tokens, lengths, pair_count, img_qkv, img_out, img_up, img_down, img_proj, gain_one, txt_qkv, txt_out, gain_two, txt_up, txt_down, txt_proj, log_scale):
    image_group = math.gcd(PAIRS, 64)
    text_group = math.gcd(PAIRS, 256)
    row_group = math.gcd(PAIRS, 1024)
    image_qkv = img_qkv.astype(jnp.float32)
    image_out = img_out.astype(jnp.float32)
    image_up = img_up.astype(jnp.float32)
    image_down = img_down.astype(jnp.float32)
    image_proj = img_proj.astype(jnp.float32)

    def image_block(tokens):
        return image_tower(tokens.astype(jnp.float32), image_qkv, image_out, image_up, image_down, image_proj)
    image_units = lax.map(image_block, image_tokens.reshape(PAIRS // image_group, image_group, LI, D))
    image_units = image_units.reshape(PAIRS, E)
    slots = jnp.arange(PAIRS)
    limits = jnp.repeat(pair_count.reshape(-1), P_DEV)
    valid = slots % P_DEV < limits
    pair_total = jnp.sum(valid.astype(jnp.float32))

    def objective(text_in, gain_a, qkv_w, out_w, gain_b, up_w, down_w, proj_w, scale_log):

        def text_block(inputs):
            tokens, lens = inputs
            return text_tower(tokens, lens, gain_a, qkv_w, out_w, gain_b, up_w, down_w, proj_w)
        grouped = (text_in.reshape(PAIRS // text_group, text_group, LT, D), lengths.reshape(PAIRS // text_group, text_group))
        text_units = lax.map(jax.checkpoint(text_block), grouped).reshape(PAIRS, E)
        return contrast(image_units, text_units, scale_log, valid, pair_total, row_group)
    loss, pullback = jax.vjp(objective, text_tokens.astype(jnp.float32), gain_one, txt_qkv.astype(jnp.float32), txt_out.astype(jnp.float32), gain_two, txt_up.astype(jnp.float32), txt_down.astype(jnp.float32), txt_proj.astype(jnp.float32), log_scale)
    grads = pullback(jnp.ones_like(loss))
    return (loss.reshape(1), grads[0].astype(jnp.bfloat16), grads[1], grads[2], grads[3], grads[4], grads[5], grads[6], grads[7], grads[8])
```

```python
import functools
import jax
import jax.numpy as jnp
from jax import lax
from jax.experimental import pallas as pl
from jax.experimental.pallas import tpu as pltpu
from jax.sharding import PartitionSpec as P

HEADS = 6
HEAD = 64
epsilon = 1e-6
F32 = jnp.float32
BF16 = jnp.bfloat16
GELU_A = 0.7978845608028654
GELU_B = 0.7978845608028654 * 0.044715
SAFE = 60.0
GROUP = 8
IMAGE_NB = 16
USE = 2
ACTIVE = 3
ORDER = 4
ORDER_ALL = 8
IMAGE_BLOCKS = 12
PLAN = 28
NB = 32
QB = 16
T1_LIMIT = 20
T2_LIMIT = 20
BACK_LIMIT = 30
SIM_LIMIT = 12


def mm(a, b):
    return lax.dot_general(a, b, (((1,), (0,)), ((), ())), preferred_element_type=F32)


def mm_t(a, b):
    return lax.dot_general(a, b, (((1,), (1,)), ((), ())), preferred_element_type=F32)


def mm_split(a, b):
    hi = a.astype(BF16)
    lo = (a - hi.astype(F32)).astype(BF16)
    return mm(hi, b) + mm(lo, b)


def normed(v):
    c = v - jnp.mean(v, axis=-1, keepdims=True)
    return c * lax.rsqrt(jnp.mean(c * c, axis=-1, keepdims=True) + epsilon)


def unit_scale(e):
    return lax.rsqrt(jnp.sum(e * e, axis=-1, keepdims=True) + epsilon)


def lane_halves():
    lane = lax.broadcasted_iota(jnp.int32, (1, 128), 1)
    low = (lane < HEAD).astype(F32)
    return low, 1.0 - low


def image_kernel(first, cut, plan_ref, x_ref, recv_ref, wqkv_ref, wout_ref, wup_ref, wdown_ref, wproj_ref, unit_ref, qkv, att, hsum, xsum):
    step = pl.program_id(0)
    length, nb, width = x_ref.shape
    rows = length * GROUP

    @pl.when(step == 0)
    def _():
        qkv[:, :, rows:, :] = jnp.zeros(qkv.shape[:2] + (qkv.shape[2] - rows, 128), F32)
        hsum[...] = jnp.zeros_like(hsum)
        xsum[...] = jnp.zeros_like(xsum)

    block = first // nb + step

    @pl.when(plan_ref[IMAGE_BLOCKS + block * (nb // GROUP)] > 0)
    def _():
        image_block(step, block, cut, plan_ref, x_ref, recv_ref, wqkv_ref, wout_ref, wup_ref, qkv, att, hsum, xsum)

    @pl.when(step == pl.num_programs(0) - 1)
    def _():
        pooled = xsum[...] * (1.0 / length) + mm_split(hsum[...] * (0.5 / length), wdown_ref[...])
        e = mm(pooled.astype(BF16), wproj_ref[...])
        unit_ref[...] = (e * unit_scale(e)).astype(BF16)


def image_block(step, block, cut, plan_ref, x_ref, recv_ref, wqkv_ref, wout_ref, wup_ref, qkv, att, hsum, xsum):
    length, nb, width = x_ref.shape
    rows = length * GROUP
    slots = qkv.shape[2] // GROUP
    tiles = width // 128
    ff = wup_ref.shape[1]
    groups = nb // GROUP
    moved = (plan_ref[USE] > 0) & (block >= cut // nb)

    def tokens(g):
        x = x_ref[...].astype(F32)
        if recv_ref is not None:
            x = jnp.where(moved, recv_ref[...].astype(F32), x)
        return x[:, g * GROUP : (g + 1) * GROUP, :].reshape(rows, width)

    low, high = lane_halves()
    key_row = lax.broadcasted_iota(jnp.int32, (2 * slots, 128), 0)
    key_lane = lax.broadcasted_iota(jnp.int32, (2 * slots, 128), 1)
    own_head = (key_row < slots) == (key_lane < HEAD)
    real = jnp.where(key_row < slots, key_row, key_row - slots) < length
    ones = jnp.where(own_head & real, 1.0, 0.0).astype(BF16)

    def pairs_of(g):
        return pl.ds(pl.multiple_of(step * nb + g * GROUP, GROUP), GROUP)

    def scores(g, p, h):
        at = pl.ds(p, slots, stride=GROUP)
        q = qkv[g, h, at, :].astype(BF16) * BF16(HEAD**-0.5)
        k = qkv[g, tiles + h, at, :]
        return mm_t(q, jnp.concatenate([k * low, k * high], axis=0).astype(BF16))

    def weighted(g, p, h, e):
        at = pl.ds(p, slots, stride=GROUP)
        v = qkv[g, 2 * tiles + h, at, :]
        vbd = jnp.concatenate([v * low, v * high], axis=0).astype(BF16)
        o = mm(e.astype(BF16), jnp.concatenate([vbd, ones], axis=1))
        att[g, h, at, :] = o[:, :128] / o[:, 128:]

    def projected(g):
        n1 = normed(tokens(g)).astype(BF16)
        for c in range(tiles):
            made = mm(n1, wqkv_ref[:, c * width : (c + 1) * width])
            for h in range(tiles):
                qkv[g, c * tiles + h, :rows, :] = made[:, h * 128 : h * 128 + 128]

    def after_attention(g):
        heads = jnp.concatenate([att[g, h, :rows, :] for h in range(tiles)], axis=1)
        x1 = tokens(g) + mm(heads.astype(BF16), wout_ref[...])
        xsum[pairs_of(g), :] = jnp.sum(x1.reshape(length, GROUP, width), axis=0)
        return normed(x1).astype(BF16)

    def gelu_sum(g, u, c):
        made = u * (1.0 + jnp.tanh(u * (GELU_A + GELU_B * (u * u))))
        hsum[pairs_of(g), pl.ds(c, 256)] = jnp.sum(made.reshape(length, GROUP, 256), axis=0)

    def feed_steps(g):
        n2 = after_attention(g)
        before = None
        for c in range(0, ff, 256):
            u = mm(n2, wup_ref[:, c : c + 256])
            if before is not None:
                gelu_sum(g, *before)
            before = (u, c)
            yield
        gelu_sum(g, *before)
        yield

    largest = jnp.zeros((slots, 2 * slots), F32)
    units = [(p, h) for p in range(GROUP) for h in range(tiles)]
    ahead = 3
    feed = iter(())
    projected(0)
    for g in range(groups):
        s_list, e_list = {}, {}
        for k in range(len(units) + 2 * ahead):
            if k < len(units):
                s_list[k] = scores(g, *units[k])
            if 0 <= k - ahead < len(units):
                s = s_list.pop(k - ahead)
                largest = jnp.maximum(largest, jnp.abs(s))
                e_list[k - ahead] = jnp.exp(s)
            if 0 <= k - 2 * ahead < len(units):
                weighted(g, *units[k - 2 * ahead], e_list.pop(k - 2 * ahead))
            if k % 4 == 2:
                next(feed, None)
            if k == len(units) // 2 and g + 1 < groups:
                projected(g + 1)
        for _ in feed:
            pass
        feed = feed_steps(g)
    for _ in feed:
        pass

    @pl.when(jnp.logical_not(jnp.max(largest) <= SAFE))
    def _():
        key = lax.broadcasted_iota(jnp.int32, (1, 2 * slots), 1)
        in_low = key < slots
        for_low = key < length
        for_high = (key >= slots) & (key < slots + length)
        @pl.loop(0, groups)
        def _(g):
            @pl.loop(0, GROUP)
            def _(p):
                @pl.loop(0, tiles)
                def _(h):
                    s = scores(g, p, h)
                    top_low = jnp.max(jnp.where(for_low, s, -1e30), axis=1, keepdims=True)
                    top_high = jnp.max(jnp.where(for_high, s, -1e30), axis=1, keepdims=True)
                    s = jnp.where(for_low | for_high, s, -1e30) - jnp.where(in_low, top_low, top_high)
                    weighted(g, p, h, jnp.exp(s))

        for g in range(groups):
            n2 = after_attention(g)

            @pl.loop(0, ff // 256)
            def _(c):
                at = pl.multiple_of(c * 256, 256)
                gelu_sum(g, mm(n2, wup_ref[:, pl.ds(at, 256)]), at)


def fixed(shape):
    zeros = (0,) * len(shape)
    return pl.BlockSpec(shape, lambda *_: zeros, pipeline_mode=pl.Buffered(1))


def image_tower(plan, tokens, received, first, count, cut, nb, cost, wqkv, wout, wup, wdown, wproj):
    length, _, width = tokens.shape
    slots = -(-length // 8) * 8
    ff = wup.shape[1]
    weights = (wqkv, wout, wup, wdown, wproj)
    at = first // nb
    specs = [pl.BlockSpec((length, nb, width), lambda i, plan: (0, at + i, 0))]
    if received is None:
        kernel = lambda plan_ref, x_ref, *refs: image_kernel(first, cut, plan_ref, x_ref, None, *refs)
        arrays = (tokens,)
    else:
        kernel = functools.partial(image_kernel, first, cut)
        last = received.shape[1] // nb - 1
        specs.append(
            pl.BlockSpec((length, nb, width), lambda i, plan: (0, jnp.clip(at + i - cut // nb, 0, last), 0))
        )
        arrays = (tokens, received)
    return pl.pallas_call(
        kernel,
        grid_spec=pltpu.PrefetchScalarGridSpec(
            num_scalar_prefetch=1,
            grid=(count // nb,),
            in_specs=specs + [fixed(w.shape) for w in weights],
            out_specs=pl.BlockSpec((count, width), lambda i, plan: (0, 0)),
            scratch_shapes=[
                pltpu.VMEM((nb // GROUP, 3 * width // 128, slots * GROUP, 128), F32),
                pltpu.VMEM((nb // GROUP, width // 128, slots * GROUP, 128), F32),
                pltpu.VMEM((count, ff), F32),
                pltpu.VMEM((count, width), F32),
            ],
        ),
        out_shape=jax.ShapeDtypeStruct((count, width), BF16),
        compiler_params=pltpu.CompilerParams(vmem_limit_bytes=60 * 2**20),
        cost_estimate=pl.CostEstimate(
            flops=int(cost * 2 * count * length * width * (4 * width + ff)),
            bytes_accessed=int(cost * (count * length * width * 2 + 4 * 2**20)),
            transcendentals=int(cost * count * length * ff),
        ),
        name="image_block",
    )(plan, *arrays, *weights)


def mm_tn(a, b):
    return lax.dot_general(a, b, (((0,), (0,)), ((), ())), preferred_element_type=F32)


def stats(v):
    c = v - jnp.mean(v, axis=-1, keepdims=True)
    inv = lax.rsqrt(jnp.mean(c * c, axis=-1, keepdims=True) + epsilon)
    return c * inv, inv


def norm_back(g, n, inv):
    return inv * (
        g - jnp.mean(g, axis=-1, keepdims=True) - n * jnp.mean(g * n, axis=-1, keepdims=True)
    )


def staggered(stages, units, ahead):
    kept = [dict() for _ in stages]
    for k in range(len(units) + (len(stages) - 1) * ahead):
        for at, stage in enumerate(stages):
            u = k - at * ahead
            if 0 <= u < len(units):
                made = stage(units[u], *([kept[at - 1].pop(u)] if at else []))
                kept[at][u] = made


def group_loop(stages, rows, width):
    @pl.loop(0, rows // 256)
    def _(half):
        first = half * 2
        units = [(first + g, h) for g in range(2) for h in range(0, width, 128)]
        staggered(stages, units, 1)


def same_pair(length):
    row = lax.broadcasted_iota(jnp.int32, (128, 128), 0) // length
    lane = lax.broadcasted_iota(jnp.int32, (128, 128), 1) // length
    return row == lane


SMEM = pl.BlockSpec(memory_space=pltpu.SMEM)
VMEM = pl.BlockSpec(memory_space=pltpu.VMEM)


def params(limit=60):
    return pltpu.CompilerParams(vmem_limit_bytes=limit * 2**20)


def as_column(row):
    size = row.shape[1]
    diagonal = lax.broadcasted_iota(jnp.int32, (size, size), 0) == lax.broadcasted_iota(jnp.int32, (size, size), 1)
    return jnp.sum(jnp.where(diagonal, row, 0.0), axis=1, keepdims=True)


def as_row(col):
    size = col.shape[0]
    diagonal = lax.broadcasted_iota(jnp.int32, (size, size), 0) == lax.broadcasted_iota(jnp.int32, (size, size), 1)
    return jnp.sum(jnp.where(diagonal, col, 0.0), axis=0, keepdims=True)


def prepare_kernel(cut, place_ref, count_ref, scale_ref, plan_ref, rlive_ref, tlive_ref, scal_ref):
    rows, cols = count_ref.shape
    across = rows - 1
    col = place_ref[0]
    row = place_ref[1]

    def limits(r, c):
        n = count_ref[r, c]
        other = count_ref[r ^ across, c]
        low = r < rows // 2
        balanced = jnp.where(low, n, other) <= cut
        return n, jnp.where(balanced, jnp.where(low, other, 0), n), low & balanced

    def mask(r, c):
        first, last, _ = limits(r, c)
        slot = lax.broadcasted_iota(jnp.int32, (1, 128), 1)
        return jnp.where(slot < jnp.where(slot < cut, first, last), 1.0, 0.0)

    for c in range(cols):
        rlive_ref[c : c + 1, :] = mask(row, c)
    for p in range(rows):
        tlive_ref[p : p + 1, :] = mask(row ^ p, col)
    first, last, use = limits(row, col)
    limit = lambda start: first if start < cut else last
    plan_ref[0] = col
    plan_ref[1] = row
    plan_ref[USE] = use.astype(jnp.int32)
    blocks = 128 // NB
    active = [(b * NB < limit(b * NB)).astype(jnp.int32) for b in range(blocks)]
    count = sum(active)
    before = jnp.int32(0)
    for b in range(blocks):
        plan_ref[ORDER_ALL + jnp.where(active[b] > 0, before, count + b - before)] = b
        before = before + active[b]
    for i in range(blocks):
        plan_ref[ORDER + i] = plan_ref[ORDER_ALL + jnp.minimum(i, count - 1)]
    plan_ref[ACTIVE] = count
    for b in range(128 // GROUP):
        plan_ref[IMAGE_BLOCKS + b] = (b * GROUP < limit(b * GROUP)).astype(jnp.int32)
    total = jnp.int32(0)
    for r in range(rows):
        for c in range(cols):
            total = total + count_ref[r, c]
    index = lax.broadcasted_iota(jnp.int32, (8, 128), 0)
    scal_ref[...] = jnp.where(index == 0, jnp.exp(jnp.full((8, 128), scale_ref[0], F32)), 0.5 / jnp.full((8, 128), total, jnp.int32).astype(F32))


def prepare(place, pair_count, log_scale, cut):
    rows, cols = pair_count.shape
    return pl.pallas_call(
        functools.partial(prepare_kernel, cut),
        in_specs=[SMEM] * 3,
        out_specs=[SMEM, VMEM, VMEM, VMEM],
        out_shape=[
            jax.ShapeDtypeStruct((PLAN,), jnp.int32),
            jax.ShapeDtypeStruct((cols, 128), F32),
            jax.ShapeDtypeStruct((rows, 128), F32),
            jax.ShapeDtypeStruct((8, 128), F32),
        ],
        name="prepare",
    )(place, pair_count, log_scale)


def lengths_of(plan_ref, cut, part, lens_ref, got_ref):
    moved = (plan_ref[USE] > 0) & (part * QB >= cut)
    got = got_ref[pl.ds(jnp.maximum(part - cut // QB, 0), 1), :]
    return as_column(jnp.where(moved, got, lens_ref[pl.ds(part, 1), :]))


def block_lengths(plan_ref, cut, block, lens_ref, got_ref):
    parts = [lengths_of(plan_ref, cut, block * (NB // QB) + k, lens_ref, got_ref) for k in range(NB // QB)]
    return jnp.concatenate(parts, axis=0)


def all_lengths(plan_ref, cut, lens_ref, got_ref):
    parts = [lengths_of(plan_ref, cut, b, lens_ref, got_ref) for b in range(lens_ref.shape[0])]
    return jnp.concatenate(parts, axis=0)


def live_pick(lens, rows):
    pairs = lens.shape[0]
    length = rows // pairs
    token = lax.broadcasted_iota(jnp.int32, (pairs, rows), 1)
    own = token // length == lax.broadcasted_iota(jnp.int32, (pairs, rows), 0)
    return jnp.where(own & ((token % length).astype(F32) < lens), 1.0, 0.0)


def text_tokens_of(plan_ref, cut, block, x_ref, recv_ref):
    nb, length, width = x_ref.shape
    moved = (plan_ref[USE] > 0) & (block * nb >= cut)
    x = jnp.where(moved, recv_ref[...].astype(F32), x_ref[...].astype(F32))
    return x.reshape(nb * length, width)


def ordered(width, rows):
    return pl.BlockSpec((rows, width), lambda i, plan: (plan[ORDER + i], 0))


def ordered_pairs(shape, order=ORDER):
    return pl.BlockSpec((NB,) + shape[1:], lambda i, plan: (plan[order + i], 0, 0))


def held(shape):
    zeros = (0,) * len(shape)
    return pl.BlockSpec(shape, lambda i, plan: zeros)


def text_first_kernel(cut, plan_ref, x_ref, recv_ref, lens_ref, got_ref, gain_ref, wqkv_ref, wout_ref, qkv_ref, att_ref, y1_ref):
    step = pl.program_id(0)
    block = plan_ref[ORDER + step]

    @pl.when(step < plan_ref[ACTIVE])
    def _():
        x = text_tokens_of(plan_ref, cut, block, x_ref, recv_ref)
        lens = block_lengths(plan_ref, cut, block, lens_ref, got_ref)
        text_attention(x, lens, x_ref.shape[1], gain_ref, wqkv_ref, wout_ref, qkv_ref, att_ref, y1_ref)


def text_attention(x, lens, length, gain_ref, wqkv_ref, wout_ref, qkv_ref, att_ref, y1_ref):
    rows, width = x.shape
    n1 = (normed(x) * gain_ref[...]).astype(BF16)
    for c in range(3):
        at = slice(c * width, (c + 1) * width)
        qkv_ref[:, at] = mm(n1, wqkv_ref[:, at]).astype(BF16)
    lane = lax.broadcasted_iota(jnp.int32, (128, 128), 1)
    low = (lane[:1] < HEAD).astype(BF16)
    high = 1 - low
    half = lax.broadcasted_iota(jnp.int32, (256, 128), 0) < 128
    ones = jnp.where(half == (lax.broadcasted_iota(jnp.int32, (256, 128), 1) < HEAD), 1.0, 0.0).astype(BF16)
    same = same_pair(length)
    live = jnp.sum(live_pick(lens, rows), axis=0, keepdims=True)
    bias = {g: jnp.where(same & (live[:, g : g + 128] > 0), 0.0, -1e30) for g in range(0, rows, 128)}

    def scores(unit):
        g, h = unit
        q = qkv_ref[g : g + 128, h : h + 128] * BF16(HEAD**-0.5)
        k = qkv_ref[g : g + 128, width + h : width + h + 128]
        return mm_t(q, jnp.concatenate([k * low, k * high], axis=0))

    def expo(unit, s):
        one = bias[unit[0]]
        parts = [s[:, :128] + one, s[:, 128:] + one]
        return jnp.concatenate([jnp.exp(p - jnp.max(p, axis=1, keepdims=True)) for p in parts], axis=1).astype(BF16)

    def weighted(unit, e):
        g, h = unit
        v = qkv_ref[g : g + 128, 2 * width + h : 2 * width + h + 128]
        vbd = jnp.concatenate([v * low, v * high], axis=0)
        o = mm(e, jnp.concatenate([vbd, ones], axis=1))
        att_ref[g : g + 128, h : h + 128] = (o[:, :128] / o[:, 128:]).astype(BF16)

    staggered([scores, expo, weighted], [(g, h) for g in range(0, rows, 128) for h in range(0, width, 128)], 1)
    y1_ref[...] = x + mm(att_ref[...], wout_ref[...])


def text_first(plan, x, received, lens, got, cut, gain_one, wqkv, wout):
    pairs, length, width = x.shape
    rows = NB * length
    tokens = pairs * length
    rest = (received, lens, got, gain_one, wqkv, wout)
    wide = [(3 * width, BF16), (width, BF16), (width, F32)]
    return pl.pallas_call(
        functools.partial(text_first_kernel, cut),
        grid_spec=pltpu.PrefetchScalarGridSpec(
            num_scalar_prefetch=1,
            grid=(pairs // NB,),
            in_specs=[ordered_pairs(x.shape)] + [fixed(w.shape) for w in rest],
            out_specs=[ordered(w, rows) for w, _ in wide],
        ),
        out_shape=[(pltpu.HBM if k == 0 else jax.ShapeDtypeStruct)((tokens, w), kind) for k, (w, kind) in enumerate(wide)],
        compiler_params=params(T1_LIMIT),
        cost_estimate=pl.CostEstimate(flops=2 * tokens * width * 5 * width, bytes_accessed=12 * 2**20, transcendentals=0),
        name="text_attention",
    )(plan, x, *rest)


def text_second_kernel(
    cut, plan_ref, y1_ref, lens_ref, got_ref, gain_two_ref, wup_ref, wdown_ref, wproj_ref,
    slope_ref, hsum_ref, pooled_ref, emb_ref, low_ref, ysum,
):
    step = pl.program_id(0)
    block = plan_ref[ORDER + step]

    @pl.when(step == 0)
    def _():
        hsum_ref[...] = jnp.zeros_like(hsum_ref)
        ysum[...] = jnp.zeros_like(ysum)

    @pl.when(step < plan_ref[ACTIVE])
    def _():
        rows = y1_ref.shape[0]
        y1 = y1_ref[...]
        pick = live_pick(block_lengths(plan_ref, cut, block, lens_ref, got_ref), rows).astype(BF16)
        pair = pl.ds(pl.multiple_of(block * NB, NB), NB)
        y1_hi = y1.astype(BF16)
        ysum[pair, :] = mm(pick, y1_hi) + mm(pick, (y1 - y1_hi.astype(F32)).astype(BF16))
        n2 = (normed(y1) * gain_two_ref[...]).astype(BF16)

        live = mm_tn(pick, jnp.ones((NB, 128), BF16))
        live = jnp.concatenate([live, live], axis=1)

        def gelu_parts(u, c):
            square = u * u
            t = 1.0 + jnp.tanh(u * (GELU_A + GELU_B * square))
            half = 0.5 * u
            hsum_ref[pair, c : c + 256] = mm(pick, (half * t).astype(BF16))
            d = t * (0.5 + (2.0 - t) * (half * (GELU_A + (3.0 * GELU_B) * square)))
            slope_ref[:, c : c + 256] = (d * live).astype(BF16)

        in_chunks(n2, wup_ref, gelu_parts)

    @pl.when(step == pl.num_programs(0) - 1)
    def _():
        inv_len = 1.0 / all_lengths(plan_ref, cut, lens_ref, got_ref)
        pooled = (ysum[...] * inv_len + mm_split(hsum_ref[...] * inv_len, wdown_ref[...])).astype(BF16)
        pooled_ref[...] = pooled
        e = mm(pooled, wproj_ref[...])
        emb_ref[...] = e
        low_ref[...] = (e * unit_scale(e)).astype(BF16)


def in_chunks(left, right_ref, use):
    before = None
    for c in range(0, right_ref.shape[1], 256):
        u = mm(left, right_ref[:, c : c + 256])
        if before is not None:
            use(*before)
        before = (u, c)
    use(*before)


def text_second(plan, y1, lens, got, cut, gain_two, wup, wdown, wproj):
    tokens, width = y1.shape
    pairs = lens.size
    rows = NB * tokens // pairs
    ff = wup.shape[1]
    rest = (lens, got, gain_two, wup, wdown, wproj)
    flat = [((pairs, ff), F32), ((pairs, width), BF16), ((pairs, width), F32), ((pairs, width), BF16)]
    return pl.pallas_call(
        functools.partial(text_second_kernel, cut),
        grid_spec=pltpu.PrefetchScalarGridSpec(
            num_scalar_prefetch=1,
            grid=(pairs // NB,),
            in_specs=[ordered(width, rows)] + [fixed(w.shape) for w in rest],
            out_specs=[ordered(ff, rows)] + [held(shape) for shape, _ in flat],
            scratch_shapes=[pltpu.VMEM((pairs, width), F32)],
        ),
        out_shape=[jax.ShapeDtypeStruct((tokens, ff), BF16)] + [jax.ShapeDtypeStruct(shape, kind) for shape, kind in flat],
        compiler_params=params(T2_LIMIT),
        cost_estimate=pl.CostEstimate(flops=2 * tokens * width * ff, bytes_accessed=12 * 2**20, transcendentals=tokens * ff),
        name="text_pool",
    )(plan, y1, *rest)


def image_groups(image_refs):
    for j, ref in enumerate(image_refs):
        yield j, ref.shape[0] // 128, len(image_refs), ref[...]


def sums_kernel(rows, ids_ref, scal_ref, tlive_ref, rlive_ref, *refs):
    text_refs = refs[:rows]
    image_refs = refs[rows:-2]
    rowsum_ref, colsum_ref = refs[-2:]
    me = ids_ref[0]
    scale = scal_ref[:1, :1]
    text = jnp.concatenate([ref[...] for ref in text_refs], axis=0)
    tlive = jnp.concatenate([as_column(tlive_ref[p : p + 1, :]) for p in range(rows)], axis=0)
    col = jnp.zeros((rows * 128, 1), F32)
    for j, high, low, images in image_groups(image_refs):
        e = jnp.exp(scale * mm_t(text, images)) * tlive
        total = jnp.sum(e, axis=0, keepdims=True)
        kept = jnp.zeros((rows * 128, 128), F32)
        for i in range(high):
            at = pl.ds(me ^ (low * i + j), 1)
            rowsum_ref[at, :] = total[:, i * 128 : i * 128 + 128]
            kept = kept + e[:, i * 128 : i * 128 + 128] * rlive_ref[at, :]
        col = col + jnp.sum(kept, axis=1, keepdims=True)
    for p in range(rows):
        colsum_ref[p : p + 1, :] = as_row(col[p * 128 : p * 128 + 128])


def sim_sums(ids, scal, texts, tlive, rlive, images):
    cols = rlive.shape[0]
    rows = len(texts)
    return pl.pallas_call(
        functools.partial(sums_kernel, rows),
        in_specs=[SMEM] + [VMEM] * (3 + rows + len(images)),
        out_specs=[VMEM, VMEM],
        out_shape=[jax.ShapeDtypeStruct((cols, 128), F32), jax.ShapeDtypeStruct((rows, 128), F32)],
        compiler_params=params(SIM_LIMIT),
        cost_estimate=pl.CostEstimate(
            flops=2 * rows * 128 * cols * 128 * 384, bytes_accessed=cols * 128 * 768, transcendentals=rows * cols * 128 * 128
        ),
        name="similarity_sums",
    )(ids, scal, tlive, rlive, *texts, *images)


def grad_kernel(rows, ids_ref, scal_ref, tlive_ref, rlive_ref, rowsum_ref, colsum_ref, *refs):
    text_refs = refs[:rows]
    image_refs = refs[rows : -rows - 1]
    dun_refs = refs[-rows - 1 : -1]
    stat_ref = refs[-1]
    me = ids_ref[0]
    scale = scal_ref[:1, :1]
    inv = scal_ref[1:2, :1]
    text = jnp.concatenate([ref[...] for ref in text_refs], axis=0)
    tlive = jnp.concatenate([as_column(tlive_ref[p : p + 1, :]) for p in range(rows)], axis=0)
    col = jnp.concatenate([as_column(colsum_ref[p : p + 1, :]) for p in range(rows)], axis=0)
    col = jnp.where(tlive > 0, col, 1.0)
    col_inv = inv / col
    total = jnp.zeros(text.shape, F32)
    moved = jnp.zeros((1, 128), F32)
    for j, high, low, images in image_groups(image_refs):
        s = scale * mm_t(text, images)
        e = jnp.exp(s) * tlive
        at = [pl.ds(me ^ (low * i + j), 1) for i in range(high)]
        rlive = jnp.concatenate([rlive_ref[one, :] for one in at], axis=1)
        row_inv = jnp.concatenate([inv / rowsum_ref[one, :] for one in at], axis=1)
        ds = (e * rlive) * (row_inv + col_inv)
        by_lane = jnp.sum(ds * s, axis=0, keepdims=True)
        for i in range(high):
            moved = moved + by_lane[:, i * 128 : i * 128 + 128]
        total = total + mm((scale * ds).astype(BF16), images)
        if j == 0:
            mine = images[:128].astype(F32)
    own_live = tlive[:128]
    cosine = jnp.sum(mine * text[:128].astype(F32), axis=1, keepdims=True)
    live_cosine = jnp.sum(cosine * own_live, axis=0, keepdims=True)
    at = pl.ds(me, 1)
    logs = jnp.sum(jnp.log(rowsum_ref[at, :]) * rlive_ref[at, :], axis=1, keepdims=True)
    logs = logs + jnp.sum(jnp.log(col[:128]) * own_live, axis=0, keepdims=True)
    loss = inv * (logs - 2.0 * scale * live_cosine)
    scale_part = jnp.sum(moved, axis=1, keepdims=True) - 2.0 * inv * scale * live_cosine
    dun_refs[0][...] = total[:128] + (scale * (-2.0 * inv * own_live)).astype(BF16).astype(F32) * mine
    for p in range(1, rows):
        dun_refs[p][...] = total[p * 128 : p * 128 + 128].astype(BF16)
    lane = lax.broadcasted_iota(jnp.int32, (8, 128), 1)
    stat_ref[...] = jnp.where(lane == 0, loss, jnp.where(lane == 1, scale_part, 0.0))


def sim_grads(ids, scal, texts, tlive, rlive, rowsum, colsum, images):
    cols = rlive.shape[0]
    rows = len(texts)
    return pl.pallas_call(
        functools.partial(grad_kernel, rows),
        in_specs=[SMEM] + [VMEM] * (5 + rows + len(images)),
        out_specs=[VMEM] * (rows + 1),
        out_shape=[jax.ShapeDtypeStruct(text.shape, BF16 if k else F32) for k, text in enumerate(texts)] + [jax.ShapeDtypeStruct((8, 128), F32)],
        compiler_params=params(SIM_LIMIT),
        cost_estimate=pl.CostEstimate(
            flops=4 * rows * 128 * cols * 128 * 384, bytes_accessed=cols * 128 * 768, transcendentals=rows * cols * 128 * 128
        ),
        name="similarity_grads",
    )(ids, scal, tlive, rlive, rowsum, colsum, *texts, *images)


def write_halves(core, blocks, keep_ref, send_ref):
    half = len(blocks) // 2
    size = blocks[0].shape[0]

    def put(first, second):
        for at, (kept, sent) in enumerate(zip(first, second)):
            keep_ref[at * size : (at + 1) * size, :] = kept.astype(BF16)
            send_ref[at * size : (at + 1) * size, :] = sent.astype(BF16)

    @pl.when(core == 0)
    def _():
        put(blocks[:half], blocks[half:])

    @pl.when(core != 0)
    def _():
        put(blocks[half:], blocks[:half])


def back_kernel(
    cut, others, plan_ref, x_ref, qkv_ref, att_ref, y1_ref, slope_ref, recv_ref, lens_ref, got_ref,
    dun_ref, emb_ref, pooled_ref, hsum_ref, gain_ref, wqkv_ref, wout_ref, gain_two_ref, wup_ref, wdown_ref, wproj_ref, *refs,
):
    other_refs = refs[:others]
    stat_ref = refs[others]
    grad_ref, keep_a, send_a, keep_b, send_b, keep_c, send_c = refs[others + 1 : others + 8]
    dyp, dhp, dproj, ddown, dmix, dheads, acc_up, acc_out, acc_qkv, bias_ref = refs[others + 8 :]
    step = pl.program_id(0)
    block = plan_ref[ORDER + step]
    active = step < plan_ref[ACTIVE]
    width = dun_ref.shape[1]
    ff = hsum_ref.shape[1]

    @pl.when(step == 0)
    def _():
        acc_up[...] = jnp.zeros_like(acc_up)
        acc_out[...] = jnp.zeros_like(acc_out)
        acc_qkv[...] = jnp.zeros_like(acc_qkv)
        g = dun_ref[...]
        for other in other_refs:
            g = g + other[...].astype(F32)
        e = emb_ref[...]
        inv = unit_scale(e)
        t = e * inv
        demb = (inv * (g - t * jnp.sum(g * t, axis=-1, keepdims=True))).astype(BF16)
        dproj[...] = mm_tn(pooled_ref[...], demb)
        back = mm_t(demb, wproj_ref[...]) * (1.0 / all_lengths(plan_ref, cut, lens_ref, got_ref))
        dyp[...] = back
        db = back.astype(BF16)
        dhp[...] = mm_t(db, wdown_ref[...])
        h = hsum_ref[...]
        hi = h.astype(BF16)
        lo = (h - hi.astype(F32)).astype(BF16)
        ddown[...] = mm_tn(hi, db) + mm_tn(lo, db)

    @pl.when(active)
    def _():
        x = text_tokens_of(plan_ref, cut, block, x_ref, recv_ref)
        lens = block_lengths(plan_ref, cut, block, lens_ref, got_ref)
        grad = back_block(
            block, x, lens, x_ref.shape[1], qkv_ref, att_ref, y1_ref, slope_ref, gain_ref, wqkv_ref, wout_ref,
            gain_two_ref, wup_ref, dyp, dhp, dmix, dheads, acc_up, acc_out, acc_qkv, bias_ref,
        )
        grad_ref[...] = grad.astype(BF16).reshape(grad_ref.shape)

    @pl.when(jnp.logical_not(active))
    def _():
        grad_ref[...] = jnp.zeros_like(grad_ref)

    @pl.when(step == pl.num_programs(0) - 1)
    def _():
        core = plan_ref[0] & 1
        index = lax.broadcasted_iota(jnp.int32, (128, width), 0)
        stat = jnp.concatenate([stat_ref[:1, :]] * (width // 128), axis=1)
        by_qkv = jnp.sum(acc_qkv[...] * wqkv_ref[...].astype(F32), axis=1, keepdims=True)
        by_up = jnp.sum(acc_up[...] * wup_ref[...].astype(F32), axis=1, keepdims=True)
        first = as_row(by_qkv) / gain_ref[...]
        second = as_row(by_up) / gain_two_ref[...]
        small = jnp.where(index == 0, first, jnp.where(index == 1, second, jnp.where(index == 2, stat, 0.0)))
        blocks = [ddown[at : at + 128, :] for at in range(0, ff, 128)]
        blocks += [dproj[at : at + 128, :] for at in range(0, width, 128)]
        write_halves(core, blocks + [small], keep_a, send_a)
        write_halves(core, [acc_up[:, c : c + width] for c in range(0, ff, width)], keep_b, send_b)
        blocks = [acc_out[...]] + [acc_qkv[:, c * width : (c + 1) * width] for c in range(3)]
        write_halves(core, blocks, keep_c, send_c)


def back_block(
    block, x, lens, length, qkv_ref, att_ref, y1_ref, slope_ref, gain_ref, wqkv_ref, wout_ref,
    gain_two_ref, wup_ref, dyp, dhp, dmix, dheads, acc_up, acc_out, acc_qkv, bias_ref,
):
    rows, width = x.shape
    ff = wup_ref.shape[1]
    pair = pl.ds(pl.multiple_of(block * NB, NB), NB)

    def spread(values):
        return jnp.broadcast_to(values[:, None, :], (NB, length, values.shape[1])).reshape(rows, values.shape[1])

    n2, inv = stats(y1_ref[...])
    n2_low = (n2 * gain_two_ref[...]).astype(BF16)
    dn2 = jnp.zeros((rows, width), F32)
    for c in range(0, ff, width):
        at = slice(c, c + width)
        du = (spread(dhp[pair, at]) * slope_ref[:, at].astype(F32)).astype(BF16)
        acc_up[:, at] += mm_tn(n2_low, du)
        dn2 = dn2 + mm_t(du, wup_ref[:, at])
    live = mm_tn(live_pick(lens, rows).astype(BF16), jnp.ones((NB, 128), BF16))
    dy1 = spread(dyp[pair, :]) * jnp.concatenate([live] * (width // 128), axis=1)
    dy1 = dy1 + norm_back(dn2 * gain_two_ref[...], n2, inv)
    da = dy1.astype(BF16)
    acc_out[...] += mm_tn(att_ref[...], da)
    dheads[...] = mm_t(da, wout_ref[...]).astype(BF16)
    attention_grads(length, live, qkv_ref, dmix, dheads, bias_ref)
    n1, inv = stats(x)
    n1_low = (n1 * gain_ref[...]).astype(BF16)
    dn1 = jnp.zeros((rows, width), F32)
    for c in range(3):
        at = slice(c * width, (c + 1) * width)
        acc_qkv[:, at] += mm_tn(n1_low, dmix[:, at])
        dn1 = dn1 + mm_t(dmix[:, at], wqkv_ref[:, at])
    return dy1 + norm_back(dn1 * gain_ref[...], n1, inv)


def attention_grads(length, live, qkv_ref, dmix, dheads, bias_ref):
    rows, width = dheads.shape
    lane = lax.broadcasted_iota(jnp.int32, (128, 128), 1)
    first = lane < HEAD
    low = first[:1].astype(BF16)
    high = 1 - low
    eye = (lane == lax.broadcasted_iota(jnp.int32, (128, 128), 0)).astype(BF16)
    same = same_pair(length)
    for g in range(rows // 128):
        bias_ref[g] = jnp.where(same & (live[g * 128 : g * 128 + 128, :] > 0), 0.0, -1e30)

    def pieces(unit, part):
        g, h = unit
        return qkv_ref[pl.ds(g * 128, 128), part * width + h : part * width + h + 128]

    def scores(unit):
        g, h = unit
        k = pieces(unit, 1)
        v = pieces(unit, 2)
        do = dheads[pl.ds(g * 128, 128), h : h + 128]
        kbd = jnp.concatenate([k * low, k * high], axis=0)
        vbd = jnp.concatenate([v * low, v * high], axis=0)
        s = mm_t(kbd, pieces(unit, 0) * BF16(HEAD**-0.5))
        return s, mm_t(vbd, do)

    def soft(unit, made):
        g, _ = unit
        s, dp = made
        s = s.reshape(2, 128, 128) + bias_ref[g][None]
        e = jnp.exp(s - jnp.max(s, axis=1, keepdims=True))
        p = e * (1.0 / jnp.sum(e, axis=1, keepdims=True))
        dp = dp.reshape(2, 128, 128)
        ds = p * (dp - jnp.sum(p * dp, axis=1, keepdims=True))
        return p.reshape(256, 128).astype(BF16), ds.reshape(256, 128).astype(BF16)

    def products(unit, made):
        g, h = unit
        p, ds = made
        at = pl.ds(g * 128, 128)
        do = dheads[at, h : h + 128]
        dv = mm(p, do)
        dmix[at, 2 * width + h : 2 * width + h + 128] = jnp.where(first, dv[:128], dv[128:]).astype(BF16)
        dk = mm(ds, pieces(unit, 0) * BF16(HEAD**-0.5))
        dmix[at, width + h : width + h + 128] = jnp.where(first, dk[:128], dk[128:]).astype(BF16)
        return mm_t(eye, ds).astype(BF16)

    def query(unit, ds):
        g, h = unit
        k = pieces(unit, 1)
        kbd = jnp.concatenate([k * low, k * high], axis=0)
        dmix[pl.ds(g * 128, 128), h : h + 128] = (mm(ds, kbd) * HEAD**-0.5).astype(BF16)

    group_loop([scores, soft, products, query], rows, width)


def text_backward(
    plan, x, qkv, att, y1, slopes, received, lens, got, cut, dun, emb, pooled, hsum,
    gain_one, wqkv, wout, gain_two, wup, wdown, wproj, others, stat,
):
    pairs, length, width = x.shape
    rows = NB * length
    tokens = pairs * length
    ff = wup.shape[1]
    rest = (received, lens, got, dun, emb, pooled, hsum, gain_one, wqkv, wout, gain_two, wup, wdown, wproj, *others, stat)
    halves = [(ff + width + 128) // 2, ff // 2, 2 * width]
    shapes = [(half, width) for half in halves for _ in range(2)]
    return pl.pallas_call(
        functools.partial(back_kernel, cut, len(others)),
        grid_spec=pltpu.PrefetchScalarGridSpec(
            num_scalar_prefetch=1,
            grid=(pairs // NB,),
            in_specs=[ordered_pairs(x.shape), ordered(3 * width, rows), ordered(width, rows), ordered(width, rows), ordered(ff, rows)]
            + [fixed(w.shape) for w in rest],
            out_specs=[ordered_pairs(x.shape, ORDER_ALL)] + [held(shape) for shape in shapes],
            scratch_shapes=[
                pltpu.VMEM((pairs, width), F32),
                pltpu.VMEM((pairs, ff), F32),
                pltpu.VMEM((width, width), F32),
                pltpu.VMEM((ff, width), F32),
                pltpu.VMEM((rows, 3 * width), BF16),
                pltpu.VMEM((rows, width), BF16),
                pltpu.VMEM((width, ff), F32),
                pltpu.VMEM((width, width), F32),
                pltpu.VMEM((width, 3 * width), F32),
                pltpu.VMEM((rows // 128, 128, 128), F32),
            ],
        ),
        out_shape=[pltpu.HBM(x.shape, BF16)] + [pltpu.HBM(shape, BF16) for shape in shapes],
        compiler_params=params(BACK_LIMIT),
        cost_estimate=pl.CostEstimate(
            flops=2 * tokens * width * (10 * width + 2 * ff), bytes_accessed=24 * 2**20, transcendentals=0
        ),
        name="text_backward",
    )(plan, x, qkv, att, y1, slopes, *rest)


def flip(values, axis, bits):
    size = lax.axis_size(axis)
    return lax.ppermute(values, axis, [(k, k ^ bits) for k in range(size)])


def reduce_round(kept, axis, unit, ways, split):
    if not split:
        low = kept.astype(BF16)
        others = [flip(low, axis, p * unit).astype(F32) for p in range(1, ways)]
        return tree_sum([low.astype(F32)] + others)
    me = (lax.axis_index(axis) // unit) % ways
    pieces = kept.reshape(ways, kept.shape[0] // ways, kept.shape[1])
    total = lax.dynamic_index_in_dim(pieces, me, 0, keepdims=False)
    for p in range(1, ways):
        piece = lax.dynamic_index_in_dim(pieces, me ^ p, 0, keepdims=False)
        total = total + flip(piece.astype(BF16), axis, p * unit).astype(F32)
    return total


def gather_round(piece, axis, unit, ways, split):
    if not split:
        return piece
    return jnp.concatenate([piece] + [flip(piece, axis, p * unit) for p in range(1, ways)], axis=0)


def exchange(keep, send, rounds, back=None):
    kept = keep.astype(F32) + flip(send, "col", 1).astype(F32)
    for one in rounds:
        kept = reduce_round(kept, *one)
    piece = kept.astype(BF16)
    if back is not None:
        piece = tie(piece, back)
    for one in reversed(rounds):
        piece = gather_round(piece, *one)
    return piece, flip(piece, "col", 1)


def tie(first, *others):
    return lax.optimization_barrier((first, *others))[0]


def tree_sum(parts):
    while len(parts) > 1:
        parts = [parts[k] + parts[k + 1] for k in range(0, len(parts), 2)]
    return parts[0]


def sum_over(values, axis, unit, ways):
    return tree_sum([values] + [flip(values, axis, p * unit) for p in range(1, ways)])


def place_kernel(targets, rounds, last, ids_ref, own_ref, other_ref, *outs):
    col = ids_ref[0]
    row = ids_ref[1]
    half, width = own_ref.shape
    steps = []
    size = half
    for axis, unit, ways, split in rounds:
        if split:
            size //= ways
            steps.append((axis, unit, ways, size))
    count = half // size
    places = outs[: len(targets) - 1] + outs[-1:] if last else outs
    for other, source in enumerate((own_ref, other_ref)):

        @pl.loop(0, count)
        def _(k):
            start = ((col & 1) ^ other) * half
            left = k
            weight = count
            for axis, unit, ways, step in steps:
                weight //= ways
                digit = left // weight
                left = left - digit * weight
                index = (col if axis == "col" else row) // unit % ways
                start = start + (index ^ digit) * step
            value = source[pl.ds(pl.multiple_of(k * size, 16), size), :].astype(F32)
            for first, past, by_row, ref in [target + (ref,) for target, ref in zip(targets, places)]:

                @pl.when((start >= first) & (start < past))
                def _():
                    inside = start - first
                    if by_row:
                        ref[pl.ds(pl.multiple_of(inside, 8), size), :] = value
                    else:
                        lane = pl.multiple_of((inside // width) * width, 128)
                        ref[pl.ds(pl.multiple_of(inside % width, 8), size), pl.ds(lane, width)] = value

    if last:
        first_gain, second_gain, loss, moved, small = outs[-5:]
        first_gain[...] = small[0, :]
        second_gain[...] = small[1, :]
        lane = lax.broadcasted_iota(jnp.int32, (1, 128), 1)
        stat = small[2:3, :128]
        loss[0] = jnp.sum(jnp.where(lane == 0, stat, 0.0))
        moved[0] = jnp.sum(jnp.where(lane == 1, stat, 0.0))


def place(ids, gathered, targets, rounds, shapes, last=False):
    width = gathered[0].shape[1]
    specs = [VMEM] * len(shapes)
    made = [jax.ShapeDtypeStruct(shape, F32) for shape in shapes]
    scratch = []
    if last:
        specs = specs + [VMEM, VMEM, SMEM, SMEM]
        made = made + [jax.ShapeDtypeStruct((size,), F32) for size in (width, width, 1, 1)]
        scratch = [pltpu.VMEM((128, width), F32)]
    return pl.pallas_call(
        functools.partial(place_kernel, targets, rounds, last),
        in_specs=[SMEM, VMEM, VMEM],
        out_specs=specs,
        out_shape=made,
        scratch_shapes=scratch,
        compiler_params=params(SIM_LIMIT),
        name="place_gradients",
    )(ids, *gathered)


def body(
    image_tokens, text_tokens, lengths, pair_count, img_qkv, img_out, img_up, img_down, img_proj,
    gain_one, txt_qkv, txt_out, gain_two, txt_up, txt_down, txt_proj, log_scale,
):
    pairs, _, width = image_tokens.shape
    ff = txt_up.shape[1]
    row_index = lax.axis_index("row")
    col_index = lax.axis_index("col")
    row_count = lax.axis_size("row")
    col_count = lax.axis_size("col")
    high = col_count // 4
    cut = pairs - NB
    across = row_count - 1

    by_token = jnp.transpose(image_tokens, (1, 0, 2))
    got_images = flip(by_token[:, cut:], "row", across)
    got_texts = flip(text_tokens[cut:], "row", across)
    lens = lengths.astype(F32).reshape(pairs // QB, QB)
    got_lens = flip(lens[cut // QB :], "row", across)
    plan, rlive, tlive, scal = prepare(jnp.stack([col_index, row_index]).astype(jnp.int32), pair_count, log_scale, cut)
    gain_one = gain_one.reshape(1, width)
    gain_two = gain_two.reshape(1, width)

    weights = (img_qkv, img_out, img_up, img_down, img_proj)
    first_unit = image_tower(plan, by_token, None, 0, cut, cut, IMAGE_NB, 1.0, *weights)
    last_unit = lax.cond(
        plan[IMAGE_BLOCKS + cut // GROUP] > 0,
        lambda: image_tower(plan, by_token, got_images, cut, NB, cut, GROUP, 0.01, *weights),
        lambda: jnp.zeros((NB, width), BF16),
    )
    unit = jnp.concatenate([first_unit, last_unit], axis=0)
    parts = [unit] + [flip(unit, "col", 4 * p) for p in range(1, high)]
    qkv, att, y1 = text_first(plan, text_tokens, got_texts, lens, got_lens, cut, gain_one, txt_qkv, txt_out)
    parts = lax.optimization_barrier((*parts, y1))
    y1 = parts[-1]
    near = jnp.concatenate(parts[:-1], axis=0)
    beside = flip(near, "col", 2)
    core_near = flip(near, "col", 1)
    slopes, hsum, pooled, emb, text_low = text_second(
        plan, y1, lens, got_lens, cut, gain_two, txt_up, txt_down, txt_proj
    )
    images = [near, core_near, beside, flip(tie(beside, text_low), "col", 1)]
    texts = [text_low] + [flip(text_low, "row", p) for p in range(1, row_count)]
    rowsum, colsum = sim_sums(plan, scal, texts, tlive, rlive, images)
    total_col = colsum
    for p in range(1, row_count):
        other = flip(colsum, "row", p)
        total_col = total_col + jnp.concatenate([other[k ^ p : (k ^ p) + 1] for k in range(row_count)], axis=0)
    for bit in range(2, (high * 4).bit_length() - 1):
        rowsum = rowsum + flip(rowsum, "col", 1 << bit)
    rowsum = sum_over(rowsum, "col", 1, 4)
    *duns, stat = sim_grads(plan, scal, texts, tlive, rlive, rowsum, total_col, images)
    others = [flip(duns[p], "row", p) for p in range(1, row_count)]
    split_row = width * 2 % (row_count * 2 * 2 * 16) == 0
    along_row = ("row", 1, row_count, split_row)
    along_y = ("col", 2, 2, True)
    along_z = ("col", 4, 2, high % 2 == 0)
    along_far = ("col", 8, high // 2, False)
    order_a = [along_row, along_y, along_z, along_far]
    order_b = [along_y, along_z, along_row, along_far]
    order_c = [along_z, along_row, along_y, along_far]
    qkv = pltpu.with_memory_space_constraint(qkv, pltpu.HBM)
    text_grad, keep_a, send_a, keep_b, send_b, keep_c, send_c = text_backward(
        plan, text_tokens, qkv, att, y1, slopes, got_texts, lens, got_lens, cut, duns[0], emb, pooled, hsum,
        gain_one, txt_qkv, txt_out, gain_two, txt_up, txt_down, txt_proj, others, stat,
    )
    back = flip(text_grad[cut:], "row", across)
    low_half = row_index < row_count // 2
    counts = pair_count[:, col_index]
    balanced = jnp.where(low_half, counts[row_index], counts[row_index ^ across]) <= cut
    last = jnp.where(balanced, jnp.where(low_half, jnp.zeros_like(back), back), text_grad[cut:])
    text_grad = lax.dynamic_update_slice_in_dim(text_grad, last, cut, 0)
    orders = [order_a, order_b, order_c]
    targets = [
        [(0, ff, True), (ff, ff + width, True), (ff + width, ff + width + 128, True)],
        [(0, ff, False)],
        [(0, width, True), (width, 4 * width, False)],
    ]
    shapes = [[(ff, width), (width, width)], [(width, ff)], [(width, width), (width, 3 * width)]]
    placed = []
    for keep, send, rounds, places, sizes in zip((keep_a, keep_b, keep_c), (send_a, send_b, send_c), orders, targets, shapes):
        gathered = exchange(keep, send, rounds, text_grad if not placed else None)
        placed += place(plan, gathered, places, rounds, sizes, not placed)
    sum_down, sum_proj, sum_one, sum_two, loss, sum_scale, sum_up, sum_out, sum_qkv = placed
    return (
        loss, text_grad, sum_one, sum_qkv, sum_out, sum_two, sum_up, sum_down, sum_proj, sum_scale,
    )


def solution(mesh):
    return jax.shard_map(
        body,
        mesh=mesh,
        in_specs=(
            P(("row", "col"), None, None),
            P(("row", "col"), None, None),
            P(("row", "col")),
            P(),
            P(),
            P(),
            P(),
            P(),
            P(),
            P(),
            P(),
            P(),
            P(),
            P(),
            P(),
            P(),
            P(),
        ),
        out_specs=(P(), P(("row", "col"), None, None), P(), P(), P(), P(), P(), P(), P(), P()),
        check_vma=False,
    )
```

```python
import functools
import jax
import jax.numpy as jnp
from jax import lax
from jax.experimental import pallas as pl
from jax.experimental.pallas import tpu as pltpu
from jax.sharding import PartitionSpec as P

HEADS = 6
HEAD = 64
epsilon = 1e-6
F32 = jnp.float32
BF16 = jnp.bfloat16
GELU_A = 0.7978845608028654
GELU_B = 0.7978845608028654 * 0.044715
SAFE = 60.0
GROUP = 8
PITCH = 9
IMAGE_NB = 16
USE = 2
ACTIVE = 3
ORDER = 4
ORDER_ALL = 8
IMAGE_BLOCKS = 12
PLAN = 28
NB = 32
QB = 16
T1_LIMIT = 20
T2_LIMIT = 20
BACK_LIMIT = 30
SIM_LIMIT = 12


def mm(a, b):
    return lax.dot_general(a, b, (((1,), (0,)), ((), ())), preferred_element_type=F32)


def mm_t(a, b):
    return lax.dot_general(a, b, (((1,), (1,)), ((), ())), preferred_element_type=F32)


def mm_split(a, b):
    hi = a.astype(BF16)
    lo = (a - hi.astype(F32)).astype(BF16)
    return mm(hi, b) + mm(lo, b)


def column_chunks(width):
    edge = width // 2 // 256 * 256
    return ((0, edge), (edge, width))


def over(a, b):
    r = pl.reciprocal(b, approx=True)
    return a * (r * (2.0 - b * r))


def normed(v):
    c = v - jnp.mean(v, axis=-1, keepdims=True)
    return c * lax.rsqrt(jnp.mean(c * c, axis=-1, keepdims=True) + epsilon)


def unit_scale(e):
    return lax.rsqrt(jnp.sum(e * e, axis=-1, keepdims=True) + epsilon)


def lane_halves():
    lane = lax.broadcasted_iota(jnp.int32, (1, 128), 1)
    low = (lane < HEAD).astype(F32)
    return low, 1.0 - low


def image_kernel(first, cut, plan_ref, x_ref, recv_ref, wqkv_ref, wout_ref, wup_ref, wdown_ref, wproj_ref, unit_ref, qkv, att, hsum, xsum):
    step = pl.program_id(0)
    length, nb, width = x_ref.shape
    rows = length * GROUP

    @pl.when(step == 0)
    def _():
        qkv[...] = jnp.zeros_like(qkv)
        hsum[...] = jnp.zeros_like(hsum)
        xsum[...] = jnp.zeros_like(xsum)

    block = first // nb + step

    @pl.when(plan_ref[IMAGE_BLOCKS + block * (nb // GROUP)] > 0)
    def _():
        image_block(step, block, cut, plan_ref, x_ref, recv_ref, wqkv_ref, wout_ref, wup_ref, qkv, att, hsum, xsum)

    @pl.when(step == pl.num_programs(0) - 1)
    def _():
        pooled = xsum[...] * (1.0 / length) + mm_split(hsum[...] * (0.5 / length), wdown_ref[...])
        e = mm(pooled.astype(BF16), wproj_ref[...])
        unit_ref[...] = (e * unit_scale(e)).astype(BF16)


def image_block(step, block, cut, plan_ref, x_ref, recv_ref, wqkv_ref, wout_ref, wup_ref, qkv, att, hsum, xsum):
    length, nb, width = x_ref.shape
    rows = length * GROUP
    slots = qkv.shape[2] // PITCH
    tiles = width // 128
    ff = wup_ref.shape[1]
    groups = nb // GROUP
    moved = (plan_ref[USE] > 0) & (block >= cut // nb)

    def tokens(g):
        x = x_ref[...].astype(F32)
        if recv_ref is not None:
            x = jnp.where(moved, recv_ref[...].astype(F32), x)
        return x[:, g * GROUP : (g + 1) * GROUP, :].reshape(rows, width)

    low, high = lane_halves()
    key_row = lax.broadcasted_iota(jnp.int32, (2 * slots, 128), 0)
    key_lane = lax.broadcasted_iota(jnp.int32, (2 * slots, 128), 1)
    own_head = (key_row < slots) == (key_lane < HEAD)
    real = jnp.where(key_row < slots, key_row, key_row - slots) < length
    ones = jnp.where(own_head & real, 1.0, 0.0).astype(BF16)

    def pairs_of(g):
        return pl.ds(pl.multiple_of(step * nb + g * GROUP, GROUP), GROUP)

    def scores(g, p, h):
        at = pl.ds(p, slots, stride=PITCH)
        q = qkv[g, h, at, :].astype(BF16) * BF16(HEAD**-0.5)
        k = qkv[g, tiles + h, at, :]
        return mm_t(q, jnp.concatenate([k * low, k * high], axis=0).astype(BF16))

    def weighted(g, p, h, e):
        at = pl.ds(p, slots, stride=PITCH)
        v = qkv[g, 2 * tiles + h, at, :]
        vbd = jnp.concatenate([v * low, v * high], axis=0).astype(BF16)
        o = mm(e.astype(BF16), jnp.concatenate([vbd, ones], axis=1))
        att[g, h, at, :] = over(o[:, :128], o[:, 128:])

    def projected(g):
        n1 = normed(tokens(g)).astype(BF16)
        for first, last in column_chunks(3 * width):
            made = mm(n1, wqkv_ref[:, first:last])
            for c in range(first // 128, last // 128):
                here = c * 128 - first
                for t in range(length):
                    qkv[g, c, t * PITCH : t * PITCH + GROUP, :] = made[t * GROUP : (t + 1) * GROUP, here : here + 128]

    def after_attention(g):
        heads = jnp.concatenate(
            [
                jnp.concatenate([att[g, h, t * PITCH : t * PITCH + GROUP, :] for t in range(length)], axis=0)
                for h in range(tiles)
            ],
            axis=1,
        )
        x1 = tokens(g) + mm(heads.astype(BF16), wout_ref[...])
        xsum[pairs_of(g), :] = jnp.sum(x1.reshape(length, GROUP, width), axis=0)
        return normed(x1).astype(BF16)

    def gelu_sum(g, u, c):
        made = u * (1.0 + jnp.tanh(u * (GELU_A + GELU_B * (u * u))))
        hsum[pairs_of(g), pl.ds(c, 256)] = jnp.sum(made.reshape(length, GROUP, 256), axis=0)

    def feed_steps(g):
        n2 = after_attention(g)
        before = None
        for c in range(0, ff, 256):
            u = mm(n2, wup_ref[:, c : c + 256])
            if before is not None:
                gelu_sum(g, *before)
            before = (u, c)
            yield
        gelu_sum(g, *before)
        yield

    largest = jnp.zeros((slots, 2 * slots), F32)
    units = [(p, h) for p in range(GROUP) for h in range(tiles)]
    ahead = 3
    feed = iter(())
    projected(0)
    for g in range(groups):
        s_list, e_list = {}, {}
        for k in range(len(units) + 2 * ahead):
            if k < len(units):
                s_list[k] = scores(g, *units[k])
            if 0 <= k - ahead < len(units):
                s = s_list.pop(k - ahead)
                largest = jnp.maximum(largest, jnp.abs(s))
                e_list[k - ahead] = jnp.exp(s)
            if 0 <= k - 2 * ahead < len(units):
                weighted(g, *units[k - 2 * ahead], e_list.pop(k - 2 * ahead))
            if k % 4 == 2:
                next(feed, None)
            if k == len(units) // 2 and g + 1 < groups:
                projected(g + 1)
        for _ in feed:
            pass
        feed = feed_steps(g)
    for _ in feed:
        pass

    @pl.when(jnp.logical_not(jnp.max(largest) <= SAFE))
    def _():
        key = lax.broadcasted_iota(jnp.int32, (1, 2 * slots), 1)
        in_low = key < slots
        for_low = key < length
        for_high = (key >= slots) & (key < slots + length)
        @pl.loop(0, groups)
        def _(g):
            @pl.loop(0, GROUP)
            def _(p):
                @pl.loop(0, tiles)
                def _(h):
                    s = scores(g, p, h)
                    top_low = jnp.max(jnp.where(for_low, s, -1e30), axis=1, keepdims=True)
                    top_high = jnp.max(jnp.where(for_high, s, -1e30), axis=1, keepdims=True)
                    s = jnp.where(for_low | for_high, s, -1e30) - jnp.where(in_low, top_low, top_high)
                    weighted(g, p, h, jnp.exp(s))

        for g in range(groups):
            n2 = after_attention(g)

            @pl.loop(0, ff // 256)
            def _(c):
                at = pl.multiple_of(c * 256, 256)
                gelu_sum(g, mm(n2, wup_ref[:, pl.ds(at, 256)]), at)


def fixed(shape):
    zeros = (0,) * len(shape)
    return pl.BlockSpec(shape, lambda *_: zeros, pipeline_mode=pl.Buffered(1))


def image_tower(plan, tokens, received, first, count, cut, nb, cost, wqkv, wout, wup, wdown, wproj):
    length, _, width = tokens.shape
    slots = -(-length // 8) * 8
    ff = wup.shape[1]
    weights = (wqkv, wout, wup, wdown, wproj)
    at = first // nb
    specs = [pl.BlockSpec((length, nb, width), lambda i, plan: (0, at + i, 0))]
    if received is None:
        kernel = lambda plan_ref, x_ref, *refs: image_kernel(first, cut, plan_ref, x_ref, None, *refs)
        arrays = (tokens,)
    else:
        kernel = functools.partial(image_kernel, first, cut)
        last = received.shape[1] // nb - 1
        specs.append(
            pl.BlockSpec((length, nb, width), lambda i, plan: (0, jnp.clip(at + i - cut // nb, 0, last), 0))
        )
        arrays = (tokens, received)
    return pl.pallas_call(
        kernel,
        grid_spec=pltpu.PrefetchScalarGridSpec(
            num_scalar_prefetch=1,
            grid=(count // nb,),
            in_specs=specs + [fixed(w.shape) for w in weights],
            out_specs=pl.BlockSpec((count, width), lambda i, plan: (0, 0)),
            scratch_shapes=[
                pltpu.VMEM((nb // GROUP, 3 * width // 128, slots * PITCH, 128), F32),
                pltpu.VMEM((nb // GROUP, width // 128, slots * PITCH, 128), F32),
                pltpu.VMEM((count, ff), F32),
                pltpu.VMEM((count, width), F32),
            ],
        ),
        out_shape=jax.ShapeDtypeStruct((count, width), BF16),
        compiler_params=pltpu.CompilerParams(vmem_limit_bytes=60 * 2**20),
        cost_estimate=pl.CostEstimate(
            flops=int(cost * 2 * count * length * width * (4 * width + ff)),
            bytes_accessed=int(cost * (count * length * width * 2 + 4 * 2**20)),
            transcendentals=int(cost * count * length * ff),
        ),
        name="image_block",
    )(plan, *arrays, *weights)


def mm_tn(a, b):
    return lax.dot_general(a, b, (((0,), (0,)), ((), ())), preferred_element_type=F32)


def stats(v):
    c = v - jnp.mean(v, axis=-1, keepdims=True)
    inv = lax.rsqrt(jnp.mean(c * c, axis=-1, keepdims=True) + epsilon)
    return c * inv, inv


def norm_back(g, n, inv):
    return inv * (
        g - jnp.mean(g, axis=-1, keepdims=True) - n * jnp.mean(g * n, axis=-1, keepdims=True)
    )


def staggered(stages, units, ahead):
    kept = [dict() for _ in stages]
    for k in range(len(units) + (len(stages) - 1) * ahead):
        for at, stage in enumerate(stages):
            u = k - at * ahead
            if 0 <= u < len(units):
                made = stage(units[u], *([kept[at - 1].pop(u)] if at else []))
                kept[at][u] = made


def group_loop(stages, rows, width):
    @pl.loop(0, rows // 256)
    def _(half):
        first = half * 2
        units = [(first + g, h) for g in range(2) for h in range(0, width, 128)]
        staggered(stages, units, 1)


def same_pair(length):
    row = lax.broadcasted_iota(jnp.int32, (128, 128), 0) // length
    lane = lax.broadcasted_iota(jnp.int32, (128, 128), 1) // length
    return row == lane


SMEM = pl.BlockSpec(memory_space=pltpu.SMEM)
VMEM = pl.BlockSpec(memory_space=pltpu.VMEM)


def params(limit=60):
    return pltpu.CompilerParams(vmem_limit_bytes=limit * 2**20)


def as_column(row):
    size = row.shape[1]
    diagonal = lax.broadcasted_iota(jnp.int32, (size, size), 0) == lax.broadcasted_iota(jnp.int32, (size, size), 1)
    return jnp.sum(jnp.where(diagonal, row, 0.0), axis=1, keepdims=True)


def as_row(col):
    size = col.shape[0]
    diagonal = lax.broadcasted_iota(jnp.int32, (size, size), 0) == lax.broadcasted_iota(jnp.int32, (size, size), 1)
    return jnp.sum(jnp.where(diagonal, col, 0.0), axis=0, keepdims=True)


def prepare_kernel(cut, count_ref, scale_ref, plan_ref, rlive_ref, tlive_ref, scal_ref):
    rows, cols = count_ref.shape
    across = rows - 1
    col = lax.axis_index("col")
    row = lax.axis_index("row")

    def limits(r, c):
        n = count_ref[r, c]
        other = count_ref[r ^ across, c]
        low = r < rows // 2
        balanced = jnp.where(low, n, other) <= cut
        return n, jnp.where(balanced, jnp.where(low, other, 0), n), low & balanced

    def mask(r, c):
        first, last, _ = limits(r, c)
        slot = lax.broadcasted_iota(jnp.int32, (1, 128), 1)
        return jnp.where(slot < jnp.where(slot < cut, first, last), 1.0, 0.0)

    for c in range(cols):
        rlive_ref[c : c + 1, :] = mask(row, c)
    for p in range(rows):
        tlive_ref[p : p + 1, :] = mask(row ^ p, col)
    first, last, use = limits(row, col)
    limit = lambda start: first if start < cut else last
    plan_ref[0] = col
    plan_ref[1] = row
    plan_ref[USE] = use.astype(jnp.int32)
    blocks = 128 // NB
    active = [(b * NB < limit(b * NB)).astype(jnp.int32) for b in range(blocks)]
    count = sum(active)
    before = jnp.int32(0)
    for b in range(blocks):
        plan_ref[ORDER_ALL + jnp.where(active[b] > 0, before, count + b - before)] = b
        before = before + active[b]
    for i in range(blocks):
        plan_ref[ORDER + i] = plan_ref[ORDER_ALL + jnp.minimum(i, count - 1)]
    plan_ref[ACTIVE] = count
    for b in range(128 // GROUP):
        plan_ref[IMAGE_BLOCKS + b] = (b * GROUP < limit(b * GROUP)).astype(jnp.int32)
    total = jnp.int32(0)
    for r in range(rows):
        for c in range(cols):
            total = total + count_ref[r, c]
    index = lax.broadcasted_iota(jnp.int32, (8, 128), 0)
    scal_ref[...] = jnp.where(index == 0, jnp.exp(jnp.full((8, 128), scale_ref[0], F32)), 0.5 / jnp.full((8, 128), total, jnp.int32).astype(F32))


def prepare(pair_count, log_scale, cut):
    rows, cols = pair_count.shape
    return pl.pallas_call(
        functools.partial(prepare_kernel, cut),
        in_specs=[SMEM] * 2,
        out_specs=[SMEM, VMEM, VMEM, VMEM],
        out_shape=[
            jax.ShapeDtypeStruct((PLAN,), jnp.int32),
            jax.ShapeDtypeStruct((cols, 128), F32),
            jax.ShapeDtypeStruct((rows, 128), F32),
            jax.ShapeDtypeStruct((8, 128), F32),
        ],
        name="prepare",
    )(pair_count, log_scale)


def lengths_of(plan_ref, cut, part, lens_ref, got_ref):
    moved = (plan_ref[USE] > 0) & (part * QB >= cut)
    got = got_ref[pl.ds(jnp.maximum(part - cut // QB, 0), 1), :]
    return as_column(jnp.where(moved, got, lens_ref[pl.ds(part, 1), :]))


def block_lengths(plan_ref, cut, block, lens_ref, got_ref):
    parts = [lengths_of(plan_ref, cut, block * (NB // QB) + k, lens_ref, got_ref) for k in range(NB // QB)]
    return jnp.concatenate(parts, axis=0)


def all_lengths(plan_ref, cut, lens_ref, got_ref):
    parts = [lengths_of(plan_ref, cut, b, lens_ref, got_ref) for b in range(lens_ref.shape[0])]
    return jnp.concatenate(parts, axis=0)


def live_pick(lens, rows):
    pairs = lens.shape[0]
    length = rows // pairs
    token = lax.broadcasted_iota(jnp.int32, (pairs, rows), 1)
    own = token // length == lax.broadcasted_iota(jnp.int32, (pairs, rows), 0)
    return jnp.where(own & ((token % length).astype(F32) < lens), 1.0, 0.0)


def text_tokens_of(plan_ref, cut, block, x_ref, recv_ref):
    nb, length, width = x_ref.shape
    moved = (plan_ref[USE] > 0) & (block * nb >= cut)
    x = jnp.where(moved, recv_ref[...].astype(F32), x_ref[...].astype(F32))
    return x.reshape(nb * length, width)


def ordered(width, rows):
    return pl.BlockSpec((rows, width), lambda i, plan: (plan[ORDER + i], 0))


def ordered_pairs(shape, order=ORDER):
    return pl.BlockSpec((NB,) + shape[1:], lambda i, plan: (plan[order + i], 0, 0))


def held(shape):
    zeros = (0,) * len(shape)
    return pl.BlockSpec(shape, lambda i, plan: zeros)


def text_first_kernel(cut, plan_ref, x_ref, recv_ref, lens_ref, got_ref, gain_ref, wqkv_ref, wout_ref, qkv_ref, att_ref, y1_ref):
    step = pl.program_id(0)
    block = plan_ref[ORDER + step]

    @pl.when(step < plan_ref[ACTIVE])
    def _():
        x = text_tokens_of(plan_ref, cut, block, x_ref, recv_ref)
        lens = block_lengths(plan_ref, cut, block, lens_ref, got_ref)
        text_attention(x, lens, x_ref.shape[1], gain_ref, wqkv_ref, wout_ref, qkv_ref, att_ref, y1_ref)


def text_attention(x, lens, length, gain_ref, wqkv_ref, wout_ref, qkv_ref, att_ref, y1_ref):
    rows, width = x.shape
    n1 = (normed(x) * gain_ref[...]).astype(BF16)
    for first, last in column_chunks(3 * width):
        qkv_ref[:, first:last] = mm(n1, wqkv_ref[:, first:last]).astype(BF16)
    lane = lax.broadcasted_iota(jnp.int32, (128, 128), 1)
    low = (lane[:1] < HEAD).astype(BF16)
    high = 1 - low
    half = lax.broadcasted_iota(jnp.int32, (256, 128), 0) < 128
    ones = jnp.where(half == (lax.broadcasted_iota(jnp.int32, (256, 128), 1) < HEAD), 1.0, 0.0).astype(BF16)
    same = same_pair(length)
    live = jnp.sum(live_pick(lens, rows), axis=0, keepdims=True)
    bias = {g: jnp.where(same & (live[:, g : g + 128] > 0), 0.0, -1e30) for g in range(0, rows, 128)}

    def scores(unit):
        g, h = unit
        q = qkv_ref[g : g + 128, h : h + 128] * BF16(HEAD**-0.5)
        k = qkv_ref[g : g + 128, width + h : width + h + 128]
        return mm_t(q, jnp.concatenate([k * low, k * high], axis=0))

    def expo(unit, s):
        one = bias[unit[0]]
        parts = [s[:, :128] + one, s[:, 128:] + one]
        return jnp.concatenate([jnp.exp(p - jnp.max(p, axis=1, keepdims=True)) for p in parts], axis=1).astype(BF16)

    def weighted(unit, e):
        g, h = unit
        v = qkv_ref[g : g + 128, 2 * width + h : 2 * width + h + 128]
        vbd = jnp.concatenate([v * low, v * high], axis=0)
        o = mm(e, jnp.concatenate([vbd, ones], axis=1))
        att_ref[g : g + 128, h : h + 128] = over(o[:, :128], o[:, 128:]).astype(BF16)

    staggered([scores, expo, weighted], [(g, h) for g in range(0, rows, 128) for h in range(0, width, 128)], 1)
    y1_ref[...] = x + mm(att_ref[...], wout_ref[...])


def text_first(plan, x, received, lens, got, cut, gain_one, wqkv, wout):
    pairs, length, width = x.shape
    rows = NB * length
    tokens = pairs * length
    rest = (received, lens, got, gain_one, wqkv, wout)
    wide = [(3 * width, BF16), (width, BF16), (width, F32)]
    return pl.pallas_call(
        functools.partial(text_first_kernel, cut),
        grid_spec=pltpu.PrefetchScalarGridSpec(
            num_scalar_prefetch=1,
            grid=(pairs // NB,),
            in_specs=[ordered_pairs(x.shape)] + [fixed(w.shape) for w in rest],
            out_specs=[ordered(w, rows) for w, _ in wide],
        ),
        out_shape=[(pltpu.HBM if k == 0 else jax.ShapeDtypeStruct)((tokens, w), kind) for k, (w, kind) in enumerate(wide)],
        compiler_params=params(T1_LIMIT),
        cost_estimate=pl.CostEstimate(flops=2 * tokens * width * 5 * width, bytes_accessed=12 * 2**20, transcendentals=0),
        name="text_attention",
    )(plan, x, *rest)


def text_second_kernel(
    cut, plan_ref, y1_ref, lens_ref, got_ref, gain_two_ref, wup_ref, wdown_ref, wproj_ref,
    slope_ref, hsum_ref, pooled_ref, emb_ref, low_ref, ysum,
):
    step = pl.program_id(0)
    block = plan_ref[ORDER + step]

    @pl.when(step == 0)
    def _():
        hsum_ref[...] = jnp.zeros_like(hsum_ref)
        ysum[...] = jnp.zeros_like(ysum)

    @pl.when(step < plan_ref[ACTIVE])
    def _():
        rows = y1_ref.shape[0]
        y1 = y1_ref[...]
        pick = live_pick(block_lengths(plan_ref, cut, block, lens_ref, got_ref), rows).astype(BF16)
        pair = pl.ds(pl.multiple_of(block * NB, NB), NB)
        y1_hi = y1.astype(BF16)
        ysum[pair, :] = mm(pick, y1_hi) + mm(pick, (y1 - y1_hi.astype(F32)).astype(BF16))
        n2 = (normed(y1) * gain_two_ref[...]).astype(BF16)

        live = mm_tn(pick, jnp.ones((NB, 128), BF16))
        live = jnp.concatenate([live, live], axis=1)

        def gelu_parts(u, c):
            square = u * u
            t = 1.0 + jnp.tanh(u * (GELU_A + GELU_B * square))
            half = 0.5 * u
            hsum_ref[pair, c : c + 256] = mm(pick, (half * t).astype(BF16))
            d = t * (0.5 + (2.0 - t) * (half * (GELU_A + (3.0 * GELU_B) * square)))
            slope_ref[:, c : c + 256] = (d * live).astype(BF16)

        in_chunks(n2, wup_ref, gelu_parts)

    @pl.when(step == pl.num_programs(0) - 1)
    def _():
        inv_len = 1.0 / all_lengths(plan_ref, cut, lens_ref, got_ref)
        pooled = (ysum[...] * inv_len + mm_split(hsum_ref[...] * inv_len, wdown_ref[...])).astype(BF16)
        pooled_ref[...] = pooled
        e = mm(pooled, wproj_ref[...])
        emb_ref[...] = e
        low_ref[...] = (e * unit_scale(e)).astype(BF16)


def in_chunks(left, right_ref, use):
    before = None
    for c in range(0, right_ref.shape[1], 256):
        u = mm(left, right_ref[:, c : c + 256])
        if before is not None:
            use(*before)
        before = (u, c)
    use(*before)


def text_second(plan, y1, lens, got, cut, gain_two, wup, wdown, wproj):
    tokens, width = y1.shape
    pairs = lens.size
    rows = NB * tokens // pairs
    ff = wup.shape[1]
    rest = (lens, got, gain_two, wup, wdown, wproj)
    flat = [((pairs, ff), F32), ((pairs, width), BF16), ((pairs, width), F32), ((pairs, width), BF16)]
    return pl.pallas_call(
        functools.partial(text_second_kernel, cut),
        grid_spec=pltpu.PrefetchScalarGridSpec(
            num_scalar_prefetch=1,
            grid=(pairs // NB,),
            in_specs=[ordered(width, rows)] + [fixed(w.shape) for w in rest],
            out_specs=[ordered(ff, rows)] + [held(shape) for shape, _ in flat],
            scratch_shapes=[pltpu.VMEM((pairs, width), F32)],
        ),
        out_shape=[jax.ShapeDtypeStruct((tokens, ff), BF16)] + [jax.ShapeDtypeStruct(shape, kind) for shape, kind in flat],
        compiler_params=params(T2_LIMIT),
        cost_estimate=pl.CostEstimate(flops=2 * tokens * width * ff, bytes_accessed=12 * 2**20, transcendentals=tokens * ff),
        name="text_pool",
    )(plan, y1, *rest)


def image_groups(image_refs):
    for j, ref in enumerate(image_refs):
        yield j, ref.shape[0] // 128, len(image_refs), ref[...]


def sums_kernel(rows, ids_ref, scal_ref, tlive_ref, rlive_ref, *refs):
    text_refs = refs[:rows]
    image_refs = refs[rows:-2]
    rowsum_ref, colsum_ref = refs[-2:]
    me = ids_ref[0]
    scale = scal_ref[:1, :1]
    text = jnp.concatenate([ref[...] for ref in text_refs], axis=0)
    tlive = jnp.concatenate([as_column(tlive_ref[p : p + 1, :]) for p in range(rows)], axis=0)
    col = jnp.zeros((rows * 128, 1), F32)
    for j, high, low, images in image_groups(image_refs):
        e = jnp.exp(scale * mm_t(text, images)) * tlive
        total = jnp.sum(e, axis=0, keepdims=True)
        kept = jnp.zeros((rows * 128, 128), F32)
        for i in range(high):
            at = pl.ds(me ^ (low * i + j), 1)
            rowsum_ref[at, :] = total[:, i * 128 : i * 128 + 128]
            kept = kept + e[:, i * 128 : i * 128 + 128] * rlive_ref[at, :]
        col = col + jnp.sum(kept, axis=1, keepdims=True)
    for p in range(rows):
        colsum_ref[p : p + 1, :] = as_row(col[p * 128 : p * 128 + 128])


def sim_sums(ids, scal, texts, tlive, rlive, images):
    cols = rlive.shape[0]
    rows = len(texts)
    return pl.pallas_call(
        functools.partial(sums_kernel, rows),
        in_specs=[SMEM] + [VMEM] * (3 + rows + len(images)),
        out_specs=[VMEM, VMEM],
        out_shape=[jax.ShapeDtypeStruct((cols, 128), F32), jax.ShapeDtypeStruct((rows, 128), F32)],
        compiler_params=params(SIM_LIMIT),
        cost_estimate=pl.CostEstimate(
            flops=2 * rows * 128 * cols * 128 * 384, bytes_accessed=cols * 128 * 768, transcendentals=rows * cols * 128 * 128
        ),
        name="similarity_sums",
    )(ids, scal, tlive, rlive, *texts, *images)


def grad_kernel(rows, ids_ref, scal_ref, tlive_ref, rlive_ref, rowsum_ref, colsum_ref, *refs):
    text_refs = refs[:rows]
    image_refs = refs[rows : -rows - 1]
    dun_refs = refs[-rows - 1 : -1]
    stat_ref = refs[-1]
    me = ids_ref[0]
    scale = scal_ref[:1, :1]
    inv = scal_ref[1:2, :1]
    text = jnp.concatenate([ref[...] for ref in text_refs], axis=0)
    tlive = jnp.concatenate([as_column(tlive_ref[p : p + 1, :]) for p in range(rows)], axis=0)
    col = jnp.concatenate([as_column(colsum_ref[p : p + 1, :]) for p in range(rows)], axis=0)
    col = jnp.where(tlive > 0, col, 1.0)
    col_inv = inv / col
    total = jnp.zeros(text.shape, F32)
    moved = jnp.zeros((1, 128), F32)
    for j, high, low, images in image_groups(image_refs):
        s = scale * mm_t(text, images)
        e = jnp.exp(s) * tlive
        at = [pl.ds(me ^ (low * i + j), 1) for i in range(high)]
        rlive = jnp.concatenate([rlive_ref[one, :] for one in at], axis=1)
        row_inv = jnp.concatenate([inv / rowsum_ref[one, :] for one in at], axis=1)
        ds = (e * rlive) * (row_inv + col_inv)
        by_lane = jnp.sum(ds * s, axis=0, keepdims=True)
        for i in range(high):
            moved = moved + by_lane[:, i * 128 : i * 128 + 128]
        total = total + mm((scale * ds).astype(BF16), images)
        if j == 0:
            mine = images[:128].astype(F32)
    own_live = tlive[:128]
    cosine = jnp.sum(mine * text[:128].astype(F32), axis=1, keepdims=True)
    live_cosine = jnp.sum(cosine * own_live, axis=0, keepdims=True)
    at = pl.ds(me, 1)
    logs = jnp.sum(jnp.log(rowsum_ref[at, :]) * rlive_ref[at, :], axis=1, keepdims=True)
    logs = logs + jnp.sum(jnp.log(col[:128]) * own_live, axis=0, keepdims=True)
    loss = inv * (logs - 2.0 * scale * live_cosine)
    scale_part = jnp.sum(moved, axis=1, keepdims=True) - 2.0 * inv * scale * live_cosine
    dun_refs[0][...] = total[:128] + (scale * (-2.0 * inv * own_live)).astype(BF16).astype(F32) * mine
    for p in range(1, rows):
        dun_refs[p][...] = total[p * 128 : p * 128 + 128].astype(BF16)
    lane = lax.broadcasted_iota(jnp.int32, (8, 128), 1)
    stat_ref[...] = jnp.where(lane == 0, loss, jnp.where(lane == 1, scale_part, 0.0))


def sim_grads(ids, scal, texts, tlive, rlive, rowsum, colsum, images):
    cols = rlive.shape[0]
    rows = len(texts)
    return pl.pallas_call(
        functools.partial(grad_kernel, rows),
        in_specs=[SMEM] + [VMEM] * (5 + rows + len(images)),
        out_specs=[VMEM] * (rows + 1),
        out_shape=[jax.ShapeDtypeStruct(text.shape, BF16 if k else F32) for k, text in enumerate(texts)] + [jax.ShapeDtypeStruct((8, 128), F32)],
        compiler_params=params(SIM_LIMIT),
        cost_estimate=pl.CostEstimate(
            flops=4 * rows * 128 * cols * 128 * 384, bytes_accessed=cols * 128 * 768, transcendentals=rows * cols * 128 * 128
        ),
        name="similarity_grads",
    )(ids, scal, tlive, rlive, rowsum, colsum, *texts, *images)


def write_halves(core, blocks, keep_ref, send_ref):
    half = len(blocks) // 2
    size = blocks[0].shape[0]

    def put(first, second):
        for at, (kept, sent) in enumerate(zip(first, second)):
            keep_ref[at * size : (at + 1) * size, :] = kept.astype(BF16)
            send_ref[at * size : (at + 1) * size, :] = sent.astype(BF16)

    @pl.when(core == 0)
    def _():
        put(blocks[:half], blocks[half:])

    @pl.when(core != 0)
    def _():
        put(blocks[half:], blocks[:half])


def back_kernel(
    cut, others, plan_ref, x_ref, qkv_ref, att_ref, y1_ref, slope_ref, recv_ref, lens_ref, got_ref,
    dun_ref, emb_ref, pooled_ref, hsum_ref, gain_ref, wqkv_ref, wout_ref, gain_two_ref, wup_ref, wdown_ref, wproj_ref, *refs,
):
    other_refs = refs[:others]
    stat_ref = refs[others]
    grad_ref, keep_a, send_a, keep_b, send_b, keep_c, send_c = refs[others + 1 : others + 8]
    dyp, dhp, dproj, ddown, dmix, dheads, acc_up, acc_out, acc_qkv, bias_ref, du_ref = refs[others + 8 :]
    step = pl.program_id(0)
    block = plan_ref[ORDER + step]
    active = step < plan_ref[ACTIVE]
    width = dun_ref.shape[1]
    ff = hsum_ref.shape[1]

    @pl.when(step == 0)
    def _():
        acc_up[...] = jnp.zeros_like(acc_up)
        acc_out[...] = jnp.zeros_like(acc_out)
        acc_qkv[...] = jnp.zeros_like(acc_qkv)
        g = dun_ref[...]
        for other in other_refs:
            g = g + other[...].astype(F32)
        e = emb_ref[...]
        inv = unit_scale(e)
        t = e * inv
        demb = (inv * (g - t * jnp.sum(g * t, axis=-1, keepdims=True))).astype(BF16)
        dproj[...] = mm_tn(pooled_ref[...], demb)
        back = mm_t(demb, wproj_ref[...]) * (1.0 / all_lengths(plan_ref, cut, lens_ref, got_ref))
        dyp[...] = back
        db = back.astype(BF16)
        dhp[...] = mm_t(db, wdown_ref[...])
        h = hsum_ref[...]
        hi = h.astype(BF16)
        lo = (h - hi.astype(F32)).astype(BF16)
        ddown[...] = mm_tn(hi, db) + mm_tn(lo, db)

    @pl.when(active)
    def _():
        x = text_tokens_of(plan_ref, cut, block, x_ref, recv_ref)
        lens = block_lengths(plan_ref, cut, block, lens_ref, got_ref)
        grad = back_block(
            block, x, lens, x_ref.shape[1], qkv_ref, att_ref, y1_ref, slope_ref, gain_ref, wqkv_ref, wout_ref,
            gain_two_ref, wup_ref, dyp, dhp, dmix, dheads, acc_up, acc_out, acc_qkv, bias_ref, du_ref,
        )
        grad_ref[...] = grad.astype(BF16).reshape(grad_ref.shape)

    @pl.when(jnp.logical_not(active))
    def _():
        grad_ref[...] = jnp.zeros_like(grad_ref)

    @pl.when(step == pl.num_programs(0) - 1)
    def _():
        core = plan_ref[0] & 1
        index = lax.broadcasted_iota(jnp.int32, (128, width), 0)
        stat = jnp.concatenate([stat_ref[:1, :]] * (width // 128), axis=1)
        by_qkv = jnp.sum(acc_qkv[...] * wqkv_ref[...].astype(F32), axis=1, keepdims=True)
        by_up = jnp.sum(acc_up[...] * wup_ref[...].astype(F32), axis=1, keepdims=True)
        first = as_row(by_qkv) / gain_ref[...]
        second = as_row(by_up) / gain_two_ref[...]
        small = jnp.where(index == 0, first, jnp.where(index == 1, second, jnp.where(index == 2, stat, 0.0)))
        blocks = [ddown[at : at + 128, :] for at in range(0, ff, 128)]
        blocks += [dproj[at : at + 128, :] for at in range(0, width, 128)]
        write_halves(core, blocks + [small], keep_a, send_a)
        write_halves(core, [acc_up[:, c : c + width] for c in range(0, ff, width)], keep_b, send_b)
        blocks = [acc_out[...]] + [acc_qkv[:, c * width : (c + 1) * width] for c in range(3)]
        write_halves(core, blocks, keep_c, send_c)


def back_block(
    block, x, lens, length, qkv_ref, att_ref, y1_ref, slope_ref, gain_ref, wqkv_ref, wout_ref,
    gain_two_ref, wup_ref, dyp, dhp, dmix, dheads, acc_up, acc_out, acc_qkv, bias_ref, du_ref,
):
    rows, width = x.shape
    ff = wup_ref.shape[1]
    pair = pl.ds(pl.multiple_of(block * NB, NB), NB)

    def spread(values):
        return jnp.broadcast_to(values[:, None, :], (NB, length, values.shape[1])).reshape(rows, values.shape[1])

    n2, inv = stats(y1_ref[...])
    n2_low = (n2 * gain_two_ref[...]).astype(BF16)
    for c in range(0, ff, width):
        at = slice(c, c + width)
        du_ref[:, at] = (spread(dhp[pair, at]) * slope_ref[:, at].astype(F32)).astype(BF16)
    dn2 = mm_t(du_ref[...], wup_ref[...])
    acc_up[...] += mm_tn(n2_low, du_ref[...])
    live = mm_tn(live_pick(lens, rows).astype(BF16), jnp.ones((NB, 128), BF16))
    dy1 = spread(dyp[pair, :]) * jnp.concatenate([live] * (width // 128), axis=1)
    dy1 = dy1 + norm_back(dn2 * gain_two_ref[...], n2, inv)
    da = dy1.astype(BF16)
    acc_out[...] += mm_tn(att_ref[...], da)
    dheads[...] = mm_t(da, wout_ref[...]).astype(BF16)
    attention_grads(length, live, qkv_ref, dmix, dheads, bias_ref)
    n1, inv = stats(x)
    n1_low = (n1 * gain_ref[...]).astype(BF16)
    dn1 = mm_t(dmix[...], wqkv_ref[...])
    acc_qkv[...] += mm_tn(n1_low, dmix[...])
    return dy1 + norm_back(dn1 * gain_ref[...], n1, inv)


def attention_grads(length, live, qkv_ref, dmix, dheads, bias_ref):
    rows, width = dheads.shape
    lane = lax.broadcasted_iota(jnp.int32, (128, 128), 1)
    first = lane < HEAD
    low = first[:1].astype(BF16)
    high = 1 - low
    eye = (lane == lax.broadcasted_iota(jnp.int32, (128, 128), 0)).astype(BF16)
    same = same_pair(length)
    for g in range(rows // 128):
        bias_ref[g] = jnp.where(same & (live[g * 128 : g * 128 + 128, :] > 0), 0.0, -1e30)

    zero = jnp.zeros((128, 128), BF16)

    def both_sides(one, two):
        return jnp.concatenate(
            [jnp.concatenate([one, zero], axis=1), jnp.concatenate([zero, two], axis=1)], axis=0
        )

    def pieces(unit, part):
        g, h = unit
        return qkv_ref[pl.ds(g * 128, 128), part * width + h : part * width + h + 128]

    def scores(unit):
        g, h = unit
        k = pieces(unit, 1)
        v = pieces(unit, 2)
        do = dheads[pl.ds(g * 128, 128), h : h + 128]
        left = jnp.concatenate(
            [jnp.concatenate([k * low, v * low], axis=1), jnp.concatenate([k * high, v * high], axis=1)], axis=0
        )
        made = mm_t(left, both_sides(pieces(unit, 0) * BF16(HEAD**-0.5), do))
        return made[:, :128], made[:, 128:]

    def soft(unit, made):
        g, _ = unit
        s, dp = made
        s = s.reshape(2, 128, 128) + bias_ref[g][None]
        e = jnp.exp(s - jnp.max(s, axis=1, keepdims=True))
        p = e * (1.0 / jnp.sum(e, axis=1, keepdims=True))
        dp = dp.reshape(2, 128, 128)
        ds = p * (dp - jnp.sum(p * dp, axis=1, keepdims=True))
        return p.reshape(256, 128).astype(BF16), ds.reshape(256, 128).astype(BF16)

    def products(unit, made):
        g, h = unit
        p, ds = made
        at = pl.ds(g * 128, 128)
        do = dheads[at, h : h + 128]
        made = mm(jnp.concatenate([p, ds], axis=1), both_sides(do, pieces(unit, 0) * BF16(HEAD**-0.5)))
        dv = made[:, :128]
        dk = made[:, 128:]
        dmix[at, 2 * width + h : 2 * width + h + 128] = jnp.where(first, dv[:128], dv[128:]).astype(BF16)
        dmix[at, width + h : width + h + 128] = jnp.where(first, dk[:128], dk[128:]).astype(BF16)
        return mm_t(eye, ds).astype(BF16)

    def query(unit, ds):
        g, h = unit
        k = pieces(unit, 1)
        kbd = jnp.concatenate([k * low, k * high], axis=0)
        dmix[pl.ds(g * 128, 128), h : h + 128] = (mm(ds, kbd) * HEAD**-0.5).astype(BF16)

    group_loop([scores, soft, products, query], rows, width)


def text_backward(
    plan, x, qkv, att, y1, slopes, received, lens, got, cut, dun, emb, pooled, hsum,
    gain_one, wqkv, wout, gain_two, wup, wdown, wproj, others, stat,
):
    pairs, length, width = x.shape
    rows = NB * length
    tokens = pairs * length
    ff = wup.shape[1]
    rest = (received, lens, got, dun, emb, pooled, hsum, gain_one, wqkv, wout, gain_two, wup, wdown, wproj, *others, stat)
    halves = [(ff + width + 128) // 2, ff // 2, 2 * width]
    shapes = [(half, width) for half in halves for _ in range(2)]
    return pl.pallas_call(
        functools.partial(back_kernel, cut, len(others)),
        grid_spec=pltpu.PrefetchScalarGridSpec(
            num_scalar_prefetch=1,
            grid=(pairs // NB,),
            in_specs=[ordered_pairs(x.shape), ordered(3 * width, rows), ordered(width, rows), ordered(width, rows), ordered(ff, rows)]
            + [fixed(w.shape) for w in rest],
            out_specs=[ordered_pairs(x.shape, ORDER_ALL)] + [held(shape) for shape in shapes],
            scratch_shapes=[
                pltpu.VMEM((pairs, width), F32),
                pltpu.VMEM((pairs, ff), F32),
                pltpu.VMEM((width, width), F32),
                pltpu.VMEM((ff, width), F32),
                pltpu.VMEM((rows, 3 * width), BF16),
                pltpu.VMEM((rows, width), BF16),
                pltpu.VMEM((width, ff), F32),
                pltpu.VMEM((width, width), F32),
                pltpu.VMEM((width, 3 * width), F32),
                pltpu.VMEM((rows // 128, 128, 128), F32),
                pltpu.VMEM((rows, ff), BF16),
            ],
        ),
        out_shape=[pltpu.HBM(x.shape, BF16)] + [pltpu.HBM(shape, BF16) for shape in shapes],
        compiler_params=params(BACK_LIMIT),
        cost_estimate=pl.CostEstimate(
            flops=2 * tokens * width * (10 * width + 2 * ff), bytes_accessed=24 * 2**20, transcendentals=0
        ),
        name="text_backward",
    )(plan, x, qkv, att, y1, slopes, *rest)


def flip(values, axis, bits):
    size = lax.axis_size(axis)
    return lax.ppermute(values, axis, [(k, k ^ bits) for k in range(size)])


def reduce_round(kept, axis, unit, ways, split):
    if not split:
        low = kept.astype(BF16)
        others = [flip(low, axis, p * unit).astype(F32) for p in range(1, ways)]
        return tree_sum([low.astype(F32)] + others)
    me = (lax.axis_index(axis) // unit) % ways
    pieces = kept.reshape(ways, kept.shape[0] // ways, kept.shape[1])
    total = lax.dynamic_index_in_dim(pieces, me, 0, keepdims=False)
    for p in range(1, ways):
        piece = lax.dynamic_index_in_dim(pieces, me ^ p, 0, keepdims=False)
        total = total + flip(piece.astype(BF16), axis, p * unit).astype(F32)
    return total


def gather_round(piece, axis, unit, ways, split):
    if not split:
        return piece
    return jnp.concatenate([piece] + [flip(piece, axis, p * unit) for p in range(1, ways)], axis=0)


def exchange(keep, send, rounds, before_gather=None, before_last=None):
    kept = keep.astype(F32) + flip(send, "col", 1).astype(F32)
    for one in rounds:
        kept = reduce_round(kept, *one)
    piece = kept.astype(BF16)
    if before_gather is not None:
        piece = tie(piece, before_gather)
    for k, one in enumerate(reversed(rounds)):
        if before_last is not None and k == len(rounds) - 1:
            piece = tie(piece, before_last)
        piece = gather_round(piece, *one)
    return piece, flip(piece, "col", 1)


def tie(first, *others):
    return lax.optimization_barrier((first, *others))[0]


def tree_sum(parts):
    while len(parts) > 1:
        parts = [parts[k] + parts[k + 1] for k in range(0, len(parts), 2)]
    return parts[0]


def sum_over(values, axis, unit, ways):
    return tree_sum([values] + [flip(values, axis, p * unit) for p in range(1, ways)])


def place_kernel(targets, rounds, last, ids_ref, own_ref, other_ref, *outs):
    col = ids_ref[0]
    row = ids_ref[1]
    half, width = own_ref.shape
    steps = []
    size = half
    for axis, unit, ways, split in rounds:
        if split:
            size //= ways
            steps.append((axis, unit, ways, size))
    count = half // size
    places = outs[: len(targets) - 1] + outs[-1:] if last else outs
    for other, source in enumerate((own_ref, other_ref)):

        @pl.loop(0, count)
        def _(k):
            start = ((col & 1) ^ other) * half
            left = k
            weight = count
            for axis, unit, ways, step in steps:
                weight //= ways
                digit = left // weight
                left = left - digit * weight
                index = (col if axis == "col" else row) // unit % ways
                start = start + (index ^ digit) * step
            value = source[pl.ds(pl.multiple_of(k * size, 16), size), :].astype(F32)
            for first, past, by_row, ref in [target + (ref,) for target, ref in zip(targets, places)]:

                @pl.when((start >= first) & (start < past))
                def _():
                    inside = start - first
                    if by_row:
                        ref[pl.ds(pl.multiple_of(inside, 8), size), :] = value
                    else:
                        lane = pl.multiple_of((inside // width) * width, 128)
                        ref[pl.ds(pl.multiple_of(inside % width, 8), size), pl.ds(lane, width)] = value

    if last:
        first_gain, second_gain, loss, moved, small = outs[-5:]
        first_gain[...] = small[0, :]
        second_gain[...] = small[1, :]
        lane = lax.broadcasted_iota(jnp.int32, (1, 128), 1)
        stat = small[2:3, :128]
        loss[0] = jnp.sum(jnp.where(lane == 0, stat, 0.0))
        moved[0] = jnp.sum(jnp.where(lane == 1, stat, 0.0))


def place(ids, gathered, targets, rounds, shapes, last=False):
    width = gathered[0].shape[1]
    specs = [VMEM] * len(shapes)
    made = [jax.ShapeDtypeStruct(shape, F32) for shape in shapes]
    scratch = []
    if last:
        specs = specs + [VMEM, VMEM, SMEM, SMEM]
        made = made + [jax.ShapeDtypeStruct((size,), F32) for size in (width, width, 1, 1)]
        scratch = [pltpu.VMEM((128, width), F32)]
    return pl.pallas_call(
        functools.partial(place_kernel, targets, rounds, last),
        in_specs=[SMEM, VMEM, VMEM],
        out_specs=specs,
        out_shape=made,
        scratch_shapes=scratch,
        compiler_params=params(SIM_LIMIT),
        name="place_gradients",
    )(ids, *gathered)


def body(
    image_tokens, text_tokens, lengths, pair_count, img_qkv, img_out, img_up, img_down, img_proj,
    gain_one, txt_qkv, txt_out, gain_two, txt_up, txt_down, txt_proj, log_scale,
):
    pairs, _, width = image_tokens.shape
    ff = txt_up.shape[1]
    row_index = lax.axis_index("row")
    col_index = lax.axis_index("col")
    row_count = lax.axis_size("row")
    col_count = lax.axis_size("col")
    high = col_count // 4
    cut = pairs - NB
    across = row_count - 1

    by_token = jnp.transpose(image_tokens, (1, 0, 2))
    got_images = flip(by_token[:, cut:], "row", across)
    got_texts = flip(text_tokens[cut:], "row", across)
    lens = lengths.astype(F32).reshape(pairs // QB, QB)
    got_lens = flip(lens[cut // QB :], "row", across)
    plan, rlive, tlive, scal = prepare(pair_count, log_scale, cut)
    gain_one = gain_one.reshape(1, width)
    gain_two = gain_two.reshape(1, width)

    weights = (img_qkv, img_out, img_up, img_down, img_proj)
    first_unit = image_tower(plan, by_token, None, 0, cut, cut, IMAGE_NB, 1.0, *weights)
    last_unit = lax.cond(
        plan[IMAGE_BLOCKS + cut // GROUP] > 0,
        lambda: image_tower(plan, by_token, got_images, cut, NB, cut, GROUP, 0.01, *weights),
        lambda: jnp.zeros((NB, width), BF16),
    )
    unit = jnp.concatenate([first_unit, last_unit], axis=0)
    parts = [unit] + [flip(unit, "col", 4 * p) for p in range(1, high)]
    qkv, att, y1 = text_first(plan, text_tokens, got_texts, lens, got_lens, cut, gain_one, txt_qkv, txt_out)
    parts = lax.optimization_barrier((*parts, y1))
    y1 = parts[-1]
    near = jnp.concatenate(parts[:-1], axis=0)
    beside = flip(near, "col", 2)
    core_near = flip(near, "col", 1)
    slopes, hsum, pooled, emb, text_low = text_second(
        plan, y1, lens, got_lens, cut, gain_two, txt_up, txt_down, txt_proj
    )
    images = [near, core_near, beside, flip(tie(beside, text_low), "col", 1)]
    texts = [text_low] + [flip(text_low, "row", p) for p in range(1, row_count)]
    rowsum, colsum = sim_sums(plan, scal, texts, tlive, rlive, images)
    total_col = colsum
    for p in range(1, row_count):
        other = flip(colsum, "row", p)
        total_col = total_col + jnp.concatenate([other[k ^ p : (k ^ p) + 1] for k in range(row_count)], axis=0)
    for bit in range(2, (high * 4).bit_length() - 1):
        rowsum = rowsum + flip(rowsum, "col", 1 << bit)
    rowsum = sum_over(rowsum, "col", 1, 4)
    *duns, stat = sim_grads(plan, scal, texts, tlive, rlive, rowsum, total_col, images)
    others = [flip(duns[p], "row", p) for p in range(1, row_count)]
    split_row = width * 2 % (row_count * 2 * 2 * 16) == 0
    along_row = ("row", 1, row_count, split_row)
    along_y = ("col", 2, 2, True)
    along_z = ("col", 4, 2, high % 2 == 0)
    along_far = ("col", 8, high // 2, False)
    order_a = [along_row, along_y, along_z, along_far]
    order_b = [along_y, along_z, along_row, along_far]
    order_c = [along_z, along_row, along_y, along_far]
    qkv = pltpu.with_memory_space_constraint(qkv, pltpu.HBM)
    text_grad, keep_a, send_a, keep_b, send_b, keep_c, send_c = text_backward(
        plan, text_tokens, qkv, att, y1, slopes, got_texts, lens, got_lens, cut, duns[0], emb, pooled, hsum,
        gain_one, txt_qkv, txt_out, gain_two, txt_up, txt_down, txt_proj, others, stat,
    )
    back = flip(text_grad[cut:], "row", across)
    low_half = row_index < row_count // 2
    counts = pair_count[:, col_index]
    balanced = jnp.where(low_half, counts[row_index], counts[row_index ^ across]) <= cut
    last = jnp.where(balanced, jnp.where(low_half, jnp.zeros_like(back), back), text_grad[cut:])
    text_grad = lax.dynamic_update_slice_in_dim(text_grad, last, cut, 0)
    orders = [order_a, order_b, order_c]
    targets = [
        [(0, ff, True), (ff, ff + width, True), (ff + width, ff + width + 128, True)],
        [(0, ff, False)],
        [(0, width, True), (width, 4 * width, False)],
    ]
    shapes = [[(ff, width), (width, width)], [(width, ff)], [(width, width), (width, 3 * width)]]
    placed = []
    waits = [(back, None), (None, None), (None, None)]
    for keep, send, rounds, places, sizes in zip((keep_a, keep_b, keep_c), (send_a, send_b, send_c), orders, targets, shapes):
        gathered = exchange(keep, send, rounds, *waits.pop(0))
        placed += place(plan, gathered, places, rounds, sizes, not placed)
    sum_down, sum_proj, sum_one, sum_two, loss, sum_scale, sum_up, sum_out, sum_qkv = placed
    return (
        loss, text_grad, sum_one, sum_qkv, sum_out, sum_two, sum_up, sum_down, sum_proj, sum_scale,
    )


def solution(mesh):
    return jax.shard_map(
        body,
        mesh=mesh,
        in_specs=(
            P(("row", "col"), None, None),
            P(("row", "col"), None, None),
            P(("row", "col")),
            P(),
            P(),
            P(),
            P(),
            P(),
            P(),
            P(),
            P(),
            P(),
            P(),
            P(),
            P(),
            P(),
            P(),
        ),
        out_specs=(P(), P(("row", "col"), None, None), P(), P(), P(), P(), P(), P(), P(), P()),
        check_vma=False,
    )
```

```python
import functools
import jax
import jax.numpy as jnp
from jax import lax
from jax.experimental import pallas as pl
from jax.experimental.pallas import tpu as pltpu
from jax.sharding import PartitionSpec as P

HEADS = 6
HEAD = 64
epsilon = 1e-6
F32 = jnp.float32
BF16 = jnp.bfloat16
GELU_A = 0.7978845608028654
GELU_B = 0.7978845608028654 * 0.044715
SAFE = 60.0
GROUP = 8
PITCH = 9
IMAGE_NB = 16
USE = 2
ACTIVE = 3
ORDER = 4
ORDER_ALL = 8
IMAGE_BLOCKS = 12
PLAN = 28
NB = 32
QB = 16
T1_LIMIT = 20
T2_LIMIT = 20
BACK_LIMIT = 30
SIM_LIMIT = 12


def mm(a, b):
    return lax.dot_general(a, b, (((1,), (0,)), ((), ())), preferred_element_type=F32)


def mm_t(a, b):
    return lax.dot_general(a, b, (((1,), (1,)), ((), ())), preferred_element_type=F32)


def mm_split(a, b):
    hi = a.astype(BF16)
    lo = (a - hi.astype(F32)).astype(BF16)
    return mm(hi, b) + mm(lo, b)


def column_chunks(width):
    edge = width // 2 // 256 * 256
    return ((0, edge), (edge, width))


def over(a, b):
    r = pl.reciprocal(b, approx=True)
    return a * (r * (2.0 - b * r))


def normed(v):
    c = v - jnp.mean(v, axis=-1, keepdims=True)
    return c * lax.rsqrt(jnp.mean(c * c, axis=-1, keepdims=True) + epsilon)


def unit_scale(e):
    return lax.rsqrt(jnp.sum(e * e, axis=-1, keepdims=True) + epsilon)


def lane_halves():
    lane = lax.broadcasted_iota(jnp.int32, (1, 128), 1)
    low = (lane < HEAD).astype(F32)
    return low, 1.0 - low


def image_kernel(first, cut, plan_ref, x_ref, recv_ref, wqkv_ref, wout_ref, wup_ref, wdown_ref, wproj_ref, unit_ref, qkv, att, hsum, xsum):
    step = pl.program_id(0)
    length, nb, width = x_ref.shape
    rows = length * GROUP

    @pl.when(step == 0)
    def _():
        qkv[...] = jnp.zeros_like(qkv)
        hsum[...] = jnp.zeros_like(hsum)
        xsum[...] = jnp.zeros_like(xsum)

    block = first // nb + step

    @pl.when(plan_ref[IMAGE_BLOCKS + block * (nb // GROUP)] > 0)
    def _():
        image_block(step, block, cut, plan_ref, x_ref, recv_ref, wqkv_ref, wout_ref, wup_ref, qkv, att, hsum, xsum)

    @pl.when(step == pl.num_programs(0) - 1)
    def _():
        pooled = xsum[...] * (1.0 / length) + mm_split(hsum[...] * (0.5 / length), wdown_ref[...])
        e = mm(pooled.astype(BF16), wproj_ref[...])
        unit_ref[...] = (e * unit_scale(e)).astype(BF16)


def image_block(step, block, cut, plan_ref, x_ref, recv_ref, wqkv_ref, wout_ref, wup_ref, qkv, att, hsum, xsum):
    length, nb, width = x_ref.shape
    rows = length * GROUP
    slots = qkv.shape[2] // PITCH
    tiles = width // 128
    ff = wup_ref.shape[1]
    groups = nb // GROUP
    moved = (plan_ref[USE] > 0) & (block >= cut // nb)

    def tokens(g):
        x = x_ref[...].astype(F32)
        if recv_ref is not None:
            x = jnp.where(moved, recv_ref[...].astype(F32), x)
        return x[:, g * GROUP : (g + 1) * GROUP, :].reshape(rows, width)

    low, high = lane_halves()
    key_row = lax.broadcasted_iota(jnp.int32, (2 * slots, 128), 0)
    key_lane = lax.broadcasted_iota(jnp.int32, (2 * slots, 128), 1)
    own_head = (key_row < slots) == (key_lane < HEAD)
    real = jnp.where(key_row < slots, key_row, key_row - slots) < length
    ones = jnp.where(own_head & real, 1.0, 0.0).astype(BF16)

    def pairs_of(g):
        return pl.ds(pl.multiple_of(step * nb + g * GROUP, GROUP), GROUP)

    def scores(g, p, h):
        at = pl.ds(p, slots, stride=PITCH)
        q = qkv[g, h, at, :].astype(BF16) * BF16(HEAD**-0.5)
        k = qkv[g, tiles + h, at, :]
        return mm_t(q, jnp.concatenate([k * low, k * high], axis=0).astype(BF16))

    def weighted(g, p, h, e):
        at = pl.ds(p, slots, stride=PITCH)
        v = qkv[g, 2 * tiles + h, at, :]
        vbd = jnp.concatenate([v * low, v * high], axis=0).astype(BF16)
        o = mm(e.astype(BF16), jnp.concatenate([vbd, ones], axis=1))
        att[g, h, at, :] = over(o[:, :128], o[:, 128:])

    def projected(g):
        n1 = normed(tokens(g)).astype(BF16)
        for first, last in column_chunks(3 * width):
            made = mm(n1, wqkv_ref[:, first:last])
            for c in range(first // 128, last // 128):
                here = c * 128 - first
                for t in range(length):
                    qkv[g, c, t * PITCH : t * PITCH + GROUP, :] = made[t * GROUP : (t + 1) * GROUP, here : here + 128]

    def after_attention(g):
        heads = jnp.concatenate(
            [
                jnp.concatenate([att[g, h, t * PITCH : t * PITCH + GROUP, :] for t in range(length)], axis=0)
                for h in range(tiles)
            ],
            axis=1,
        )
        x1 = tokens(g) + mm(heads.astype(BF16), wout_ref[...])
        xsum[pairs_of(g), :] = jnp.sum(x1.reshape(length, GROUP, width), axis=0)
        return normed(x1).astype(BF16)

    def gelu_sum(g, u, c):
        made = u * (1.0 + jnp.tanh(u * (GELU_A + GELU_B * (u * u))))
        hsum[pairs_of(g), pl.ds(c, 256)] = jnp.sum(made.reshape(length, GROUP, 256), axis=0)

    def feed_steps(g):
        n2 = after_attention(g)
        before = None
        for c in range(0, ff, 256):
            u = mm(n2, wup_ref[:, c : c + 256])
            if before is not None:
                gelu_sum(g, *before)
            before = (u, c)
            yield
        gelu_sum(g, *before)
        yield

    largest = jnp.zeros((slots, 2 * slots), F32)
    units = [(p, h) for p in range(GROUP) for h in range(tiles)]
    ahead = 4
    feed = iter(())
    projected(0)
    for g in range(groups):
        s_list, e_list = {}, {}
        for k in range(len(units) + 2 * ahead):
            if k < len(units):
                s_list[k] = scores(g, *units[k])
            if 0 <= k - ahead < len(units):
                s = s_list.pop(k - ahead)
                largest = jnp.maximum(largest, jnp.abs(s))
                e_list[k - ahead] = jnp.exp(s)
            if 0 <= k - 2 * ahead < len(units):
                weighted(g, *units[k - 2 * ahead], e_list.pop(k - 2 * ahead))
            if k % 4 == 2:
                next(feed, None)
            if k == len(units) // 2 and g + 1 < groups:
                projected(g + 1)
        for _ in feed:
            pass
        feed = feed_steps(g)
    for _ in feed:
        pass

    @pl.when(jnp.logical_not(jnp.max(largest) <= SAFE))
    def _():
        key = lax.broadcasted_iota(jnp.int32, (1, 2 * slots), 1)
        in_low = key < slots
        for_low = key < length
        for_high = (key >= slots) & (key < slots + length)
        @pl.loop(0, groups)
        def _(g):
            @pl.loop(0, GROUP)
            def _(p):
                @pl.loop(0, tiles)
                def _(h):
                    s = scores(g, p, h)
                    top_low = jnp.max(jnp.where(for_low, s, -1e30), axis=1, keepdims=True)
                    top_high = jnp.max(jnp.where(for_high, s, -1e30), axis=1, keepdims=True)
                    s = jnp.where(for_low | for_high, s, -1e30) - jnp.where(in_low, top_low, top_high)
                    weighted(g, p, h, jnp.exp(s))

        for g in range(groups):
            n2 = after_attention(g)

            @pl.loop(0, ff // 256)
            def _(c):
                at = pl.multiple_of(c * 256, 256)
                gelu_sum(g, mm(n2, wup_ref[:, pl.ds(at, 256)]), at)


def fixed(shape):
    zeros = (0,) * len(shape)
    return pl.BlockSpec(shape, lambda *_: zeros, pipeline_mode=pl.Buffered(1))


def image_tower(plan, tokens, received, first, count, cut, nb, cost, wqkv, wout, wup, wdown, wproj):
    length, _, width = tokens.shape
    slots = -(-length // 8) * 8
    ff = wup.shape[1]
    weights = (wqkv, wout, wup, wdown, wproj)
    at = first // nb
    specs = [pl.BlockSpec((length, nb, width), lambda i, plan: (0, at + i, 0))]
    if received is None:
        kernel = lambda plan_ref, x_ref, *refs: image_kernel(first, cut, plan_ref, x_ref, None, *refs)
        arrays = (tokens,)
    else:
        kernel = functools.partial(image_kernel, first, cut)
        last = received.shape[1] // nb - 1
        specs.append(
            pl.BlockSpec((length, nb, width), lambda i, plan: (0, jnp.clip(at + i - cut // nb, 0, last), 0))
        )
        arrays = (tokens, received)
    return pl.pallas_call(
        kernel,
        grid_spec=pltpu.PrefetchScalarGridSpec(
            num_scalar_prefetch=1,
            grid=(count // nb,),
            in_specs=specs + [fixed(w.shape) for w in weights],
            out_specs=pl.BlockSpec((count, width), lambda i, plan: (0, 0)),
            scratch_shapes=[
                pltpu.VMEM((nb // GROUP, 3 * width // 128, slots * PITCH, 128), F32),
                pltpu.VMEM((nb // GROUP, width // 128, slots * PITCH, 128), F32),
                pltpu.VMEM((count, ff), F32),
                pltpu.VMEM((count, width), F32),
            ],
        ),
        out_shape=jax.ShapeDtypeStruct((count, width), BF16),
        compiler_params=pltpu.CompilerParams(vmem_limit_bytes=60 * 2**20),
        cost_estimate=pl.CostEstimate(
            flops=int(cost * 2 * count * length * width * (4 * width + ff)),
            bytes_accessed=int(cost * (count * length * width * 2 + 4 * 2**20)),
            transcendentals=int(cost * count * length * ff),
        ),
        name="image_block",
    )(plan, *arrays, *weights)


def mm_tn(a, b):
    return lax.dot_general(a, b, (((0,), (0,)), ((), ())), preferred_element_type=F32)


def stats(v):
    c = v - jnp.mean(v, axis=-1, keepdims=True)
    inv = lax.rsqrt(jnp.mean(c * c, axis=-1, keepdims=True) + epsilon)
    return c * inv, inv


def norm_back(g, n, inv):
    return inv * (
        g - jnp.mean(g, axis=-1, keepdims=True) - n * jnp.mean(g * n, axis=-1, keepdims=True)
    )


def staggered(stages, units, ahead):
    kept = [dict() for _ in stages]
    for k in range(len(units) + (len(stages) - 1) * ahead):
        for at, stage in enumerate(stages):
            u = k - at * ahead
            if 0 <= u < len(units):
                made = stage(units[u], *([kept[at - 1].pop(u)] if at else []))
                kept[at][u] = made


def same_pair(length):
    row = lax.broadcasted_iota(jnp.int32, (128, 128), 0) // length
    lane = lax.broadcasted_iota(jnp.int32, (128, 128), 1) // length
    return row == lane


SMEM = pl.BlockSpec(memory_space=pltpu.SMEM)
VMEM = pl.BlockSpec(memory_space=pltpu.VMEM)


def params(limit=60):
    return pltpu.CompilerParams(vmem_limit_bytes=limit * 2**20)


def as_column(row):
    size = row.shape[1]
    diagonal = lax.broadcasted_iota(jnp.int32, (size, size), 0) == lax.broadcasted_iota(jnp.int32, (size, size), 1)
    return jnp.sum(jnp.where(diagonal, row, 0.0), axis=1, keepdims=True)


def as_row(col):
    size = col.shape[0]
    diagonal = lax.broadcasted_iota(jnp.int32, (size, size), 0) == lax.broadcasted_iota(jnp.int32, (size, size), 1)
    return jnp.sum(jnp.where(diagonal, col, 0.0), axis=0, keepdims=True)


def prepare_kernel(cut, count_ref, scale_ref, plan_ref, rlive_ref, tlive_ref, scal_ref):
    rows, cols = count_ref.shape
    across = rows - 1
    col = lax.axis_index("col")
    row = lax.axis_index("row")

    def limits(r, c):
        n = count_ref[r, c]
        other = count_ref[r ^ across, c]
        low = r < rows // 2
        balanced = jnp.where(low, n, other) <= cut
        return n, jnp.where(balanced, jnp.where(low, other, 0), n), low & balanced

    def mask(r, c):
        first, last, _ = limits(r, c)
        slot = lax.broadcasted_iota(jnp.int32, (1, 128), 1)
        return jnp.where(slot < jnp.where(slot < cut, first, last), 1.0, 0.0)

    for c in range(cols):
        rlive_ref[c : c + 1, :] = mask(row, c)
    for p in range(rows):
        tlive_ref[p : p + 1, :] = mask(row ^ p, col)
    first, last, use = limits(row, col)
    limit = lambda start: first if start < cut else last
    plan_ref[0] = col
    plan_ref[1] = row
    plan_ref[USE] = use.astype(jnp.int32)
    blocks = 128 // NB
    active = [(b * NB < limit(b * NB)).astype(jnp.int32) for b in range(blocks)]
    count = sum(active)
    before = jnp.int32(0)
    for b in range(blocks):
        plan_ref[ORDER_ALL + jnp.where(active[b] > 0, before, count + b - before)] = b
        before = before + active[b]
    for i in range(blocks):
        plan_ref[ORDER + i] = plan_ref[ORDER_ALL + jnp.minimum(i, count - 1)]
    plan_ref[ACTIVE] = count
    for b in range(128 // GROUP):
        plan_ref[IMAGE_BLOCKS + b] = (b * GROUP < limit(b * GROUP)).astype(jnp.int32)
    total = jnp.int32(0)
    for r in range(rows):
        for c in range(cols):
            total = total + count_ref[r, c]
    index = lax.broadcasted_iota(jnp.int32, (8, 128), 0)
    scal_ref[...] = jnp.where(index == 0, jnp.exp(jnp.full((8, 128), scale_ref[0], F32)), 0.5 / jnp.full((8, 128), total, jnp.int32).astype(F32))


def prepare(pair_count, log_scale, cut):
    rows, cols = pair_count.shape
    return pl.pallas_call(
        functools.partial(prepare_kernel, cut),
        in_specs=[SMEM] * 2,
        out_specs=[SMEM, VMEM, VMEM, VMEM],
        out_shape=[
            jax.ShapeDtypeStruct((PLAN,), jnp.int32),
            jax.ShapeDtypeStruct((cols, 128), F32),
            jax.ShapeDtypeStruct((rows, 128), F32),
            jax.ShapeDtypeStruct((8, 128), F32),
        ],
        name="prepare",
    )(pair_count, log_scale)


def lengths_of(plan_ref, cut, part, lens_ref, got_ref):
    moved = (plan_ref[USE] > 0) & (part * QB >= cut)
    got = got_ref[pl.ds(jnp.maximum(part - cut // QB, 0), 1), :]
    return as_column(jnp.where(moved, got, lens_ref[pl.ds(part, 1), :]))


def block_lengths(plan_ref, cut, block, lens_ref, got_ref):
    parts = [lengths_of(plan_ref, cut, block * (NB // QB) + k, lens_ref, got_ref) for k in range(NB // QB)]
    return jnp.concatenate(parts, axis=0)


def all_lengths(plan_ref, cut, lens_ref, got_ref):
    parts = [lengths_of(plan_ref, cut, b, lens_ref, got_ref) for b in range(lens_ref.shape[0])]
    return jnp.concatenate(parts, axis=0)


def live_pick(lens, rows):
    pairs = lens.shape[0]
    length = rows // pairs
    token = lax.broadcasted_iota(jnp.int32, (pairs, rows), 1)
    own = token // length == lax.broadcasted_iota(jnp.int32, (pairs, rows), 0)
    return jnp.where(own & ((token % length).astype(F32) < lens), 1.0, 0.0)


def text_tokens_of(plan_ref, cut, block, x_ref, recv_ref):
    nb, length, width = x_ref.shape
    moved = (plan_ref[USE] > 0) & (block * nb >= cut)
    x = jnp.where(moved, recv_ref[...].astype(F32), x_ref[...].astype(F32))
    return x.reshape(nb * length, width)


def ordered(width, rows):
    return pl.BlockSpec((rows, width), lambda i, plan: (plan[ORDER + i], 0))


def ordered_pairs(shape, order=ORDER):
    return pl.BlockSpec((NB,) + shape[1:], lambda i, plan: (plan[order + i], 0, 0))


def held(shape):
    zeros = (0,) * len(shape)
    return pl.BlockSpec(shape, lambda i, plan: zeros)


def text_first_kernel(cut, plan_ref, x_ref, recv_ref, lens_ref, got_ref, gain_ref, wqkv_ref, wout_ref, qkv_ref, att_ref, y1_ref):
    step = pl.program_id(0)
    block = plan_ref[ORDER + step]

    @pl.when(step < plan_ref[ACTIVE])
    def _():
        x = text_tokens_of(plan_ref, cut, block, x_ref, recv_ref)
        lens = block_lengths(plan_ref, cut, block, lens_ref, got_ref)
        text_attention(x, lens, x_ref.shape[1], gain_ref, wqkv_ref, wout_ref, qkv_ref, att_ref, y1_ref)


def text_attention(x, lens, length, gain_ref, wqkv_ref, wout_ref, qkv_ref, att_ref, y1_ref):
    rows, width = x.shape
    n1 = (normed(x) * gain_ref[...]).astype(BF16)
    for first, last in column_chunks(3 * width):
        qkv_ref[:, first:last] = mm(n1, wqkv_ref[:, first:last]).astype(BF16)
    lane = lax.broadcasted_iota(jnp.int32, (128, 128), 1)
    low = (lane[:1] < HEAD).astype(BF16)
    high = 1 - low
    half = lax.broadcasted_iota(jnp.int32, (256, 128), 0) < 128
    ones = jnp.where(half == (lax.broadcasted_iota(jnp.int32, (256, 128), 1) < HEAD), 1.0, 0.0).astype(BF16)
    same = same_pair(length)
    live = jnp.sum(live_pick(lens, rows), axis=0, keepdims=True)
    bias = {g: jnp.where(same & (live[:, g : g + 128] > 0), 0.0, -1e30) for g in range(0, rows, 128)}

    def scores(unit):
        g, h = unit
        q = qkv_ref[g : g + 128, h : h + 128] * BF16(HEAD**-0.5)
        k = qkv_ref[g : g + 128, width + h : width + h + 128]
        return mm_t(q, jnp.concatenate([k * low, k * high], axis=0))

    def expo(unit, s):
        one = bias[unit[0]]
        parts = [s[:, :128] + one, s[:, 128:] + one]
        return jnp.concatenate([jnp.exp(p - jnp.max(p, axis=1, keepdims=True)) for p in parts], axis=1).astype(BF16)

    def weighted(unit, e):
        g, h = unit
        v = qkv_ref[g : g + 128, 2 * width + h : 2 * width + h + 128]
        vbd = jnp.concatenate([v * low, v * high], axis=0)
        o = mm(e, jnp.concatenate([vbd, ones], axis=1))
        att_ref[g : g + 128, h : h + 128] = over(o[:, :128], o[:, 128:]).astype(BF16)

    staggered([scores, expo, weighted], [(g, h) for g in range(0, rows, 128) for h in range(0, width, 128)], 2)
    y1_ref[...] = x + mm(att_ref[...], wout_ref[...])


def text_first(plan, x, received, lens, got, cut, gain_one, wqkv, wout):
    pairs, length, width = x.shape
    rows = NB * length
    tokens = pairs * length
    rest = (received, lens, got, gain_one, wqkv, wout)
    wide = [(3 * width, BF16), (width, BF16), (width, F32)]
    return pl.pallas_call(
        functools.partial(text_first_kernel, cut),
        grid_spec=pltpu.PrefetchScalarGridSpec(
            num_scalar_prefetch=1,
            grid=(pairs // NB,),
            in_specs=[ordered_pairs(x.shape)] + [fixed(w.shape) for w in rest],
            out_specs=[ordered(w, rows) for w, _ in wide],
        ),
        out_shape=[(pltpu.HBM if k == 0 else jax.ShapeDtypeStruct)((tokens, w), kind) for k, (w, kind) in enumerate(wide)],
        compiler_params=params(T1_LIMIT),
        cost_estimate=pl.CostEstimate(flops=2 * tokens * width * 5 * width, bytes_accessed=12 * 2**20, transcendentals=0),
        name="text_attention",
    )(plan, x, *rest)


def text_second_kernel(
    cut, plan_ref, y1_ref, lens_ref, got_ref, gain_two_ref, wup_ref, wdown_ref, wproj_ref,
    slope_ref, hsum_ref, pooled_ref, emb_ref, low_ref, ysum,
):
    step = pl.program_id(0)
    block = plan_ref[ORDER + step]

    @pl.when(step == 0)
    def _():
        hsum_ref[...] = jnp.zeros_like(hsum_ref)
        ysum[...] = jnp.zeros_like(ysum)

    @pl.when(step < plan_ref[ACTIVE])
    def _():
        rows = y1_ref.shape[0]
        y1 = y1_ref[...]
        pick = live_pick(block_lengths(plan_ref, cut, block, lens_ref, got_ref), rows).astype(BF16)
        pair = pl.ds(pl.multiple_of(block * NB, NB), NB)
        y1_hi = y1.astype(BF16)
        ysum[pair, :] = mm(pick, y1_hi) + mm(pick, (y1 - y1_hi.astype(F32)).astype(BF16))
        n2 = (normed(y1) * gain_two_ref[...]).astype(BF16)

        live = mm_tn(pick, jnp.ones((NB, 128), BF16))
        live = jnp.concatenate([live, live], axis=1)

        def gelu_parts(u, c):
            square = u * u
            t = 1.0 + jnp.tanh(u * (GELU_A + GELU_B * square))
            half = 0.5 * u
            hsum_ref[pair, c : c + 256] = mm(pick, (half * t).astype(BF16))
            d = t * (0.5 + (2.0 - t) * (half * (GELU_A + (3.0 * GELU_B) * square)))
            slope_ref[:, c : c + 256] = (d * live).astype(BF16)

        in_chunks(n2, wup_ref, gelu_parts)

    @pl.when(step == pl.num_programs(0) - 1)
    def _():
        inv_len = 1.0 / all_lengths(plan_ref, cut, lens_ref, got_ref)
        pooled = (ysum[...] * inv_len + mm_split(hsum_ref[...] * inv_len, wdown_ref[...])).astype(BF16)
        pooled_ref[...] = pooled
        e = mm(pooled, wproj_ref[...])
        emb_ref[...] = e
        low_ref[...] = (e * unit_scale(e)).astype(BF16)


def in_chunks(left, right_ref, use):
    before = None
    for c in range(0, right_ref.shape[1], 256):
        u = mm(left, right_ref[:, c : c + 256])
        if before is not None:
            use(*before)
        before = (u, c)
    use(*before)


def text_second(plan, y1, lens, got, cut, gain_two, wup, wdown, wproj):
    tokens, width = y1.shape
    pairs = lens.size
    rows = NB * tokens // pairs
    ff = wup.shape[1]
    rest = (lens, got, gain_two, wup, wdown, wproj)
    flat = [((pairs, ff), F32), ((pairs, width), BF16), ((pairs, width), F32), ((pairs, width), BF16)]
    return pl.pallas_call(
        functools.partial(text_second_kernel, cut),
        grid_spec=pltpu.PrefetchScalarGridSpec(
            num_scalar_prefetch=1,
            grid=(pairs // NB,),
            in_specs=[ordered(width, rows)] + [fixed(w.shape) for w in rest],
            out_specs=[ordered(ff, rows)] + [held(shape) for shape, _ in flat],
            scratch_shapes=[pltpu.VMEM((pairs, width), F32)],
        ),
        out_shape=[jax.ShapeDtypeStruct((tokens, ff), BF16)] + [jax.ShapeDtypeStruct(shape, kind) for shape, kind in flat],
        compiler_params=params(T2_LIMIT),
        cost_estimate=pl.CostEstimate(flops=2 * tokens * width * ff, bytes_accessed=12 * 2**20, transcendentals=tokens * ff),
        name="text_pool",
    )(plan, y1, *rest)


def image_groups(image_refs):
    for j, ref in enumerate(image_refs):
        yield j, ref.shape[0] // 128, len(image_refs), ref[...]


def sums_kernel(rows, ids_ref, scal_ref, tlive_ref, rlive_ref, *refs):
    text_refs = refs[:rows]
    image_refs = refs[rows:-2]
    rowsum_ref, colsum_ref = refs[-2:]
    me = ids_ref[0]
    scale = scal_ref[:1, :1]
    text = jnp.concatenate([ref[...] for ref in text_refs], axis=0)
    tlive = jnp.concatenate([as_column(tlive_ref[p : p + 1, :]) for p in range(rows)], axis=0)
    col = jnp.zeros((rows * 128, 1), F32)
    for j, high, low, images in image_groups(image_refs):
        e = jnp.exp(scale * mm_t(text, images)) * tlive
        total = jnp.sum(e, axis=0, keepdims=True)
        kept = jnp.zeros((rows * 128, 128), F32)
        for i in range(high):
            at = pl.ds(me ^ (low * i + j), 1)
            rowsum_ref[at, :] = total[:, i * 128 : i * 128 + 128]
            kept = kept + e[:, i * 128 : i * 128 + 128] * rlive_ref[at, :]
        col = col + jnp.sum(kept, axis=1, keepdims=True)
    for p in range(rows):
        colsum_ref[p : p + 1, :] = as_row(col[p * 128 : p * 128 + 128])


def sim_sums(ids, scal, texts, tlive, rlive, images):
    cols = rlive.shape[0]
    rows = len(texts)
    return pl.pallas_call(
        functools.partial(sums_kernel, rows),
        in_specs=[SMEM] + [VMEM] * (3 + rows + len(images)),
        out_specs=[VMEM, VMEM],
        out_shape=[jax.ShapeDtypeStruct((cols, 128), F32), jax.ShapeDtypeStruct((rows, 128), F32)],
        compiler_params=params(SIM_LIMIT),
        cost_estimate=pl.CostEstimate(
            flops=2 * rows * 128 * cols * 128 * 384, bytes_accessed=cols * 128 * 768, transcendentals=rows * cols * 128 * 128
        ),
        name="similarity_sums",
    )(ids, scal, tlive, rlive, *texts, *images)


def grad_kernel(rows, ids_ref, scal_ref, tlive_ref, rlive_ref, rowsum_ref, colsum_ref, *refs):
    text_refs = refs[:rows]
    image_refs = refs[rows : -rows - 1]
    dun_refs = refs[-rows - 1 : -1]
    stat_ref = refs[-1]
    me = ids_ref[0]
    scale = scal_ref[:1, :1]
    inv = scal_ref[1:2, :1]
    text = jnp.concatenate([ref[...] for ref in text_refs], axis=0)
    tlive = jnp.concatenate([as_column(tlive_ref[p : p + 1, :]) for p in range(rows)], axis=0)
    col = jnp.concatenate([as_column(colsum_ref[p : p + 1, :]) for p in range(rows)], axis=0)
    col = jnp.where(tlive > 0, col, 1.0)
    col_inv = inv / col
    total = jnp.zeros(text.shape, F32)
    moved = jnp.zeros((1, 128), F32)
    for j, high, low, images in image_groups(image_refs):
        s = scale * mm_t(text, images)
        e = jnp.exp(s) * tlive
        at = [pl.ds(me ^ (low * i + j), 1) for i in range(high)]
        rlive = jnp.concatenate([rlive_ref[one, :] for one in at], axis=1)
        row_inv = jnp.concatenate([inv / rowsum_ref[one, :] for one in at], axis=1)
        ds = (e * rlive) * (row_inv + col_inv)
        by_lane = jnp.sum(ds * s, axis=0, keepdims=True)
        for i in range(high):
            moved = moved + by_lane[:, i * 128 : i * 128 + 128]
        total = total + mm((scale * ds).astype(BF16), images)
        if j == 0:
            mine = images[:128].astype(F32)
    own_live = tlive[:128]
    cosine = jnp.sum(mine * text[:128].astype(F32), axis=1, keepdims=True)
    live_cosine = jnp.sum(cosine * own_live, axis=0, keepdims=True)
    at = pl.ds(me, 1)
    logs = jnp.sum(jnp.log(rowsum_ref[at, :]) * rlive_ref[at, :], axis=1, keepdims=True)
    logs = logs + jnp.sum(jnp.log(col[:128]) * own_live, axis=0, keepdims=True)
    loss = inv * (logs - 2.0 * scale * live_cosine)
    scale_part = jnp.sum(moved, axis=1, keepdims=True) - 2.0 * inv * scale * live_cosine
    dun_refs[0][...] = total[:128] + (scale * (-2.0 * inv * own_live)).astype(BF16).astype(F32) * mine
    for p in range(1, rows):
        dun_refs[p][...] = total[p * 128 : p * 128 + 128].astype(BF16)
    lane = lax.broadcasted_iota(jnp.int32, (8, 128), 1)
    stat_ref[...] = jnp.where(lane == 0, loss, jnp.where(lane == 1, scale_part, 0.0))


def sim_grads(ids, scal, texts, tlive, rlive, rowsum, colsum, images):
    cols = rlive.shape[0]
    rows = len(texts)
    return pl.pallas_call(
        functools.partial(grad_kernel, rows),
        in_specs=[SMEM] + [VMEM] * (5 + rows + len(images)),
        out_specs=[VMEM] * (rows + 1),
        out_shape=[jax.ShapeDtypeStruct(text.shape, BF16 if k else F32) for k, text in enumerate(texts)] + [jax.ShapeDtypeStruct((8, 128), F32)],
        compiler_params=params(SIM_LIMIT),
        cost_estimate=pl.CostEstimate(
            flops=4 * rows * 128 * cols * 128 * 384, bytes_accessed=cols * 128 * 768, transcendentals=rows * cols * 128 * 128
        ),
        name="similarity_grads",
    )(ids, scal, tlive, rlive, rowsum, colsum, *texts, *images)


def write_halves(core, blocks, keep_ref, send_ref):
    half = len(blocks) // 2
    size = blocks[0].shape[0]

    def put(first, second):
        for at, (kept, sent) in enumerate(zip(first, second)):
            keep_ref[at * size : (at + 1) * size, :] = kept.astype(BF16)
            send_ref[at * size : (at + 1) * size, :] = sent.astype(BF16)

    @pl.when(core == 0)
    def _():
        put(blocks[:half], blocks[half:])

    @pl.when(core != 0)
    def _():
        put(blocks[half:], blocks[:half])


def back_kernel(
    cut, others, plan_ref, x_ref, qkv_ref, att_ref, y1_ref, slope_ref, recv_ref, lens_ref, got_ref,
    dun_ref, emb_ref, pooled_ref, hsum_ref, gain_ref, wqkv_ref, wout_ref, gain_two_ref, wup_ref, wdown_ref, wproj_ref, *refs,
):
    other_refs = refs[:others]
    stat_ref = refs[others]
    grad_ref, keep_a, send_a, keep_b, send_b, keep_c, send_c = refs[others + 1 : others + 8]
    dyp, dhp, dproj, ddown, dmix, dheads, acc_up, acc_out, acc_qkv, bias_ref, du_ref = refs[others + 8 :]
    step = pl.program_id(0)
    block = plan_ref[ORDER + step]
    active = step < plan_ref[ACTIVE]
    width = dun_ref.shape[1]
    ff = hsum_ref.shape[1]

    @pl.when(step == 0)
    def _():
        acc_up[...] = jnp.zeros_like(acc_up)
        acc_out[...] = jnp.zeros_like(acc_out)
        acc_qkv[...] = jnp.zeros_like(acc_qkv)
        g = dun_ref[...]
        for other in other_refs:
            g = g + other[...].astype(F32)
        e = emb_ref[...]
        inv = unit_scale(e)
        t = e * inv
        demb = (inv * (g - t * jnp.sum(g * t, axis=-1, keepdims=True))).astype(BF16)
        dproj[...] = mm_tn(pooled_ref[...], demb)
        back = mm_t(demb, wproj_ref[...]) * (1.0 / all_lengths(plan_ref, cut, lens_ref, got_ref))
        dyp[...] = back
        db = back.astype(BF16)
        dhp[...] = mm_t(db, wdown_ref[...])
        h = hsum_ref[...]
        hi = h.astype(BF16)
        lo = (h - hi.astype(F32)).astype(BF16)
        ddown[...] = mm_tn(hi, db) + mm_tn(lo, db)

    @pl.when(active)
    def _():
        x = text_tokens_of(plan_ref, cut, block, x_ref, recv_ref)
        lens = block_lengths(plan_ref, cut, block, lens_ref, got_ref)
        grad = back_block(
            block, x, lens, x_ref.shape[1], qkv_ref, att_ref, y1_ref, slope_ref, gain_ref, wqkv_ref, wout_ref,
            gain_two_ref, wup_ref, dyp, dhp, dmix, dheads, acc_up, acc_out, acc_qkv, bias_ref, du_ref,
        )
        grad_ref[...] = grad.astype(BF16).reshape(grad_ref.shape)

    @pl.when(jnp.logical_not(active))
    def _():
        grad_ref[...] = jnp.zeros_like(grad_ref)

    @pl.when(step == pl.num_programs(0) - 1)
    def _():
        core = plan_ref[0] & 1
        index = lax.broadcasted_iota(jnp.int32, (128, width), 0)
        stat = jnp.concatenate([stat_ref[:1, :]] * (width // 128), axis=1)
        by_qkv = jnp.sum(acc_qkv[...] * wqkv_ref[...].astype(F32), axis=1, keepdims=True)
        by_up = jnp.sum(acc_up[...] * wup_ref[...].astype(F32), axis=1, keepdims=True)
        first = as_row(by_qkv) / gain_ref[...]
        second = as_row(by_up) / gain_two_ref[...]
        small = jnp.where(index == 0, first, jnp.where(index == 1, second, jnp.where(index == 2, stat, 0.0)))
        blocks = [ddown[at : at + 128, :] for at in range(0, ff, 128)]
        blocks += [dproj[at : at + 128, :] for at in range(0, width, 128)]
        write_halves(core, blocks + [small], keep_a, send_a)
        write_halves(core, [acc_up[:, c : c + width] for c in range(0, ff, width)], keep_b, send_b)
        blocks = [acc_out[...]] + [acc_qkv[:, c * width : (c + 1) * width] for c in range(3)]
        write_halves(core, blocks, keep_c, send_c)


def back_block(
    block, x, lens, length, qkv_ref, att_ref, y1_ref, slope_ref, gain_ref, wqkv_ref, wout_ref,
    gain_two_ref, wup_ref, dyp, dhp, dmix, dheads, acc_up, acc_out, acc_qkv, bias_ref, du_ref,
):
    rows, width = x.shape
    ff = wup_ref.shape[1]
    pair = pl.ds(pl.multiple_of(block * NB, NB), NB)

    def spread(values):
        return jnp.broadcast_to(values[:, None, :], (NB, length, values.shape[1])).reshape(rows, values.shape[1])

    n2, inv = stats(y1_ref[...])
    n2_low = (n2 * gain_two_ref[...]).astype(BF16)
    for c in range(0, ff, width):
        at = slice(c, c + width)
        du_ref[:, at] = (spread(dhp[pair, at]) * slope_ref[:, at].astype(F32)).astype(BF16)
    dn2 = mm_t(du_ref[...], wup_ref[...])
    acc_up[...] += mm_tn(n2_low, du_ref[...])
    live = mm_tn(live_pick(lens, rows).astype(BF16), jnp.ones((NB, 128), BF16))
    dy1 = spread(dyp[pair, :]) * jnp.concatenate([live] * (width // 128), axis=1)
    dy1 = dy1 + norm_back(dn2 * gain_two_ref[...], n2, inv)
    da = dy1.astype(BF16)
    acc_out[...] += mm_tn(att_ref[...], da)
    dheads[...] = mm_t(da, wout_ref[...]).astype(BF16)
    attention_grads(length, live, qkv_ref, dmix, dheads, bias_ref)
    n1, inv = stats(x)
    n1_low = (n1 * gain_ref[...]).astype(BF16)
    dn1 = mm_t(dmix[...], wqkv_ref[...])
    acc_qkv[...] += mm_tn(n1_low, dmix[...])
    return dy1 + norm_back(dn1 * gain_ref[...], n1, inv)


def attention_grads(length, live, qkv_ref, dmix, dheads, bias_ref):
    rows, width = dheads.shape
    lane = lax.broadcasted_iota(jnp.int32, (128, 128), 1)
    first = lane < HEAD
    low = first[:1].astype(BF16)
    high = 1 - low
    eye = (lane == lax.broadcasted_iota(jnp.int32, (128, 128), 0)).astype(BF16)
    same = same_pair(length)
    for g in range(rows // 128):
        bias_ref[g] = jnp.where(same & (live[g * 128 : g * 128 + 128, :] > 0), 0.0, -1e30)

    zero = jnp.zeros((128, 128), BF16)

    def both_sides(one, two):
        return jnp.concatenate(
            [jnp.concatenate([one, zero], axis=1), jnp.concatenate([zero, two], axis=1)], axis=0
        )

    def pieces(unit, part):
        g, h = unit
        return qkv_ref[pl.ds(g * 128, 128), part * width + h : part * width + h + 128]

    def scores(unit):
        g, h = unit
        k = pieces(unit, 1)
        v = pieces(unit, 2)
        do = dheads[pl.ds(g * 128, 128), h : h + 128]
        left = jnp.concatenate(
            [jnp.concatenate([k * low, v * low], axis=1), jnp.concatenate([k * high, v * high], axis=1)], axis=0
        )
        made = mm_t(left, both_sides(pieces(unit, 0) * BF16(HEAD**-0.5), do))
        return made[:, :128], made[:, 128:]

    def soft(unit, made):
        g, _ = unit
        s, dp = made
        s = s.reshape(2, 128, 128) + bias_ref[g][None]
        e = jnp.exp(s - jnp.max(s, axis=1, keepdims=True))
        p = e * (1.0 / jnp.sum(e, axis=1, keepdims=True))
        dp = dp.reshape(2, 128, 128)
        ds = p * (dp - jnp.sum(p * dp, axis=1, keepdims=True))
        return p.reshape(256, 128).astype(BF16), ds.reshape(256, 128).astype(BF16)

    def products(unit, made):
        g, h = unit
        p, ds = made
        at = pl.ds(g * 128, 128)
        do = dheads[at, h : h + 128]
        made = mm(jnp.concatenate([p, ds], axis=1), both_sides(do, pieces(unit, 0) * BF16(HEAD**-0.5)))
        dv = made[:, :128]
        dk = made[:, 128:]
        dmix[at, 2 * width + h : 2 * width + h + 128] = jnp.where(first, dv[:128], dv[128:]).astype(BF16)
        dmix[at, width + h : width + h + 128] = jnp.where(first, dk[:128], dk[128:]).astype(BF16)
        return mm_t(eye, ds).astype(BF16)

    def query(unit, ds):
        g, h = unit
        k = pieces(unit, 1)
        kbd = jnp.concatenate([k * low, k * high], axis=0)
        dmix[pl.ds(g * 128, 128), h : h + 128] = (mm(ds, kbd) * HEAD**-0.5).astype(BF16)

    staggered([scores, soft, products, query], [(g, h) for g in range(rows // 128) for h in range(0, width, 128)], 2)


def text_backward(
    plan, x, qkv, att, y1, slopes, received, lens, got, cut, dun, emb, pooled, hsum,
    gain_one, wqkv, wout, gain_two, wup, wdown, wproj, others, stat,
):
    pairs, length, width = x.shape
    rows = NB * length
    tokens = pairs * length
    ff = wup.shape[1]
    rest = (received, lens, got, dun, emb, pooled, hsum, gain_one, wqkv, wout, gain_two, wup, wdown, wproj, *others, stat)
    halves = [(ff + width + 128) // 2, ff // 2, 2 * width]
    shapes = [(half, width) for half in halves for _ in range(2)]
    return pl.pallas_call(
        functools.partial(back_kernel, cut, len(others)),
        grid_spec=pltpu.PrefetchScalarGridSpec(
            num_scalar_prefetch=1,
            grid=(pairs // NB,),
            in_specs=[ordered_pairs(x.shape), ordered(3 * width, rows), ordered(width, rows), ordered(width, rows), ordered(ff, rows)]
            + [fixed(w.shape) for w in rest],
            out_specs=[ordered_pairs(x.shape, ORDER_ALL)] + [held(shape) for shape in shapes],
            scratch_shapes=[
                pltpu.VMEM((pairs, width), F32),
                pltpu.VMEM((pairs, ff), F32),
                pltpu.VMEM((width, width), F32),
                pltpu.VMEM((ff, width), F32),
                pltpu.VMEM((rows, 3 * width), BF16),
                pltpu.VMEM((rows, width), BF16),
                pltpu.VMEM((width, ff), F32),
                pltpu.VMEM((width, width), F32),
                pltpu.VMEM((width, 3 * width), F32),
                pltpu.VMEM((rows // 128, 128, 128), F32),
                pltpu.VMEM((rows, ff), BF16),
            ],
        ),
        out_shape=[pltpu.HBM(x.shape, BF16)] + [pltpu.HBM(shape, BF16) for shape in shapes],
        compiler_params=params(BACK_LIMIT),
        cost_estimate=pl.CostEstimate(
            flops=2 * tokens * width * (10 * width + 2 * ff), bytes_accessed=24 * 2**20, transcendentals=0
        ),
        name="text_backward",
    )(plan, x, qkv, att, y1, slopes, *rest)


def flip(values, axis, bits):
    size = lax.axis_size(axis)
    return lax.ppermute(values, axis, [(k, k ^ bits) for k in range(size)])


def reduce_round(kept, axis, unit, ways, split):
    if not split:
        low = kept.astype(BF16)
        others = [flip(low, axis, p * unit).astype(F32) for p in range(1, ways)]
        return tree_sum([low.astype(F32)] + others)
    me = (lax.axis_index(axis) // unit) % ways
    pieces = kept.reshape(ways, kept.shape[0] // ways, kept.shape[1])
    total = lax.dynamic_index_in_dim(pieces, me, 0, keepdims=False)
    for p in range(1, ways):
        piece = lax.dynamic_index_in_dim(pieces, me ^ p, 0, keepdims=False)
        total = total + flip(piece.astype(BF16), axis, p * unit).astype(F32)
    return total


def gather_round(piece, axis, unit, ways, split):
    if not split:
        return piece
    return jnp.concatenate([piece] + [flip(piece, axis, p * unit) for p in range(1, ways)], axis=0)


def exchange(keep, send, rounds, before_gather=None, before_last=None):
    kept = keep.astype(F32) + flip(send, "col", 1).astype(F32)
    for one in rounds:
        kept = reduce_round(kept, *one)
    piece = kept.astype(BF16)
    if before_gather is not None:
        piece = tie(piece, before_gather)
    for k, one in enumerate(reversed(rounds)):
        if before_last is not None and k == len(rounds) - 1:
            piece = tie(piece, before_last)
        piece = gather_round(piece, *one)
    return piece, flip(piece, "col", 1)


def tie(first, *others):
    return lax.optimization_barrier((first, *others))[0]


def tree_sum(parts):
    while len(parts) > 1:
        parts = [parts[k] + parts[k + 1] for k in range(0, len(parts), 2)]
    return parts[0]


def sum_over(values, axis, unit, ways):
    return tree_sum([values] + [flip(values, axis, p * unit) for p in range(1, ways)])


def place_kernel(targets, rounds, last, ids_ref, own_ref, other_ref, *outs):
    col = ids_ref[0]
    row = ids_ref[1]
    half, width = own_ref.shape
    steps = []
    size = half
    for axis, unit, ways, split in rounds:
        if split:
            size //= ways
            steps.append((axis, unit, ways, size))
    count = half // size
    places = outs[: len(targets) - 1] + outs[-1:] if last else outs
    for other, source in enumerate((own_ref, other_ref)):

        @pl.loop(0, count)
        def _(k):
            start = ((col & 1) ^ other) * half
            left = k
            weight = count
            for axis, unit, ways, step in steps:
                weight //= ways
                digit = left // weight
                left = left - digit * weight
                index = (col if axis == "col" else row) // unit % ways
                start = start + (index ^ digit) * step
            value = source[pl.ds(pl.multiple_of(k * size, 16), size), :].astype(F32)
            for first, past, by_row, ref in [target + (ref,) for target, ref in zip(targets, places)]:

                @pl.when((start >= first) & (start < past))
                def _():
                    inside = start - first
                    if by_row:
                        ref[pl.ds(pl.multiple_of(inside, 8), size), :] = value
                    else:
                        lane = pl.multiple_of((inside // width) * width, 128)
                        ref[pl.ds(pl.multiple_of(inside % width, 8), size), pl.ds(lane, width)] = value

    if last:
        first_gain, second_gain, loss, moved, small = outs[-5:]
        first_gain[...] = small[0, :]
        second_gain[...] = small[1, :]
        lane = lax.broadcasted_iota(jnp.int32, (1, 128), 1)
        stat = small[2:3, :128]
        loss[0] = jnp.sum(jnp.where(lane == 0, stat, 0.0))
        moved[0] = jnp.sum(jnp.where(lane == 1, stat, 0.0))


def place(ids, gathered, targets, rounds, shapes, last=False):
    width = gathered[0].shape[1]
    specs = [VMEM] * len(shapes)
    made = [jax.ShapeDtypeStruct(shape, F32) for shape in shapes]
    scratch = []
    if last:
        specs = specs + [VMEM, VMEM, SMEM, SMEM]
        made = made + [jax.ShapeDtypeStruct((size,), F32) for size in (width, width, 1, 1)]
        scratch = [pltpu.VMEM((128, width), F32)]
    return pl.pallas_call(
        functools.partial(place_kernel, targets, rounds, last),
        in_specs=[SMEM, VMEM, VMEM],
        out_specs=specs,
        out_shape=made,
        scratch_shapes=scratch,
        compiler_params=params(SIM_LIMIT),
        name="place_gradients",
    )(ids, *gathered)


def body(
    image_tokens, text_tokens, lengths, pair_count, img_qkv, img_out, img_up, img_down, img_proj,
    gain_one, txt_qkv, txt_out, gain_two, txt_up, txt_down, txt_proj, log_scale,
):
    pairs, _, width = image_tokens.shape
    ff = txt_up.shape[1]
    row_index = lax.axis_index("row")
    col_index = lax.axis_index("col")
    row_count = lax.axis_size("row")
    col_count = lax.axis_size("col")
    high = col_count // 4
    cut = pairs - NB
    across = row_count - 1

    by_token = jnp.transpose(image_tokens, (1, 0, 2))
    got_images = flip(by_token[:, cut:], "row", across)
    got_texts = flip(text_tokens[cut:], "row", across)
    lens = lengths.astype(F32).reshape(pairs // QB, QB)
    got_lens = flip(lens[cut // QB :], "row", across)
    plan, rlive, tlive, scal = prepare(pair_count, log_scale, cut)
    gain_one = gain_one.reshape(1, width)
    gain_two = gain_two.reshape(1, width)

    weights = (img_qkv, img_out, img_up, img_down, img_proj)
    first_unit = image_tower(plan, by_token, None, 0, cut, cut, IMAGE_NB, 1.0, *weights)
    last_unit = lax.cond(
        plan[IMAGE_BLOCKS + cut // GROUP] > 0,
        lambda: image_tower(plan, by_token, got_images, cut, NB, cut, GROUP, 0.01, *weights),
        lambda: jnp.zeros((NB, width), BF16),
    )
    unit = jnp.concatenate([first_unit, last_unit], axis=0)
    parts = [unit] + [flip(unit, "col", 4 * p) for p in range(1, high)]
    qkv, att, y1 = text_first(plan, text_tokens, got_texts, lens, got_lens, cut, gain_one, txt_qkv, txt_out)
    parts = lax.optimization_barrier((*parts, y1))
    y1 = parts[-1]
    near = jnp.concatenate(parts[:-1], axis=0)
    beside = flip(near, "col", 2)
    core_near = flip(near, "col", 1)
    slopes, hsum, pooled, emb, text_low = text_second(
        plan, y1, lens, got_lens, cut, gain_two, txt_up, txt_down, txt_proj
    )
    images = [near, core_near, beside, flip(tie(beside, text_low), "col", 1)]
    texts = [text_low] + [flip(text_low, "row", p) for p in range(1, row_count)]
    rowsum, colsum = sim_sums(plan, scal, texts, tlive, rlive, images)
    total_col = colsum
    for p in range(1, row_count):
        other = flip(colsum, "row", p)
        total_col = total_col + jnp.concatenate([other[k ^ p : (k ^ p) + 1] for k in range(row_count)], axis=0)
    for bit in range(2, (high * 4).bit_length() - 1):
        rowsum = rowsum + flip(rowsum, "col", 1 << bit)
    rowsum = sum_over(rowsum, "col", 1, 4)
    *duns, stat = sim_grads(plan, scal, texts, tlive, rlive, rowsum, total_col, images)
    others = [flip(duns[p], "row", p) for p in range(1, row_count)]
    split_row = width * 2 % (row_count * 2 * 2 * 16) == 0
    along_row = ("row", 1, row_count, split_row)
    along_y = ("col", 2, 2, True)
    along_z = ("col", 4, 2, high % 2 == 0)
    along_far = ("col", 8, high // 2, False)
    order_a = [along_row, along_y, along_z, along_far]
    order_b = [along_y, along_z, along_row, along_far]
    order_c = [along_z, along_row, along_y, along_far]
    qkv = pltpu.with_memory_space_constraint(qkv, pltpu.HBM)
    text_grad, keep_a, send_a, keep_b, send_b, keep_c, send_c = text_backward(
        plan, text_tokens, qkv, att, y1, slopes, got_texts, lens, got_lens, cut, duns[0], emb, pooled, hsum,
        gain_one, txt_qkv, txt_out, gain_two, txt_up, txt_down, txt_proj, others, stat,
    )
    back = flip(text_grad[cut:], "row", across)
    low_half = row_index < row_count // 2
    counts = pair_count[:, col_index]
    balanced = jnp.where(low_half, counts[row_index], counts[row_index ^ across]) <= cut
    last = jnp.where(balanced, jnp.where(low_half, jnp.zeros_like(back), back), text_grad[cut:])
    text_grad = lax.dynamic_update_slice_in_dim(text_grad, last, cut, 0)
    orders = [order_a, order_b, order_c]
    targets = [
        [(0, ff, True), (ff, ff + width, True), (ff + width, ff + width + 128, True)],
        [(0, ff, False)],
        [(0, width, True), (width, 4 * width, False)],
    ]
    shapes = [[(ff, width), (width, width)], [(width, ff)], [(width, width), (width, 3 * width)]]
    placed = []
    waits = [(back, None), (None, None), (None, None)]
    for keep, send, rounds, places, sizes in zip((keep_a, keep_b, keep_c), (send_a, send_b, send_c), orders, targets, shapes):
        gathered = exchange(keep, send, rounds, *waits.pop(0))
        placed += place(plan, gathered, places, rounds, sizes, not placed)
    sum_down, sum_proj, sum_one, sum_two, loss, sum_scale, sum_up, sum_out, sum_qkv = placed
    return (
        loss, text_grad, sum_one, sum_qkv, sum_out, sum_two, sum_up, sum_down, sum_proj, sum_scale,
    )


def solution(mesh):
    return jax.shard_map(
        body,
        mesh=mesh,
        in_specs=(
            P(("row", "col"), None, None),
            P(("row", "col"), None, None),
            P(("row", "col")),
            P(),
            P(),
            P(),
            P(),
            P(),
            P(),
            P(),
            P(),
            P(),
            P(),
            P(),
            P(),
            P(),
            P(),
        ),
        out_specs=(P(), P(("row", "col"), None, None), P(), P(), P(), P(), P(), P(), P(), P()),
        check_vma=False,
    )
```

```python
import functools
import jax
import jax.numpy as jnp
from jax import lax
from jax.experimental import pallas as pl
from jax.experimental.pallas import tpu as pltpu
from jax.sharding import PartitionSpec as P

HEADS = 6
HEAD = 64
epsilon = 1e-6
F32 = jnp.float32
BF16 = jnp.bfloat16
GELU_A = 0.7978845608028654
GELU_B = 0.7978845608028654 * 0.044715
SAFE = 60.0
GROUP = 8
PITCH = 9
IMAGE_NB = 16
USE = 2
ACTIVE = 3
ORDER = 4
ORDER_ALL = 8
IMAGE_BLOCKS = 12
PLAN = 28
NB = 32
QB = 16
T1_LIMIT = 20
T2_LIMIT = 20
BACK_LIMIT = 30
SIM_LIMIT = 12


def mm(a, b):
    return lax.dot_general(a, b, (((1,), (0,)), ((), ())), preferred_element_type=F32)


def mm_t(a, b):
    return lax.dot_general(a, b, (((1,), (1,)), ((), ())), preferred_element_type=F32)


def mm_split(a, b):
    hi = a.astype(BF16)
    lo = (a - hi.astype(F32)).astype(BF16)
    return mm(hi, b) + mm(lo, b)


def column_chunks(width):
    edge = width // 2 // 256 * 256
    return ((0, edge), (edge, width))


def over(a, b):
    r = pl.reciprocal(b, approx=True)
    return a * (r * (2.0 - b * r))


def normed(v):
    c = v - jnp.mean(v, axis=-1, keepdims=True)
    return c * lax.rsqrt(jnp.mean(c * c, axis=-1, keepdims=True) + epsilon)


def unit_scale(e):
    return lax.rsqrt(jnp.sum(e * e, axis=-1, keepdims=True) + epsilon)


def lane_halves():
    lane = lax.broadcasted_iota(jnp.int32, (1, 128), 1)
    low = (lane < HEAD).astype(F32)
    return low, 1.0 - low


def image_kernel(first, cut, plan_ref, x_ref, recv_ref, wqkv_ref, wout_ref, wup_ref, wdown_ref, wproj_ref, unit_ref, qkv, att, hsum, xsum):
    step = pl.program_id(0)
    length, nb, width = x_ref.shape
    rows = length * GROUP

    @pl.when(step == 0)
    def _():
        qkv[...] = jnp.zeros_like(qkv)
        hsum[...] = jnp.zeros_like(hsum)
        xsum[...] = jnp.zeros_like(xsum)

    block = first // nb + step

    @pl.when(plan_ref[IMAGE_BLOCKS + block * (nb // GROUP)] > 0)
    def _():
        image_block(step, block, cut, plan_ref, x_ref, recv_ref, wqkv_ref, wout_ref, wup_ref, qkv, att, hsum, xsum)

    @pl.when(step == pl.num_programs(0) - 1)
    def _():
        pooled = xsum[...] * (1.0 / length) + mm_split(hsum[...] * (0.5 / length), wdown_ref[...])
        e = mm(pooled.astype(BF16), wproj_ref[...])
        unit_ref[...] = (e * unit_scale(e)).astype(BF16)


def image_block(step, block, cut, plan_ref, x_ref, recv_ref, wqkv_ref, wout_ref, wup_ref, qkv, att, hsum, xsum):
    length, nb, width = x_ref.shape
    rows = length * GROUP
    slots = qkv.shape[2] // PITCH
    tiles = width // 128
    ff = wup_ref.shape[1]
    groups = nb // GROUP
    moved = (plan_ref[USE] > 0) & (block >= cut // nb)

    def tokens(g):
        x = x_ref[...].astype(F32)
        if recv_ref is not None:
            x = jnp.where(moved, recv_ref[...].astype(F32), x)
        return x[:, g * GROUP : (g + 1) * GROUP, :].reshape(rows, width)

    low, high = lane_halves()
    key_row = lax.broadcasted_iota(jnp.int32, (2 * slots, 128), 0)
    key_lane = lax.broadcasted_iota(jnp.int32, (2 * slots, 128), 1)
    own_head = (key_row < slots) == (key_lane < HEAD)
    real = jnp.where(key_row < slots, key_row, key_row - slots) < length
    ones = jnp.where(own_head & real, 1.0, 0.0).astype(BF16)

    def pairs_of(g):
        return pl.ds(pl.multiple_of(step * nb + g * GROUP, GROUP), GROUP)

    def scores(g, p, h):
        at = pl.ds(p, slots, stride=PITCH)
        q = qkv[g, h, at, :].astype(BF16) * BF16(HEAD**-0.5)
        k = qkv[g, tiles + h, at, :]
        return mm_t(q, jnp.concatenate([k * low, k * high], axis=0).astype(BF16))

    def weighted(g, p, h, e):
        at = pl.ds(p, slots, stride=PITCH)
        v = qkv[g, 2 * tiles + h, at, :]
        vbd = jnp.concatenate([v * low, v * high], axis=0).astype(BF16)
        o = mm(e.astype(BF16), jnp.concatenate([vbd, ones], axis=1))
        att[g, h, at, :] = over(o[:, :128], o[:, 128:])

    def projected(g):
        n1 = normed(tokens(g)).astype(BF16)
        for first, last in column_chunks(3 * width):
            made = mm(n1, wqkv_ref[:, first:last])
            for c in range(first // 128, last // 128):
                here = c * 128 - first
                for t in range(length):
                    qkv[g, c, t * PITCH : t * PITCH + GROUP, :] = made[t * GROUP : (t + 1) * GROUP, here : here + 128]

    def after_attention(g):
        heads = jnp.concatenate(
            [
                jnp.concatenate([att[g, h, t * PITCH : t * PITCH + GROUP, :] for t in range(length)], axis=0)
                for h in range(tiles)
            ],
            axis=1,
        )
        x1 = tokens(g) + mm(heads.astype(BF16), wout_ref[...])
        xsum[pairs_of(g), :] = jnp.sum(x1.reshape(length, GROUP, width), axis=0)
        return normed(x1).astype(BF16)

    def gelu_sum(g, u, c):
        made = u * (1.0 + jnp.tanh(u * (GELU_A + GELU_B * (u * u))))
        hsum[pairs_of(g), pl.ds(c, 256)] = jnp.sum(made.reshape(length, GROUP, 256), axis=0)

    def feed_steps(g):
        n2 = after_attention(g)
        before = None
        for c in range(0, ff, 256):
            u = mm(n2, wup_ref[:, c : c + 256])
            if before is not None:
                gelu_sum(g, *before)
            before = (u, c)
            yield
        gelu_sum(g, *before)
        yield

    largest = jnp.zeros((slots, 2 * slots), F32)
    units = [(p, h) for p in range(GROUP) for h in range(tiles)]
    ahead = 6
    feed = iter(())
    projected(0)
    for g in range(groups):
        s_list, e_list = {}, {}
        for k in range(len(units) + 2 * ahead):
            if k < len(units):
                s_list[k] = scores(g, *units[k])
            if 0 <= k - ahead < len(units):
                s = s_list.pop(k - ahead)
                largest = jnp.maximum(largest, jnp.abs(s))
                e_list[k - ahead] = jnp.exp(s)
            if 0 <= k - 2 * ahead < len(units):
                weighted(g, *units[k - 2 * ahead], e_list.pop(k - 2 * ahead))
            if k % 4 == 2:
                next(feed, None)
            if k == len(units) // 2 and g + 1 < groups:
                projected(g + 1)
        for _ in feed:
            pass
        feed = feed_steps(g)
    for _ in feed:
        pass

    @pl.when(jnp.logical_not(jnp.max(largest) <= SAFE))
    def _():
        key = lax.broadcasted_iota(jnp.int32, (1, 2 * slots), 1)
        in_low = key < slots
        for_low = key < length
        for_high = (key >= slots) & (key < slots + length)
        @pl.loop(0, groups)
        def _(g):
            @pl.loop(0, GROUP)
            def _(p):
                @pl.loop(0, tiles)
                def _(h):
                    s = scores(g, p, h)
                    top_low = jnp.max(jnp.where(for_low, s, -1e30), axis=1, keepdims=True)
                    top_high = jnp.max(jnp.where(for_high, s, -1e30), axis=1, keepdims=True)
                    s = jnp.where(for_low | for_high, s, -1e30) - jnp.where(in_low, top_low, top_high)
                    weighted(g, p, h, jnp.exp(s))

        for g in range(groups):
            n2 = after_attention(g)

            @pl.loop(0, ff // 256)
            def _(c):
                at = pl.multiple_of(c * 256, 256)
                gelu_sum(g, mm(n2, wup_ref[:, pl.ds(at, 256)]), at)


def fixed(shape):
    zeros = (0,) * len(shape)
    return pl.BlockSpec(shape, lambda *_: zeros, pipeline_mode=pl.Buffered(1))


def image_tower(plan, tokens, received, first, count, cut, nb, cost, wqkv, wout, wup, wdown, wproj):
    length, _, width = tokens.shape
    slots = -(-length // 8) * 8
    ff = wup.shape[1]
    weights = (wqkv, wout, wup, wdown, wproj)
    at = first // nb
    specs = [pl.BlockSpec((length, nb, width), lambda i, plan: (0, at + i, 0))]
    if received is None:
        kernel = lambda plan_ref, x_ref, *refs: image_kernel(first, cut, plan_ref, x_ref, None, *refs)
        arrays = (tokens,)
    else:
        kernel = functools.partial(image_kernel, first, cut)
        last = received.shape[1] // nb - 1
        specs.append(
            pl.BlockSpec((length, nb, width), lambda i, plan: (0, jnp.clip(at + i - cut // nb, 0, last), 0))
        )
        arrays = (tokens, received)
    return pl.pallas_call(
        kernel,
        grid_spec=pltpu.PrefetchScalarGridSpec(
            num_scalar_prefetch=1,
            grid=(count // nb,),
            in_specs=specs + [fixed(w.shape) for w in weights],
            out_specs=pl.BlockSpec((count, width), lambda i, plan: (0, 0)),
            scratch_shapes=[
                pltpu.VMEM((nb // GROUP, 3 * width // 128, slots * PITCH, 128), F32),
                pltpu.VMEM((nb // GROUP, width // 128, slots * PITCH, 128), F32),
                pltpu.VMEM((count, ff), F32),
                pltpu.VMEM((count, width), F32),
            ],
        ),
        out_shape=jax.ShapeDtypeStruct((count, width), BF16),
        compiler_params=pltpu.CompilerParams(vmem_limit_bytes=60 * 2**20),
        cost_estimate=pl.CostEstimate(
            flops=int(cost * 2 * count * length * width * (4 * width + ff)),
            bytes_accessed=int(cost * (count * length * width * 2 + 4 * 2**20)),
            transcendentals=int(cost * count * length * ff),
        ),
        name="image_block",
    )(plan, *arrays, *weights)


def mm_tn(a, b):
    return lax.dot_general(a, b, (((0,), (0,)), ((), ())), preferred_element_type=F32)


def stats(v):
    c = v - jnp.mean(v, axis=-1, keepdims=True)
    inv = lax.rsqrt(jnp.mean(c * c, axis=-1, keepdims=True) + epsilon)
    return c * inv, inv


def norm_back(g, n, inv):
    return inv * (
        g - jnp.mean(g, axis=-1, keepdims=True) - n * jnp.mean(g * n, axis=-1, keepdims=True)
    )


def staggered(stages, units, ahead):
    kept = [dict() for _ in stages]
    for k in range(len(units) + (len(stages) - 1) * ahead):
        for at, stage in enumerate(stages):
            u = k - at * ahead
            if 0 <= u < len(units):
                made = stage(units[u], *([kept[at - 1].pop(u)] if at else []))
                kept[at][u] = made


def same_pair(length):
    row = lax.broadcasted_iota(jnp.int32, (128, 128), 0) // length
    lane = lax.broadcasted_iota(jnp.int32, (128, 128), 1) // length
    return row == lane


SMEM = pl.BlockSpec(memory_space=pltpu.SMEM)
VMEM = pl.BlockSpec(memory_space=pltpu.VMEM)


def params(limit=60):
    return pltpu.CompilerParams(vmem_limit_bytes=limit * 2**20)


def as_column(row):
    size = row.shape[1]
    diagonal = lax.broadcasted_iota(jnp.int32, (size, size), 0) == lax.broadcasted_iota(jnp.int32, (size, size), 1)
    return jnp.sum(jnp.where(diagonal, row, 0.0), axis=1, keepdims=True)


def as_row(col):
    size = col.shape[0]
    diagonal = lax.broadcasted_iota(jnp.int32, (size, size), 0) == lax.broadcasted_iota(jnp.int32, (size, size), 1)
    return jnp.sum(jnp.where(diagonal, col, 0.0), axis=0, keepdims=True)


def prepare_kernel(cut, count_ref, scale_ref, plan_ref, rlive_ref, tlive_ref, scal_ref):
    rows, cols = count_ref.shape
    across = rows - 1
    col = lax.axis_index("col")
    row = lax.axis_index("row")

    def limits(r, c):
        n = count_ref[r, c]
        other = count_ref[r ^ across, c]
        low = r < rows // 2
        balanced = jnp.where(low, n, other) <= cut
        return n, jnp.where(balanced, jnp.where(low, other, 0), n), low & balanced

    def mask(r, c):
        first, last, _ = limits(r, c)
        slot = lax.broadcasted_iota(jnp.int32, (1, 128), 1)
        return jnp.where(slot < jnp.where(slot < cut, first, last), 1.0, 0.0)

    for c in range(cols):
        rlive_ref[c : c + 1, :] = mask(row, c)
    for p in range(rows):
        tlive_ref[p : p + 1, :] = mask(row ^ p, col)
    first, last, use = limits(row, col)
    limit = lambda start: first if start < cut else last
    plan_ref[0] = col
    plan_ref[1] = row
    plan_ref[USE] = use.astype(jnp.int32)
    blocks = 128 // NB
    active = [(b * NB < limit(b * NB)).astype(jnp.int32) for b in range(blocks)]
    count = sum(active)
    before = jnp.int32(0)
    for b in range(blocks):
        plan_ref[ORDER_ALL + jnp.where(active[b] > 0, before, count + b - before)] = b
        before = before + active[b]
    for i in range(blocks):
        plan_ref[ORDER + i] = plan_ref[ORDER_ALL + jnp.minimum(i, count - 1)]
    plan_ref[ACTIVE] = count
    for b in range(128 // GROUP):
        plan_ref[IMAGE_BLOCKS + b] = (b * GROUP < limit(b * GROUP)).astype(jnp.int32)
    total = jnp.int32(0)
    for r in range(rows):
        for c in range(cols):
            total = total + count_ref[r, c]
    index = lax.broadcasted_iota(jnp.int32, (8, 128), 0)
    scal_ref[...] = jnp.where(index == 0, jnp.exp(jnp.full((8, 128), scale_ref[0], F32)), 0.5 / jnp.full((8, 128), total, jnp.int32).astype(F32))


def prepare(pair_count, log_scale, cut):
    rows, cols = pair_count.shape
    return pl.pallas_call(
        functools.partial(prepare_kernel, cut),
        in_specs=[SMEM] * 2,
        out_specs=[SMEM, VMEM, VMEM, VMEM],
        out_shape=[
            jax.ShapeDtypeStruct((PLAN,), jnp.int32),
            jax.ShapeDtypeStruct((cols, 128), F32),
            jax.ShapeDtypeStruct((rows, 128), F32),
            jax.ShapeDtypeStruct((8, 128), F32),
        ],
        name="prepare",
    )(pair_count, log_scale)


def lengths_of(plan_ref, cut, part, lens_ref, got_ref):
    moved = (plan_ref[USE] > 0) & (part * QB >= cut)
    got = got_ref[pl.ds(jnp.maximum(part - cut // QB, 0), 1), :]
    return as_column(jnp.where(moved, got, lens_ref[pl.ds(part, 1), :]))


def block_lengths(plan_ref, cut, block, lens_ref, got_ref):
    parts = [lengths_of(plan_ref, cut, block * (NB // QB) + k, lens_ref, got_ref) for k in range(NB // QB)]
    return jnp.concatenate(parts, axis=0)


def all_lengths(plan_ref, cut, lens_ref, got_ref):
    parts = [lengths_of(plan_ref, cut, b, lens_ref, got_ref) for b in range(lens_ref.shape[0])]
    return jnp.concatenate(parts, axis=0)


def live_pick(lens, rows):
    pairs = lens.shape[0]
    length = rows // pairs
    token = lax.broadcasted_iota(jnp.int32, (pairs, rows), 1)
    own = token // length == lax.broadcasted_iota(jnp.int32, (pairs, rows), 0)
    return jnp.where(own & ((token % length).astype(F32) < lens), 1.0, 0.0)


def text_tokens_of(plan_ref, cut, block, x_ref, recv_ref):
    nb, length, width = x_ref.shape
    moved = (plan_ref[USE] > 0) & (block * nb >= cut)
    x = jnp.where(moved, recv_ref[...].astype(F32), x_ref[...].astype(F32))
    return x.reshape(nb * length, width)


def ordered(width, rows):
    return pl.BlockSpec((rows, width), lambda i, plan: (plan[ORDER + i], 0))


def ordered_pairs(shape, order=ORDER):
    return pl.BlockSpec((NB,) + shape[1:], lambda i, plan: (plan[order + i], 0, 0))


def held(shape):
    zeros = (0,) * len(shape)
    return pl.BlockSpec(shape, lambda i, plan: zeros)


def text_first_kernel(cut, plan_ref, x_ref, recv_ref, lens_ref, got_ref, gain_ref, wqkv_ref, wout_ref, qkv_ref, att_ref, y1_ref):
    step = pl.program_id(0)
    block = plan_ref[ORDER + step]

    @pl.when(step < plan_ref[ACTIVE])
    def _():
        x = text_tokens_of(plan_ref, cut, block, x_ref, recv_ref)
        lens = block_lengths(plan_ref, cut, block, lens_ref, got_ref)
        text_attention(x, lens, x_ref.shape[1], gain_ref, wqkv_ref, wout_ref, qkv_ref, att_ref, y1_ref)


def text_attention(x, lens, length, gain_ref, wqkv_ref, wout_ref, qkv_ref, att_ref, y1_ref):
    rows, width = x.shape
    n1 = (normed(x) * gain_ref[...]).astype(BF16)
    for first, last in column_chunks(3 * width):
        qkv_ref[:, first:last] = mm(n1, wqkv_ref[:, first:last]).astype(BF16)
    lane = lax.broadcasted_iota(jnp.int32, (128, 128), 1)
    low = (lane[:1] < HEAD).astype(BF16)
    high = 1 - low
    half = lax.broadcasted_iota(jnp.int32, (256, 128), 0) < 128
    ones = jnp.where(half == (lax.broadcasted_iota(jnp.int32, (256, 128), 1) < HEAD), 1.0, 0.0).astype(BF16)
    same = same_pair(length)
    live = jnp.sum(live_pick(lens, rows), axis=0, keepdims=True)
    bias = {g: jnp.where(same & (live[:, g : g + 128] > 0), 0.0, -1e30) for g in range(0, rows, 128)}

    def scores(unit):
        g, h = unit
        q = qkv_ref[g : g + 128, h : h + 128] * BF16(HEAD**-0.5)
        k = qkv_ref[g : g + 128, width + h : width + h + 128]
        return mm_t(q, jnp.concatenate([k * low, k * high], axis=0))

    def expo(unit, s):
        one = bias[unit[0]]
        parts = [s[:, :128] + one, s[:, 128:] + one]
        return jnp.concatenate([jnp.exp(p - jnp.max(p, axis=1, keepdims=True)) for p in parts], axis=1).astype(BF16)

    def weighted(unit, e):
        g, h = unit
        v = qkv_ref[g : g + 128, 2 * width + h : 2 * width + h + 128]
        vbd = jnp.concatenate([v * low, v * high], axis=0)
        o = mm(e, jnp.concatenate([vbd, ones], axis=1))
        att_ref[g : g + 128, h : h + 128] = over(o[:, :128], o[:, 128:]).astype(BF16)

    staggered([scores, expo, weighted], [(g, h) for g in range(0, rows, 128) for h in range(0, width, 128)], 2)
    y1_ref[...] = x + mm(att_ref[...], wout_ref[...])


def text_first(plan, x, received, lens, got, cut, gain_one, wqkv, wout):
    pairs, length, width = x.shape
    rows = NB * length
    tokens = pairs * length
    rest = (received, lens, got, gain_one, wqkv, wout)
    wide = [(3 * width, BF16), (width, BF16), (width, F32)]
    return pl.pallas_call(
        functools.partial(text_first_kernel, cut),
        grid_spec=pltpu.PrefetchScalarGridSpec(
            num_scalar_prefetch=1,
            grid=(pairs // NB,),
            in_specs=[ordered_pairs(x.shape)] + [fixed(w.shape) for w in rest],
            out_specs=[ordered(w, rows) for w, _ in wide],
        ),
        out_shape=[(pltpu.HBM if k == 0 else jax.ShapeDtypeStruct)((tokens, w), kind) for k, (w, kind) in enumerate(wide)],
        compiler_params=params(T1_LIMIT),
        cost_estimate=pl.CostEstimate(flops=2 * tokens * width * 5 * width, bytes_accessed=12 * 2**20, transcendentals=0),
        name="text_attention",
    )(plan, x, *rest)


def text_second_kernel(
    cut, plan_ref, y1_ref, lens_ref, got_ref, gain_two_ref, wup_ref, wdown_ref, wproj_ref,
    slope_ref, hsum_ref, pooled_ref, emb_ref, low_ref, ysum,
):
    step = pl.program_id(0)
    block = plan_ref[ORDER + step]

    @pl.when(step == 0)
    def _():
        hsum_ref[...] = jnp.zeros_like(hsum_ref)
        ysum[...] = jnp.zeros_like(ysum)

    @pl.when(step < plan_ref[ACTIVE])
    def _():
        rows = y1_ref.shape[0]
        y1 = y1_ref[...]
        pick = live_pick(block_lengths(plan_ref, cut, block, lens_ref, got_ref), rows).astype(BF16)
        pair = pl.ds(pl.multiple_of(block * NB, NB), NB)
        y1_hi = y1.astype(BF16)
        ysum[pair, :] = mm(pick, y1_hi) + mm(pick, (y1 - y1_hi.astype(F32)).astype(BF16))
        n2 = (normed(y1) * gain_two_ref[...]).astype(BF16)

        live = mm_tn(pick, jnp.ones((NB, 128), BF16))
        live = jnp.concatenate([live, live], axis=1)

        def gelu_parts(u, c):
            square = u * u
            t = 1.0 + jnp.tanh(u * (GELU_A + GELU_B * square))
            half = 0.5 * u
            hsum_ref[pair, c : c + 256] = mm(pick, (half * t).astype(BF16))
            d = t * (0.5 + (2.0 - t) * (half * (GELU_A + (3.0 * GELU_B) * square)))
            slope_ref[:, c : c + 256] = (d * live).astype(BF16)

        in_chunks(n2, wup_ref, gelu_parts)

    @pl.when(step == pl.num_programs(0) - 1)
    def _():
        inv_len = 1.0 / all_lengths(plan_ref, cut, lens_ref, got_ref)
        pooled = (ysum[...] * inv_len + mm_split(hsum_ref[...] * inv_len, wdown_ref[...])).astype(BF16)
        pooled_ref[...] = pooled
        e = mm(pooled, wproj_ref[...])
        emb_ref[...] = e
        low_ref[...] = (e * unit_scale(e)).astype(BF16)


def in_chunks(left, right_ref, use):
    before = None
    for c in range(0, right_ref.shape[1], 256):
        u = mm(left, right_ref[:, c : c + 256])
        if before is not None:
            use(*before)
        before = (u, c)
    use(*before)


def text_second(plan, y1, lens, got, cut, gain_two, wup, wdown, wproj):
    tokens, width = y1.shape
    pairs = lens.size
    rows = NB * tokens // pairs
    ff = wup.shape[1]
    rest = (lens, got, gain_two, wup, wdown, wproj)
    flat = [((pairs, ff), F32), ((pairs, width), BF16), ((pairs, width), F32), ((pairs, width), BF16)]
    return pl.pallas_call(
        functools.partial(text_second_kernel, cut),
        grid_spec=pltpu.PrefetchScalarGridSpec(
            num_scalar_prefetch=1,
            grid=(pairs // NB,),
            in_specs=[ordered(width, rows)] + [fixed(w.shape) for w in rest],
            out_specs=[ordered(ff, rows)] + [held(shape) for shape, _ in flat],
            scratch_shapes=[pltpu.VMEM((pairs, width), F32)],
        ),
        out_shape=[jax.ShapeDtypeStruct((tokens, ff), BF16)] + [jax.ShapeDtypeStruct(shape, kind) for shape, kind in flat],
        compiler_params=params(T2_LIMIT),
        cost_estimate=pl.CostEstimate(flops=2 * tokens * width * ff, bytes_accessed=12 * 2**20, transcendentals=tokens * ff),
        name="text_pool",
    )(plan, y1, *rest)


def image_groups(image_refs):
    for j, ref in enumerate(image_refs):
        yield j, ref.shape[0] // 128, len(image_refs), ref[...]


def sums_kernel(rows, ids_ref, scal_ref, tlive_ref, rlive_ref, *refs):
    text_refs = refs[:rows]
    image_refs = refs[rows:-2]
    rowsum_ref, colsum_ref = refs[-2:]
    me = ids_ref[0]
    scale = scal_ref[:1, :1]
    text = jnp.concatenate([ref[...] for ref in text_refs], axis=0)
    tlive = jnp.concatenate([as_column(tlive_ref[p : p + 1, :]) for p in range(rows)], axis=0)
    col = jnp.zeros((rows * 128, 1), F32)
    for j, high, low, images in image_groups(image_refs):
        e = jnp.exp(scale * mm_t(text, images)) * tlive
        total = jnp.sum(e, axis=0, keepdims=True)
        kept = jnp.zeros((rows * 128, 128), F32)
        for i in range(high):
            at = pl.ds(me ^ (low * i + j), 1)
            rowsum_ref[at, :] = total[:, i * 128 : i * 128 + 128]
            kept = kept + e[:, i * 128 : i * 128 + 128] * rlive_ref[at, :]
        col = col + jnp.sum(kept, axis=1, keepdims=True)
    for p in range(rows):
        colsum_ref[p : p + 1, :] = as_row(col[p * 128 : p * 128 + 128])


def sim_sums(ids, scal, texts, tlive, rlive, images):
    cols = rlive.shape[0]
    rows = len(texts)
    return pl.pallas_call(
        functools.partial(sums_kernel, rows),
        in_specs=[SMEM] + [VMEM] * (3 + rows + len(images)),
        out_specs=[VMEM, VMEM],
        out_shape=[jax.ShapeDtypeStruct((cols, 128), F32), jax.ShapeDtypeStruct((rows, 128), F32)],
        compiler_params=params(SIM_LIMIT),
        cost_estimate=pl.CostEstimate(
            flops=2 * rows * 128 * cols * 128 * 384, bytes_accessed=cols * 128 * 768, transcendentals=rows * cols * 128 * 128
        ),
        name="similarity_sums",
    )(ids, scal, tlive, rlive, *texts, *images)


def grad_kernel(rows, ids_ref, scal_ref, tlive_ref, rlive_ref, rowsum_ref, colsum_ref, *refs):
    text_refs = refs[:rows]
    image_refs = refs[rows : -rows - 1]
    dun_refs = refs[-rows - 1 : -1]
    stat_ref = refs[-1]
    me = ids_ref[0]
    scale = scal_ref[:1, :1]
    inv = scal_ref[1:2, :1]
    text = jnp.concatenate([ref[...] for ref in text_refs], axis=0)
    tlive = jnp.concatenate([as_column(tlive_ref[p : p + 1, :]) for p in range(rows)], axis=0)
    col = jnp.concatenate([as_column(colsum_ref[p : p + 1, :]) for p in range(rows)], axis=0)
    col = jnp.where(tlive > 0, col, 1.0)
    col_inv = inv / col
    total = jnp.zeros(text.shape, F32)
    moved = jnp.zeros((1, 128), F32)
    for j, high, low, images in image_groups(image_refs):
        s = scale * mm_t(text, images)
        e = jnp.exp(s) * tlive
        at = [pl.ds(me ^ (low * i + j), 1) for i in range(high)]
        rlive = jnp.concatenate([rlive_ref[one, :] for one in at], axis=1)
        row_inv = jnp.concatenate([inv / rowsum_ref[one, :] for one in at], axis=1)
        ds = (e * rlive) * (row_inv + col_inv)
        by_lane = jnp.sum(ds * s, axis=0, keepdims=True)
        for i in range(high):
            moved = moved + by_lane[:, i * 128 : i * 128 + 128]
        total = total + mm((scale * ds).astype(BF16), images)
        if j == 0:
            mine = images[:128].astype(F32)
    own_live = tlive[:128]
    cosine = jnp.sum(mine * text[:128].astype(F32), axis=1, keepdims=True)
    live_cosine = jnp.sum(cosine * own_live, axis=0, keepdims=True)
    at = pl.ds(me, 1)
    logs = jnp.sum(jnp.log(rowsum_ref[at, :]) * rlive_ref[at, :], axis=1, keepdims=True)
    logs = logs + jnp.sum(jnp.log(col[:128]) * own_live, axis=0, keepdims=True)
    loss = inv * (logs - 2.0 * scale * live_cosine)
    scale_part = jnp.sum(moved, axis=1, keepdims=True) - 2.0 * inv * scale * live_cosine
    dun_refs[0][...] = total[:128] + (scale * (-2.0 * inv * own_live)).astype(BF16).astype(F32) * mine
    for p in range(1, rows):
        dun_refs[p][...] = total[p * 128 : p * 128 + 128].astype(BF16)
    lane = lax.broadcasted_iota(jnp.int32, (8, 128), 1)
    stat_ref[...] = jnp.where(lane == 0, loss, jnp.where(lane == 1, scale_part, 0.0))


def sim_grads(ids, scal, texts, tlive, rlive, rowsum, colsum, images):
    cols = rlive.shape[0]
    rows = len(texts)
    return pl.pallas_call(
        functools.partial(grad_kernel, rows),
        in_specs=[SMEM] + [VMEM] * (5 + rows + len(images)),
        out_specs=[VMEM] * (rows + 1),
        out_shape=[jax.ShapeDtypeStruct(text.shape, BF16 if k else F32) for k, text in enumerate(texts)] + [jax.ShapeDtypeStruct((8, 128), F32)],
        compiler_params=params(SIM_LIMIT),
        cost_estimate=pl.CostEstimate(
            flops=4 * rows * 128 * cols * 128 * 384, bytes_accessed=cols * 128 * 768, transcendentals=rows * cols * 128 * 128
        ),
        name="similarity_grads",
    )(ids, scal, tlive, rlive, rowsum, colsum, *texts, *images)


def write_halves(core, blocks, keep_ref, send_ref):
    half = len(blocks) // 2
    size = blocks[0].shape[0]

    def put(first, second):
        for at, (kept, sent) in enumerate(zip(first, second)):
            keep_ref[at * size : (at + 1) * size, :] = kept.astype(BF16)
            send_ref[at * size : (at + 1) * size, :] = sent.astype(BF16)

    @pl.when(core == 0)
    def _():
        put(blocks[:half], blocks[half:])

    @pl.when(core != 0)
    def _():
        put(blocks[half:], blocks[:half])


def back_kernel(
    cut, others, plan_ref, x_ref, qkv_ref, att_ref, y1_ref, slope_ref, recv_ref, lens_ref, got_ref,
    dun_ref, emb_ref, pooled_ref, hsum_ref, gain_ref, wqkv_ref, wout_ref, gain_two_ref, wup_ref, wdown_ref, wproj_ref, *refs,
):
    other_refs = refs[:others]
    stat_ref = refs[others]
    grad_ref, keep_a, send_a, keep_b, send_b, keep_c, send_c = refs[others + 1 : others + 8]
    dyp, dhp, dproj, ddown, dmix, dheads, acc_up, acc_out, acc_qkv, bias_ref, du_ref = refs[others + 8 :]
    step = pl.program_id(0)
    block = plan_ref[ORDER + step]
    active = step < plan_ref[ACTIVE]
    width = dun_ref.shape[1]
    ff = hsum_ref.shape[1]

    @pl.when(step == 0)
    def _():
        acc_up[...] = jnp.zeros_like(acc_up)
        acc_out[...] = jnp.zeros_like(acc_out)
        acc_qkv[...] = jnp.zeros_like(acc_qkv)
        g = dun_ref[...]
        for other in other_refs:
            g = g + other[...].astype(F32)
        e = emb_ref[...]
        inv = unit_scale(e)
        t = e * inv
        demb = (inv * (g - t * jnp.sum(g * t, axis=-1, keepdims=True))).astype(BF16)
        dproj[...] = mm_tn(pooled_ref[...], demb)
        back = mm_t(demb, wproj_ref[...]) * (1.0 / all_lengths(plan_ref, cut, lens_ref, got_ref))
        dyp[...] = back
        db = back.astype(BF16)
        dhp[...] = mm_t(db, wdown_ref[...])
        h = hsum_ref[...]
        hi = h.astype(BF16)
        lo = (h - hi.astype(F32)).astype(BF16)
        ddown[...] = mm_tn(hi, db) + mm_tn(lo, db)

    @pl.when(active)
    def _():
        x = text_tokens_of(plan_ref, cut, block, x_ref, recv_ref)
        lens = block_lengths(plan_ref, cut, block, lens_ref, got_ref)
        grad = back_block(
            block, x, lens, x_ref.shape[1], qkv_ref, att_ref, y1_ref, slope_ref, gain_ref, wqkv_ref, wout_ref,
            gain_two_ref, wup_ref, dyp, dhp, dmix, dheads, acc_up, acc_out, acc_qkv, bias_ref, du_ref,
        )
        grad_ref[...] = grad.astype(BF16).reshape(grad_ref.shape)

    @pl.when(jnp.logical_not(active))
    def _():
        grad_ref[...] = jnp.zeros_like(grad_ref)

    @pl.when(step == pl.num_programs(0) - 1)
    def _():
        core = plan_ref[0] & 1
        index = lax.broadcasted_iota(jnp.int32, (128, width), 0)
        stat = jnp.concatenate([stat_ref[:1, :]] * (width // 128), axis=1)
        by_qkv = jnp.sum(acc_qkv[...] * wqkv_ref[...].astype(F32), axis=1, keepdims=True)
        by_up = jnp.sum(acc_up[...] * wup_ref[...].astype(F32), axis=1, keepdims=True)
        first = as_row(by_qkv) / gain_ref[...]
        second = as_row(by_up) / gain_two_ref[...]
        small = jnp.where(index == 0, first, jnp.where(index == 1, second, jnp.where(index == 2, stat, 0.0)))
        blocks = [ddown[at : at + 128, :] for at in range(0, ff, 128)]
        blocks += [dproj[at : at + 128, :] for at in range(0, width, 128)]
        write_halves(core, blocks + [small], keep_a, send_a)
        write_halves(core, [acc_up[:, c : c + width] for c in range(0, ff, width)], keep_b, send_b)
        blocks = [acc_out[...]] + [acc_qkv[:, c * width : (c + 1) * width] for c in range(3)]
        write_halves(core, blocks, keep_c, send_c)


def back_block(
    block, x, lens, length, qkv_ref, att_ref, y1_ref, slope_ref, gain_ref, wqkv_ref, wout_ref,
    gain_two_ref, wup_ref, dyp, dhp, dmix, dheads, acc_up, acc_out, acc_qkv, bias_ref, du_ref,
):
    rows, width = x.shape
    ff = wup_ref.shape[1]
    pair = pl.ds(pl.multiple_of(block * NB, NB), NB)

    def spread(values):
        return jnp.broadcast_to(values[:, None, :], (NB, length, values.shape[1])).reshape(rows, values.shape[1])

    n2, inv = stats(y1_ref[...])
    n2_low = (n2 * gain_two_ref[...]).astype(BF16)
    for c in range(0, ff, width):
        at = slice(c, c + width)
        du_ref[:, at] = (spread(dhp[pair, at]) * slope_ref[:, at].astype(F32)).astype(BF16)
    dn2 = mm_t(du_ref[...], wup_ref[...])
    acc_up[...] += mm_tn(n2_low, du_ref[...])
    live = mm_tn(live_pick(lens, rows).astype(BF16), jnp.ones((NB, 128), BF16))
    dy1 = spread(dyp[pair, :]) * jnp.concatenate([live] * (width // 128), axis=1)
    dy1 = dy1 + norm_back(dn2 * gain_two_ref[...], n2, inv)
    da = dy1.astype(BF16)
    acc_out[...] += mm_tn(att_ref[...], da)
    dheads[...] = mm_t(da, wout_ref[...]).astype(BF16)
    attention_grads(length, live, qkv_ref, dmix, dheads, bias_ref)
    n1, inv = stats(x)
    n1_low = (n1 * gain_ref[...]).astype(BF16)
    dn1 = mm_t(dmix[...], wqkv_ref[...])
    acc_qkv[...] += mm_tn(n1_low, dmix[...])
    return dy1 + norm_back(dn1 * gain_ref[...], n1, inv)


def attention_grads(length, live, qkv_ref, dmix, dheads, bias_ref):
    rows, width = dheads.shape
    lane = lax.broadcasted_iota(jnp.int32, (128, 128), 1)
    first = lane < HEAD
    low = first[:1].astype(BF16)
    high = 1 - low
    eye = (lane == lax.broadcasted_iota(jnp.int32, (128, 128), 0)).astype(BF16)
    same = same_pair(length)
    for g in range(rows // 128):
        bias_ref[g] = jnp.where(same & (live[g * 128 : g * 128 + 128, :] > 0), 0.0, -1e30)

    zero = jnp.zeros((128, 128), BF16)

    def both_sides(one, two):
        return jnp.concatenate(
            [jnp.concatenate([one, zero], axis=1), jnp.concatenate([zero, two], axis=1)], axis=0
        )

    def pieces(unit, part):
        g, h = unit
        return qkv_ref[pl.ds(g * 128, 128), part * width + h : part * width + h + 128]

    def scores(unit):
        g, h = unit
        k = pieces(unit, 1)
        v = pieces(unit, 2)
        do = dheads[pl.ds(g * 128, 128), h : h + 128]
        left = jnp.concatenate(
            [jnp.concatenate([k * low, v * low], axis=1), jnp.concatenate([k * high, v * high], axis=1)], axis=0
        )
        made = mm_t(left, both_sides(pieces(unit, 0) * BF16(HEAD**-0.5), do))
        return made[:, :128], made[:, 128:]

    def soft(unit, made):
        g, _ = unit
        s, dp = made
        s = s.reshape(2, 128, 128) + bias_ref[g][None]
        e = jnp.exp(s - jnp.max(s, axis=1, keepdims=True))
        p = e * (1.0 / jnp.sum(e, axis=1, keepdims=True))
        dp = dp.reshape(2, 128, 128)
        ds = p * (dp - jnp.sum(p * dp, axis=1, keepdims=True))
        return p.reshape(256, 128).astype(BF16), ds.reshape(256, 128).astype(BF16)

    def products(unit, made):
        g, h = unit
        p, ds = made
        at = pl.ds(g * 128, 128)
        do = dheads[at, h : h + 128]
        made = mm(jnp.concatenate([p, ds], axis=1), both_sides(do, pieces(unit, 0) * BF16(HEAD**-0.5)))
        dv = made[:, :128]
        dk = made[:, 128:]
        dmix[at, 2 * width + h : 2 * width + h + 128] = jnp.where(first, dv[:128], dv[128:]).astype(BF16)
        dmix[at, width + h : width + h + 128] = jnp.where(first, dk[:128], dk[128:]).astype(BF16)
        return mm_t(eye, ds).astype(BF16)

    def query(unit, ds):
        g, h = unit
        k = pieces(unit, 1)
        kbd = jnp.concatenate([k * low, k * high], axis=0)
        dmix[pl.ds(g * 128, 128), h : h + 128] = (mm(ds, kbd) * HEAD**-0.5).astype(BF16)

    staggered([scores, soft, products, query], [(g, h) for g in range(rows // 128) for h in range(0, width, 128)], 3)


def text_backward(
    plan, x, qkv, att, y1, slopes, received, lens, got, cut, dun, emb, pooled, hsum,
    gain_one, wqkv, wout, gain_two, wup, wdown, wproj, others, stat,
):
    pairs, length, width = x.shape
    rows = NB * length
    tokens = pairs * length
    ff = wup.shape[1]
    rest = (received, lens, got, dun, emb, pooled, hsum, gain_one, wqkv, wout, gain_two, wup, wdown, wproj, *others, stat)
    halves = [(ff + width + 128) // 2, ff // 2, 2 * width]
    shapes = [(half, width) for half in halves for _ in range(2)]
    return pl.pallas_call(
        functools.partial(back_kernel, cut, len(others)),
        grid_spec=pltpu.PrefetchScalarGridSpec(
            num_scalar_prefetch=1,
            grid=(pairs // NB,),
            in_specs=[ordered_pairs(x.shape), ordered(3 * width, rows), ordered(width, rows), ordered(width, rows), ordered(ff, rows)]
            + [fixed(w.shape) for w in rest],
            out_specs=[ordered_pairs(x.shape, ORDER_ALL)] + [held(shape) for shape in shapes],
            scratch_shapes=[
                pltpu.VMEM((pairs, width), F32),
                pltpu.VMEM((pairs, ff), F32),
                pltpu.VMEM((width, width), F32),
                pltpu.VMEM((ff, width), F32),
                pltpu.VMEM((rows, 3 * width), BF16),
                pltpu.VMEM((rows, width), BF16),
                pltpu.VMEM((width, ff), F32),
                pltpu.VMEM((width, width), F32),
                pltpu.VMEM((width, 3 * width), F32),
                pltpu.VMEM((rows // 128, 128, 128), F32),
                pltpu.VMEM((rows, ff), BF16),
            ],
        ),
        out_shape=[pltpu.HBM(x.shape, BF16)] + [pltpu.HBM(shape, BF16) for shape in shapes],
        compiler_params=params(BACK_LIMIT),
        cost_estimate=pl.CostEstimate(
            flops=2 * tokens * width * (10 * width + 2 * ff), bytes_accessed=24 * 2**20, transcendentals=0
        ),
        name="text_backward",
    )(plan, x, qkv, att, y1, slopes, *rest)


def flip(values, axis, bits):
    size = lax.axis_size(axis)
    return lax.ppermute(values, axis, [(k, k ^ bits) for k in range(size)])


def reduce_round(kept, axis, unit, ways, split):
    if not split:
        low = kept.astype(BF16)
        others = [flip(low, axis, p * unit).astype(F32) for p in range(1, ways)]
        return tree_sum([low.astype(F32)] + others)
    me = (lax.axis_index(axis) // unit) % ways
    pieces = kept.reshape(ways, kept.shape[0] // ways, kept.shape[1])
    total = lax.dynamic_index_in_dim(pieces, me, 0, keepdims=False)
    for p in range(1, ways):
        piece = lax.dynamic_index_in_dim(pieces, me ^ p, 0, keepdims=False)
        total = total + flip(piece.astype(BF16), axis, p * unit).astype(F32)
    return total


def gather_round(piece, axis, unit, ways, split):
    if not split:
        return piece
    return jnp.concatenate([piece] + [flip(piece, axis, p * unit) for p in range(1, ways)], axis=0)


def exchange(keep, send, rounds, before_gather=None, before_last=None):
    kept = keep.astype(F32) + flip(send, "col", 1).astype(F32)
    for one in rounds:
        kept = reduce_round(kept, *one)
    piece = kept.astype(BF16)
    if before_gather is not None:
        piece = tie(piece, before_gather)
    for k, one in enumerate(reversed(rounds)):
        if before_last is not None and k == len(rounds) - 1:
            piece = tie(piece, before_last)
        piece = gather_round(piece, *one)
    return piece, flip(piece, "col", 1)


def tie(first, *others):
    return lax.optimization_barrier((first, *others))[0]


def tree_sum(parts):
    while len(parts) > 1:
        parts = [parts[k] + parts[k + 1] for k in range(0, len(parts), 2)]
    return parts[0]


def sum_over(values, axis, unit, ways):
    return tree_sum([values] + [flip(values, axis, p * unit) for p in range(1, ways)])


def place_kernel(targets, rounds, last, ids_ref, own_ref, other_ref, *outs):
    col = ids_ref[0]
    row = ids_ref[1]
    half, width = own_ref.shape
    steps = []
    size = half
    for axis, unit, ways, split in rounds:
        if split:
            size //= ways
            steps.append((axis, unit, ways, size))
    count = half // size
    places = outs[: len(targets) - 1] + outs[-1:] if last else outs
    for other, source in enumerate((own_ref, other_ref)):

        @pl.loop(0, count)
        def _(k):
            start = ((col & 1) ^ other) * half
            left = k
            weight = count
            for axis, unit, ways, step in steps:
                weight //= ways
                digit = left // weight
                left = left - digit * weight
                index = (col if axis == "col" else row) // unit % ways
                start = start + (index ^ digit) * step
            value = source[pl.ds(pl.multiple_of(k * size, 16), size), :].astype(F32)
            for first, past, by_row, ref in [target + (ref,) for target, ref in zip(targets, places)]:

                @pl.when((start >= first) & (start < past))
                def _():
                    inside = start - first
                    if by_row:
                        ref[pl.ds(pl.multiple_of(inside, 8), size), :] = value
                    else:
                        lane = pl.multiple_of((inside // width) * width, 128)
                        ref[pl.ds(pl.multiple_of(inside % width, 8), size), pl.ds(lane, width)] = value

    if last:
        first_gain, second_gain, loss, moved, small = outs[-5:]
        first_gain[...] = small[0, :]
        second_gain[...] = small[1, :]
        lane = lax.broadcasted_iota(jnp.int32, (1, 128), 1)
        stat = small[2:3, :128]
        loss[0] = jnp.sum(jnp.where(lane == 0, stat, 0.0))
        moved[0] = jnp.sum(jnp.where(lane == 1, stat, 0.0))


def place(ids, gathered, targets, rounds, shapes, last=False):
    width = gathered[0].shape[1]
    specs = [VMEM] * len(shapes)
    made = [jax.ShapeDtypeStruct(shape, F32) for shape in shapes]
    scratch = []
    if last:
        specs = specs + [VMEM, VMEM, SMEM, SMEM]
        made = made + [jax.ShapeDtypeStruct((size,), F32) for size in (width, width, 1, 1)]
        scratch = [pltpu.VMEM((128, width), F32)]
    return pl.pallas_call(
        functools.partial(place_kernel, targets, rounds, last),
        in_specs=[SMEM, VMEM, VMEM],
        out_specs=specs,
        out_shape=made,
        scratch_shapes=scratch,
        compiler_params=params(SIM_LIMIT),
        name="place_gradients",
    )(ids, *gathered)


def body(
    image_tokens, text_tokens, lengths, pair_count, img_qkv, img_out, img_up, img_down, img_proj,
    gain_one, txt_qkv, txt_out, gain_two, txt_up, txt_down, txt_proj, log_scale,
):
    pairs, _, width = image_tokens.shape
    ff = txt_up.shape[1]
    row_index = lax.axis_index("row")
    col_index = lax.axis_index("col")
    row_count = lax.axis_size("row")
    col_count = lax.axis_size("col")
    high = col_count // 4
    cut = pairs - NB
    across = row_count - 1

    by_token = jnp.transpose(image_tokens, (1, 0, 2))
    got_images = flip(by_token[:, cut:], "row", across)
    got_texts = flip(text_tokens[cut:], "row", across)
    lens = lengths.astype(F32).reshape(pairs // QB, QB)
    got_lens = flip(lens[cut // QB :], "row", across)
    plan, rlive, tlive, scal = prepare(pair_count, log_scale, cut)
    gain_one = gain_one.reshape(1, width)
    gain_two = gain_two.reshape(1, width)

    weights = (img_qkv, img_out, img_up, img_down, img_proj)
    first_unit = image_tower(plan, by_token, None, 0, cut, cut, IMAGE_NB, 1.0, *weights)
    last_unit = lax.cond(
        plan[IMAGE_BLOCKS + cut // GROUP] > 0,
        lambda: image_tower(plan, by_token, got_images, cut, NB, cut, GROUP, 0.01, *weights),
        lambda: jnp.zeros((NB, width), BF16),
    )
    unit = jnp.concatenate([first_unit, last_unit], axis=0)
    parts = [unit] + [flip(unit, "col", 4 * p) for p in range(1, high)]
    qkv, att, y1 = text_first(plan, text_tokens, got_texts, lens, got_lens, cut, gain_one, txt_qkv, txt_out)
    parts = lax.optimization_barrier((*parts, y1))
    y1 = parts[-1]
    near = jnp.concatenate(parts[:-1], axis=0)
    beside = flip(near, "col", 2)
    core_near = flip(near, "col", 1)
    slopes, hsum, pooled, emb, text_low = text_second(
        plan, y1, lens, got_lens, cut, gain_two, txt_up, txt_down, txt_proj
    )
    images = [near, core_near, beside, flip(tie(beside, text_low), "col", 1)]
    texts = [text_low] + [flip(text_low, "row", p) for p in range(1, row_count)]
    rowsum, colsum = sim_sums(plan, scal, texts, tlive, rlive, images)
    total_col = colsum
    for p in range(1, row_count):
        other = flip(colsum, "row", p)
        total_col = total_col + jnp.concatenate([other[k ^ p : (k ^ p) + 1] for k in range(row_count)], axis=0)
    for bit in range(2, (high * 4).bit_length() - 1):
        rowsum = rowsum + flip(rowsum, "col", 1 << bit)
    rowsum = sum_over(rowsum, "col", 1, 4)
    *duns, stat = sim_grads(plan, scal, texts, tlive, rlive, rowsum, total_col, images)
    others = [flip(duns[p], "row", p) for p in range(1, row_count)]
    split_row = width * 2 % (row_count * 2 * 2 * 16) == 0
    along_row = ("row", 1, row_count, split_row)
    along_y = ("col", 2, 2, True)
    along_z = ("col", 4, 2, high % 2 == 0)
    along_far = ("col", 8, high // 2, False)
    order_a = [along_row, along_y, along_z, along_far]
    order_b = [along_y, along_z, along_row, along_far]
    order_c = [along_z, along_row, along_y, along_far]
    qkv = pltpu.with_memory_space_constraint(qkv, pltpu.HBM)
    text_grad, keep_a, send_a, keep_b, send_b, keep_c, send_c = text_backward(
        plan, text_tokens, qkv, att, y1, slopes, got_texts, lens, got_lens, cut, duns[0], emb, pooled, hsum,
        gain_one, txt_qkv, txt_out, gain_two, txt_up, txt_down, txt_proj, others, stat,
    )
    back = flip(text_grad[cut:], "row", across)
    low_half = row_index < row_count // 2
    counts = pair_count[:, col_index]
    balanced = jnp.where(low_half, counts[row_index], counts[row_index ^ across]) <= cut
    last = jnp.where(balanced, jnp.where(low_half, jnp.zeros_like(back), back), text_grad[cut:])
    text_grad = lax.dynamic_update_slice_in_dim(text_grad, last, cut, 0)
    orders = [order_a, order_b, order_c]
    targets = [
        [(0, ff, True), (ff, ff + width, True), (ff + width, ff + width + 128, True)],
        [(0, ff, False)],
        [(0, width, True), (width, 4 * width, False)],
    ]
    shapes = [[(ff, width), (width, width)], [(width, ff)], [(width, width), (width, 3 * width)]]
    placed = []
    waits = [(back, None), (None, None), (None, None)]
    for keep, send, rounds, places, sizes in zip((keep_a, keep_b, keep_c), (send_a, send_b, send_c), orders, targets, shapes):
        gathered = exchange(keep, send, rounds, *waits.pop(0))
        placed += place(plan, gathered, places, rounds, sizes, not placed)
    sum_down, sum_proj, sum_one, sum_two, loss, sum_scale, sum_up, sum_out, sum_qkv = placed
    return (
        loss, text_grad, sum_one, sum_qkv, sum_out, sum_two, sum_up, sum_down, sum_proj, sum_scale,
    )


def solution(mesh):
    return jax.shard_map(
        body,
        mesh=mesh,
        in_specs=(
            P(("row", "col"), None, None),
            P(("row", "col"), None, None),
            P(("row", "col")),
            P(),
            P(),
            P(),
            P(),
            P(),
            P(),
            P(),
            P(),
            P(),
            P(),
            P(),
            P(),
            P(),
            P(),
        ),
        out_specs=(P(), P(("row", "col"), None, None), P(), P(), P(), P(), P(), P(), P(), P()),
        check_vma=False,
    )
```

```python
import functools
import jax
import jax.numpy as jnp
from jax import lax
from jax.experimental import pallas as pl
from jax.experimental.pallas import tpu as pltpu
from jax.sharding import PartitionSpec as P

HEADS = 6
HEAD = 64
epsilon = 1e-6
F32 = jnp.float32
BF16 = jnp.bfloat16
GELU_A = 0.7978845608028654
GELU_B = 0.7978845608028654 * 0.044715
SAFE = 60.0
GROUP = 8
PITCH = 9
IMAGE_NB = 16
USE = 2
ACTIVE = 3
ORDER = 4
ORDER_ALL = 8
IMAGE_BLOCKS = 12
PLAN = 28
NB = 32
QB = 16
T1_LIMIT = 20
T2_LIMIT = 20
BACK_LIMIT = 30
SIM_LIMIT = 12


def mm(a, b):
    return lax.dot_general(a, b, (((1,), (0,)), ((), ())), preferred_element_type=F32)


def mm_t(a, b):
    return lax.dot_general(a, b, (((1,), (1,)), ((), ())), preferred_element_type=F32)


def mm_split(a, b):
    hi = a.astype(BF16)
    lo = (a - hi.astype(F32)).astype(BF16)
    return mm(hi, b) + mm(lo, b)


def column_chunks(width):
    edge = width // 2 // 256 * 256
    return ((0, edge), (edge, width))


def over(a, b):
    r = pl.reciprocal(b, approx=True)
    return a * (r * (2.0 - b * r))


def normed(v):
    c = v - jnp.mean(v, axis=-1, keepdims=True)
    return c * lax.rsqrt(jnp.mean(c * c, axis=-1, keepdims=True) + epsilon)


def unit_scale(e):
    return lax.rsqrt(jnp.sum(e * e, axis=-1, keepdims=True) + epsilon)


def lane_halves():
    lane = lax.broadcasted_iota(jnp.int32, (1, 128), 1)
    low = (lane < HEAD).astype(F32)
    return low, 1.0 - low


def image_kernel(first, cut, plan_ref, x_ref, recv_ref, wqkv_ref, wout_ref, wup_ref, wdown_ref, wproj_ref, unit_ref, qkv, att, hsum, xsum):
    step = pl.program_id(0)
    length, nb, width = x_ref.shape
    rows = length * GROUP

    @pl.when(step == 0)
    def _():
        qkv[...] = jnp.zeros_like(qkv)
        hsum[...] = jnp.zeros_like(hsum)
        xsum[...] = jnp.zeros_like(xsum)

    block = first // nb + step

    @pl.when(plan_ref[IMAGE_BLOCKS + block * (nb // GROUP)] > 0)
    def _():
        image_block(step, block, cut, plan_ref, x_ref, recv_ref, wqkv_ref, wout_ref, wup_ref, qkv, att, hsum, xsum)

    @pl.when(step == pl.num_programs(0) - 1)
    def _():
        pooled = xsum[...] * (1.0 / length) + mm_split(hsum[...] * (0.5 / length), wdown_ref[...])
        e = mm(pooled.astype(BF16), wproj_ref[...])
        unit_ref[...] = (e * unit_scale(e)).astype(BF16)


def image_block(step, block, cut, plan_ref, x_ref, recv_ref, wqkv_ref, wout_ref, wup_ref, qkv, att, hsum, xsum):
    length, nb, width = x_ref.shape
    rows = length * GROUP
    slots = qkv.shape[2] // PITCH
    tiles = width // 128
    ff = wup_ref.shape[1]
    groups = nb // GROUP
    moved = (plan_ref[USE] > 0) & (block >= cut // nb)

    def tokens(g):
        x = x_ref[...].astype(F32)
        if recv_ref is not None:
            x = jnp.where(moved, recv_ref[...].astype(F32), x)
        return x[:, g * GROUP : (g + 1) * GROUP, :].reshape(rows, width)

    low, high = lane_halves()
    key_row = lax.broadcasted_iota(jnp.int32, (2 * slots, 128), 0)
    key_lane = lax.broadcasted_iota(jnp.int32, (2 * slots, 128), 1)
    own_head = (key_row < slots) == (key_lane < HEAD)
    real = jnp.where(key_row < slots, key_row, key_row - slots) < length
    ones = jnp.where(own_head & real, 1.0, 0.0).astype(BF16)

    def pairs_of(g):
        return pl.ds(pl.multiple_of(step * nb + g * GROUP, GROUP), GROUP)

    def scores(g, p, h):
        at = pl.ds(p, slots, stride=PITCH)
        q = qkv[g, h, at, :].astype(BF16) * BF16(HEAD**-0.5)
        k = qkv[g, tiles + h, at, :]
        return mm_t(q, jnp.concatenate([k * low, k * high], axis=0).astype(BF16))

    def weighted(g, p, h, e):
        at = pl.ds(p, slots, stride=PITCH)
        v = qkv[g, 2 * tiles + h, at, :]
        vbd = jnp.concatenate([v * low, v * high], axis=0).astype(BF16)
        o = mm(e.astype(BF16), jnp.concatenate([vbd, ones], axis=1))
        att[g, h, at, :] = over(o[:, :128], o[:, 128:])

    def projected(g):
        n1 = normed(tokens(g)).astype(BF16)
        for first, last in column_chunks(3 * width):
            made = mm(n1, wqkv_ref[:, first:last])
            for c in range(first // 128, last // 128):
                here = c * 128 - first
                for t in range(length):
                    qkv[g, c, t * PITCH : t * PITCH + GROUP, :] = made[t * GROUP : (t + 1) * GROUP, here : here + 128]

    def after_attention(g):
        heads = jnp.concatenate(
            [
                jnp.concatenate([att[g, h, t * PITCH : t * PITCH + GROUP, :] for t in range(length)], axis=0)
                for h in range(tiles)
            ],
            axis=1,
        )
        x1 = tokens(g) + mm(heads.astype(BF16), wout_ref[...])
        xsum[pairs_of(g), :] = jnp.sum(x1.reshape(length, GROUP, width), axis=0)
        return normed(x1).astype(BF16)

    def gelu_sum(g, u, c):
        made = u * (1.0 + jnp.tanh(u * (GELU_A + GELU_B * (u * u))))
        hsum[pairs_of(g), pl.ds(c, 256)] = jnp.sum(made.reshape(length, GROUP, 256), axis=0)

    def feed_steps(g):
        n2 = after_attention(g)
        before = None
        for c in range(0, ff, 256):
            u = mm(n2, wup_ref[:, c : c + 256])
            if before is not None:
                gelu_sum(g, *before)
            before = (u, c)
            yield
        gelu_sum(g, *before)
        yield

    largest = jnp.zeros((slots, 2 * slots), F32)
    units = [(p, h) for p in range(GROUP) for h in range(tiles)]
    ahead = 4
    feed = iter(())
    projected(0)
    for g in range(groups):
        s_list, e_list = {}, {}
        for k in range(len(units) + 2 * ahead):
            if k < len(units):
                s_list[k] = scores(g, *units[k])
            if 0 <= k - ahead < len(units):
                s = s_list.pop(k - ahead)
                largest = jnp.maximum(largest, jnp.abs(s))
                e_list[k - ahead] = jnp.exp(s)
            if 0 <= k - 2 * ahead < len(units):
                weighted(g, *units[k - 2 * ahead], e_list.pop(k - 2 * ahead))
            if k % 4 == 2:
                next(feed, None)
            if k == len(units) // 2 and g + 1 < groups:
                projected(g + 1)
        for _ in feed:
            pass
        feed = feed_steps(g)
    for _ in feed:
        pass

    @pl.when(jnp.logical_not(jnp.max(largest) <= SAFE))
    def _():
        key = lax.broadcasted_iota(jnp.int32, (1, 2 * slots), 1)
        in_low = key < slots
        for_low = key < length
        for_high = (key >= slots) & (key < slots + length)
        @pl.loop(0, groups)
        def _(g):
            @pl.loop(0, GROUP)
            def _(p):
                @pl.loop(0, tiles)
                def _(h):
                    s = scores(g, p, h)
                    top_low = jnp.max(jnp.where(for_low, s, -1e30), axis=1, keepdims=True)
                    top_high = jnp.max(jnp.where(for_high, s, -1e30), axis=1, keepdims=True)
                    s = jnp.where(for_low | for_high, s, -1e30) - jnp.where(in_low, top_low, top_high)
                    weighted(g, p, h, jnp.exp(s))

        for g in range(groups):
            n2 = after_attention(g)

            @pl.loop(0, ff // 256)
            def _(c):
                at = pl.multiple_of(c * 256, 256)
                gelu_sum(g, mm(n2, wup_ref[:, pl.ds(at, 256)]), at)


def fixed(shape):
    zeros = (0,) * len(shape)
    return pl.BlockSpec(shape, lambda *_: zeros, pipeline_mode=pl.Buffered(1))


def image_tower(plan, tokens, received, first, count, cut, nb, cost, wqkv, wout, wup, wdown, wproj):
    length, _, width = tokens.shape
    slots = -(-length // 8) * 8
    ff = wup.shape[1]
    weights = (wqkv, wout, wup, wdown, wproj)
    at = first // nb
    specs = [pl.BlockSpec((length, nb, width), lambda i, plan: (0, at + i, 0))]
    if received is None:
        kernel = lambda plan_ref, x_ref, *refs: image_kernel(first, cut, plan_ref, x_ref, None, *refs)
        arrays = (tokens,)
    else:
        kernel = functools.partial(image_kernel, first, cut)
        last = received.shape[1] // nb - 1
        specs.append(
            pl.BlockSpec((length, nb, width), lambda i, plan: (0, jnp.clip(at + i - cut // nb, 0, last), 0))
        )
        arrays = (tokens, received)
    return pl.pallas_call(
        kernel,
        grid_spec=pltpu.PrefetchScalarGridSpec(
            num_scalar_prefetch=1,
            grid=(count // nb,),
            in_specs=specs + [fixed(w.shape) for w in weights],
            out_specs=pl.BlockSpec((count, width), lambda i, plan: (0, 0)),
            scratch_shapes=[
                pltpu.VMEM((nb // GROUP, 3 * width // 128, slots * PITCH, 128), F32),
                pltpu.VMEM((nb // GROUP, width // 128, slots * PITCH, 128), F32),
                pltpu.VMEM((count, ff), F32),
                pltpu.VMEM((count, width), F32),
            ],
        ),
        out_shape=jax.ShapeDtypeStruct((count, width), BF16),
        compiler_params=pltpu.CompilerParams(vmem_limit_bytes=60 * 2**20),
        cost_estimate=pl.CostEstimate(
            flops=int(cost * 2 * count * length * width * (4 * width + ff)),
            bytes_accessed=int(cost * (count * length * width * 2 + 4 * 2**20)),
            transcendentals=int(cost * count * length * ff),
        ),
        name="image_block",
    )(plan, *arrays, *weights)


def mm_tn(a, b):
    return lax.dot_general(a, b, (((0,), (0,)), ((), ())), preferred_element_type=F32)


def stats(v):
    c = v - jnp.mean(v, axis=-1, keepdims=True)
    inv = lax.rsqrt(jnp.mean(c * c, axis=-1, keepdims=True) + epsilon)
    return c * inv, inv


def norm_back(g, n, inv):
    return inv * (
        g - jnp.mean(g, axis=-1, keepdims=True) - n * jnp.mean(g * n, axis=-1, keepdims=True)
    )


def staggered(stages, units, ahead):
    kept = [dict() for _ in stages]
    for k in range(len(units) + (len(stages) - 1) * ahead):
        for at, stage in enumerate(stages):
            u = k - at * ahead
            if 0 <= u < len(units):
                made = stage(units[u], *([kept[at - 1].pop(u)] if at else []))
                kept[at][u] = made


def same_pair(length):
    row = lax.broadcasted_iota(jnp.int32, (128, 128), 0) // length
    lane = lax.broadcasted_iota(jnp.int32, (128, 128), 1) // length
    return row == lane


SMEM = pl.BlockSpec(memory_space=pltpu.SMEM)
VMEM = pl.BlockSpec(memory_space=pltpu.VMEM)


def params(limit=60):
    return pltpu.CompilerParams(vmem_limit_bytes=limit * 2**20)


def as_column(row):
    size = row.shape[1]
    diagonal = lax.broadcasted_iota(jnp.int32, (size, size), 0) == lax.broadcasted_iota(jnp.int32, (size, size), 1)
    return jnp.sum(jnp.where(diagonal, row, 0.0), axis=1, keepdims=True)


def as_row(col):
    size = col.shape[0]
    diagonal = lax.broadcasted_iota(jnp.int32, (size, size), 0) == lax.broadcasted_iota(jnp.int32, (size, size), 1)
    return jnp.sum(jnp.where(diagonal, col, 0.0), axis=0, keepdims=True)


def prepare_kernel(cut, count_ref, scale_ref, plan_ref, rlive_ref, tlive_ref, scal_ref):
    rows, cols = count_ref.shape
    across = rows - 1
    col = lax.axis_index("col")
    row = lax.axis_index("row")

    def limits(r, c):
        n = count_ref[r, c]
        other = count_ref[r ^ across, c]
        low = r < rows // 2
        balanced = jnp.where(low, n, other) <= cut
        return n, jnp.where(balanced, jnp.where(low, other, 0), n), low & balanced

    def mask(r, c):
        first, last, _ = limits(r, c)
        slot = lax.broadcasted_iota(jnp.int32, (1, 128), 1)
        return jnp.where(slot < jnp.where(slot < cut, first, last), 1.0, 0.0)

    for c in range(cols):
        rlive_ref[c : c + 1, :] = mask(row, c)
    for p in range(rows):
        tlive_ref[p : p + 1, :] = mask(row ^ p, col)
    first, last, use = limits(row, col)
    limit = lambda start: first if start < cut else last
    plan_ref[0] = col
    plan_ref[1] = row
    plan_ref[USE] = use.astype(jnp.int32)
    blocks = 128 // NB
    active = [(b * NB < limit(b * NB)).astype(jnp.int32) for b in range(blocks)]
    count = sum(active)
    before = jnp.int32(0)
    for b in range(blocks):
        plan_ref[ORDER_ALL + jnp.where(active[b] > 0, before, count + b - before)] = b
        before = before + active[b]
    for i in range(blocks):
        plan_ref[ORDER + i] = plan_ref[ORDER_ALL + jnp.minimum(i, count - 1)]
    plan_ref[ACTIVE] = count
    for b in range(128 // GROUP):
        plan_ref[IMAGE_BLOCKS + b] = (b * GROUP < limit(b * GROUP)).astype(jnp.int32)
    total = jnp.int32(0)
    for r in range(rows):
        for c in range(cols):
            total = total + count_ref[r, c]
    index = lax.broadcasted_iota(jnp.int32, (8, 128), 0)
    scal_ref[...] = jnp.where(index == 0, jnp.exp(jnp.full((8, 128), scale_ref[0], F32)), 0.5 / jnp.full((8, 128), total, jnp.int32).astype(F32))


def prepare(pair_count, log_scale, cut):
    rows, cols = pair_count.shape
    return pl.pallas_call(
        functools.partial(prepare_kernel, cut),
        in_specs=[SMEM] * 2,
        out_specs=[SMEM, VMEM, VMEM, VMEM],
        out_shape=[
            jax.ShapeDtypeStruct((PLAN,), jnp.int32),
            jax.ShapeDtypeStruct((cols, 128), F32),
            jax.ShapeDtypeStruct((rows, 128), F32),
            jax.ShapeDtypeStruct((8, 128), F32),
        ],
        name="prepare",
    )(pair_count, log_scale)


def lengths_of(plan_ref, cut, part, lens_ref, got_ref):
    moved = (plan_ref[USE] > 0) & (part * QB >= cut)
    got = got_ref[pl.ds(jnp.maximum(part - cut // QB, 0), 1), :]
    return as_column(jnp.where(moved, got, lens_ref[pl.ds(part, 1), :]))


def block_lengths(plan_ref, cut, block, lens_ref, got_ref):
    parts = [lengths_of(plan_ref, cut, block * (NB // QB) + k, lens_ref, got_ref) for k in range(NB // QB)]
    return jnp.concatenate(parts, axis=0)


def all_lengths(plan_ref, cut, lens_ref, got_ref):
    parts = [lengths_of(plan_ref, cut, b, lens_ref, got_ref) for b in range(lens_ref.shape[0])]
    return jnp.concatenate(parts, axis=0)


def live_pick(lens, rows):
    pairs = lens.shape[0]
    length = rows // pairs
    token = lax.broadcasted_iota(jnp.int32, (pairs, rows), 1)
    own = token // length == lax.broadcasted_iota(jnp.int32, (pairs, rows), 0)
    return jnp.where(own & ((token % length).astype(F32) < lens), 1.0, 0.0)


def text_tokens_of(plan_ref, cut, block, x_ref, recv_ref):
    nb, length, width = x_ref.shape
    moved = (plan_ref[USE] > 0) & (block * nb >= cut)
    x = jnp.where(moved, recv_ref[...].astype(F32), x_ref[...].astype(F32))
    return x.reshape(nb * length, width)


def ordered(width, rows):
    return pl.BlockSpec((rows, width), lambda i, plan: (plan[ORDER + i], 0))


def ordered_pairs(shape, order=ORDER):
    return pl.BlockSpec((NB,) + shape[1:], lambda i, plan: (plan[order + i], 0, 0))


def held(shape):
    zeros = (0,) * len(shape)
    return pl.BlockSpec(shape, lambda i, plan: zeros)


def text_first_kernel(cut, plan_ref, x_ref, recv_ref, lens_ref, got_ref, gain_ref, wqkv_ref, wout_ref, qkv_ref, att_ref, y1_ref):
    step = pl.program_id(0)
    block = plan_ref[ORDER + step]

    @pl.when(step < plan_ref[ACTIVE])
    def _():
        x = text_tokens_of(plan_ref, cut, block, x_ref, recv_ref)
        lens = block_lengths(plan_ref, cut, block, lens_ref, got_ref)
        text_attention(x, lens, x_ref.shape[1], gain_ref, wqkv_ref, wout_ref, qkv_ref, att_ref, y1_ref)


def text_attention(x, lens, length, gain_ref, wqkv_ref, wout_ref, qkv_ref, att_ref, y1_ref):
    rows, width = x.shape
    n1 = (normed(x) * gain_ref[...]).astype(BF16)
    for first, last in column_chunks(3 * width):
        qkv_ref[:, first:last] = mm(n1, wqkv_ref[:, first:last]).astype(BF16)
    lane = lax.broadcasted_iota(jnp.int32, (128, 128), 1)
    low = (lane[:1] < HEAD).astype(BF16)
    high = 1 - low
    half = lax.broadcasted_iota(jnp.int32, (256, 128), 0) < 128
    ones = jnp.where(half == (lax.broadcasted_iota(jnp.int32, (256, 128), 1) < HEAD), 1.0, 0.0).astype(BF16)
    same = same_pair(length)
    live = jnp.sum(live_pick(lens, rows), axis=0, keepdims=True)
    bias = {g: jnp.where(same & (live[:, g : g + 128] > 0), 0.0, -1e30) for g in range(0, rows, 128)}

    def scores(unit):
        g, h = unit
        q = qkv_ref[g : g + 128, h : h + 128] * BF16(HEAD**-0.5)
        k = qkv_ref[g : g + 128, width + h : width + h + 128]
        return mm_t(q, jnp.concatenate([k * low, k * high], axis=0))

    def expo(unit, s):
        one = bias[unit[0]]
        parts = [s[:, :128] + one, s[:, 128:] + one]
        return jnp.concatenate([jnp.exp(p - jnp.max(p, axis=1, keepdims=True)) for p in parts], axis=1).astype(BF16)

    def weighted(unit, e):
        g, h = unit
        v = qkv_ref[g : g + 128, 2 * width + h : 2 * width + h + 128]
        vbd = jnp.concatenate([v * low, v * high], axis=0)
        o = mm(e, jnp.concatenate([vbd, ones], axis=1))
        att_ref[g : g + 128, h : h + 128] = over(o[:, :128], o[:, 128:]).astype(BF16)

    staggered([scores, expo, weighted], [(g, h) for g in range(0, rows, 128) for h in range(0, width, 128)], 2)
    y1_ref[...] = x + mm(att_ref[...], wout_ref[...])


def text_first(plan, x, received, lens, got, cut, gain_one, wqkv, wout):
    pairs, length, width = x.shape
    rows = NB * length
    tokens = pairs * length
    rest = (received, lens, got, gain_one, wqkv, wout)
    wide = [(3 * width, BF16), (width, BF16), (width, F32)]
    return pl.pallas_call(
        functools.partial(text_first_kernel, cut),
        grid_spec=pltpu.PrefetchScalarGridSpec(
            num_scalar_prefetch=1,
            grid=(pairs // NB,),
            in_specs=[ordered_pairs(x.shape)] + [fixed(w.shape) for w in rest],
            out_specs=[ordered(w, rows) for w, _ in wide],
        ),
        out_shape=[(pltpu.HBM if k == 0 else jax.ShapeDtypeStruct)((tokens, w), kind) for k, (w, kind) in enumerate(wide)],
        compiler_params=params(T1_LIMIT),
        cost_estimate=pl.CostEstimate(flops=2 * tokens * width * 5 * width, bytes_accessed=12 * 2**20, transcendentals=0),
        name="text_attention",
    )(plan, x, *rest)


def text_second_kernel(
    cut, plan_ref, y1_ref, lens_ref, got_ref, gain_two_ref, wup_ref, wdown_ref, wproj_ref,
    slope_ref, hsum_ref, pooled_ref, emb_ref, low_ref, ysum,
):
    step = pl.program_id(0)
    block = plan_ref[ORDER + step]

    @pl.when(step == 0)
    def _():
        hsum_ref[...] = jnp.zeros_like(hsum_ref)
        ysum[...] = jnp.zeros_like(ysum)

    @pl.when(step < plan_ref[ACTIVE])
    def _():
        rows = y1_ref.shape[0]
        y1 = y1_ref[...]
        pick = live_pick(block_lengths(plan_ref, cut, block, lens_ref, got_ref), rows).astype(BF16)
        pair = pl.ds(pl.multiple_of(block * NB, NB), NB)
        y1_hi = y1.astype(BF16)
        ysum[pair, :] = mm(pick, y1_hi) + mm(pick, (y1 - y1_hi.astype(F32)).astype(BF16))
        n2 = (normed(y1) * gain_two_ref[...]).astype(BF16)

        live = mm_tn(pick, jnp.ones((NB, 128), BF16))
        live = jnp.concatenate([live, live], axis=1)

        def gelu_parts(u, c):
            square = u * u
            t = 1.0 + jnp.tanh(u * (GELU_A + GELU_B * square))
            half = 0.5 * u
            hsum_ref[pair, c : c + 256] = mm(pick, (half * t).astype(BF16))
            d = t * (0.5 + (2.0 - t) * (half * (GELU_A + (3.0 * GELU_B) * square)))
            slope_ref[:, c : c + 256] = (d * live).astype(BF16)

        in_chunks(n2, wup_ref, gelu_parts)

    @pl.when(step == pl.num_programs(0) - 1)
    def _():
        inv_len = 1.0 / all_lengths(plan_ref, cut, lens_ref, got_ref)
        pooled = (ysum[...] * inv_len + mm_split(hsum_ref[...] * inv_len, wdown_ref[...])).astype(BF16)
        pooled_ref[...] = pooled
        e = mm(pooled, wproj_ref[...])
        emb_ref[...] = e
        low_ref[...] = (e * unit_scale(e)).astype(BF16)


def in_chunks(left, right_ref, use):
    before = None
    for c in range(0, right_ref.shape[1], 256):
        u = mm(left, right_ref[:, c : c + 256])
        if before is not None:
            use(*before)
        before = (u, c)
    use(*before)


def text_second(plan, y1, lens, got, cut, gain_two, wup, wdown, wproj):
    tokens, width = y1.shape
    pairs = lens.size
    rows = NB * tokens // pairs
    ff = wup.shape[1]
    rest = (lens, got, gain_two, wup, wdown, wproj)
    flat = [((pairs, ff), F32), ((pairs, width), BF16), ((pairs, width), F32), ((pairs, width), BF16)]
    return pl.pallas_call(
        functools.partial(text_second_kernel, cut),
        grid_spec=pltpu.PrefetchScalarGridSpec(
            num_scalar_prefetch=1,
            grid=(pairs // NB,),
            in_specs=[ordered(width, rows)] + [fixed(w.shape) for w in rest],
            out_specs=[ordered(ff, rows)] + [held(shape) for shape, _ in flat],
            scratch_shapes=[pltpu.VMEM((pairs, width), F32)],
        ),
        out_shape=[jax.ShapeDtypeStruct((tokens, ff), BF16)] + [jax.ShapeDtypeStruct(shape, kind) for shape, kind in flat],
        compiler_params=params(T2_LIMIT),
        cost_estimate=pl.CostEstimate(flops=2 * tokens * width * ff, bytes_accessed=12 * 2**20, transcendentals=tokens * ff),
        name="text_pool",
    )(plan, y1, *rest)


def image_groups(image_refs):
    for j, ref in enumerate(image_refs):
        yield j, ref.shape[0] // 128, len(image_refs), ref[...]


def sums_kernel(rows, ids_ref, scal_ref, tlive_ref, rlive_ref, *refs):
    text_refs = refs[:rows]
    image_refs = refs[rows:-2]
    rowsum_ref, colsum_ref = refs[-2:]
    me = ids_ref[0]
    scale = scal_ref[:1, :1]
    text = jnp.concatenate([ref[...] for ref in text_refs], axis=0)
    tlive = jnp.concatenate([as_column(tlive_ref[p : p + 1, :]) for p in range(rows)], axis=0)
    col = jnp.zeros((rows * 128, 1), F32)
    for j, high, low, images in image_groups(image_refs):
        e = jnp.exp(scale * mm_t(text, images)) * tlive
        total = jnp.sum(e, axis=0, keepdims=True)
        kept = jnp.zeros((rows * 128, 128), F32)
        for i in range(high):
            at = pl.ds(me ^ (low * i + j), 1)
            rowsum_ref[at, :] = total[:, i * 128 : i * 128 + 128]
            kept = kept + e[:, i * 128 : i * 128 + 128] * rlive_ref[at, :]
        col = col + jnp.sum(kept, axis=1, keepdims=True)
    for p in range(rows):
        colsum_ref[p : p + 1, :] = as_row(col[p * 128 : p * 128 + 128])


def sim_sums(ids, scal, texts, tlive, rlive, images):
    cols = rlive.shape[0]
    rows = len(texts)
    return pl.pallas_call(
        functools.partial(sums_kernel, rows),
        in_specs=[SMEM] + [VMEM] * (3 + rows + len(images)),
        out_specs=[VMEM, VMEM],
        out_shape=[jax.ShapeDtypeStruct((cols, 128), F32), jax.ShapeDtypeStruct((rows, 128), F32)],
        compiler_params=params(SIM_LIMIT),
        cost_estimate=pl.CostEstimate(
            flops=2 * rows * 128 * cols * 128 * 384, bytes_accessed=cols * 128 * 768, transcendentals=rows * cols * 128 * 128
        ),
        name="similarity_sums",
    )(ids, scal, tlive, rlive, *texts, *images)


def grad_kernel(rows, ids_ref, scal_ref, tlive_ref, rlive_ref, rowsum_ref, colsum_ref, *refs):
    text_refs = refs[:rows]
    image_refs = refs[rows : -rows - 1]
    dun_refs = refs[-rows - 1 : -1]
    stat_ref = refs[-1]
    me = ids_ref[0]
    scale = scal_ref[:1, :1]
    inv = scal_ref[1:2, :1]
    text = jnp.concatenate([ref[...] for ref in text_refs], axis=0)
    tlive = jnp.concatenate([as_column(tlive_ref[p : p + 1, :]) for p in range(rows)], axis=0)
    col = jnp.concatenate([as_column(colsum_ref[p : p + 1, :]) for p in range(rows)], axis=0)
    col = jnp.where(tlive > 0, col, 1.0)
    col_inv = inv / col
    total = jnp.zeros(text.shape, F32)
    moved = jnp.zeros((1, 128), F32)
    for j, high, low, images in image_groups(image_refs):
        s = scale * mm_t(text, images)
        e = jnp.exp(s) * tlive
        at = [pl.ds(me ^ (low * i + j), 1) for i in range(high)]
        rlive = jnp.concatenate([rlive_ref[one, :] for one in at], axis=1)
        row_inv = jnp.concatenate([inv / rowsum_ref[one, :] for one in at], axis=1)
        ds = (e * rlive) * (row_inv + col_inv)
        by_lane = jnp.sum(ds * s, axis=0, keepdims=True)
        for i in range(high):
            moved = moved + by_lane[:, i * 128 : i * 128 + 128]
        total = total + mm((scale * ds).astype(BF16), images)
        if j == 0:
            mine = images[:128].astype(F32)
    own_live = tlive[:128]
    cosine = jnp.sum(mine * text[:128].astype(F32), axis=1, keepdims=True)
    live_cosine = jnp.sum(cosine * own_live, axis=0, keepdims=True)
    at = pl.ds(me, 1)
    logs = jnp.sum(jnp.log(rowsum_ref[at, :]) * rlive_ref[at, :], axis=1, keepdims=True)
    logs = logs + jnp.sum(jnp.log(col[:128]) * own_live, axis=0, keepdims=True)
    loss = inv * (logs - 2.0 * scale * live_cosine)
    scale_part = jnp.sum(moved, axis=1, keepdims=True) - 2.0 * inv * scale * live_cosine
    dun_refs[0][...] = total[:128] + (scale * (-2.0 * inv * own_live)).astype(BF16).astype(F32) * mine
    for p in range(1, rows):
        dun_refs[p][...] = total[p * 128 : p * 128 + 128].astype(BF16)
    lane = lax.broadcasted_iota(jnp.int32, (8, 128), 1)
    stat_ref[...] = jnp.where(lane == 0, loss, jnp.where(lane == 1, scale_part, 0.0))


def sim_grads(ids, scal, texts, tlive, rlive, rowsum, colsum, images):
    cols = rlive.shape[0]
    rows = len(texts)
    return pl.pallas_call(
        functools.partial(grad_kernel, rows),
        in_specs=[SMEM] + [VMEM] * (5 + rows + len(images)),
        out_specs=[VMEM] * (rows + 1),
        out_shape=[jax.ShapeDtypeStruct(text.shape, BF16 if k else F32) for k, text in enumerate(texts)] + [jax.ShapeDtypeStruct((8, 128), F32)],
        compiler_params=params(SIM_LIMIT),
        cost_estimate=pl.CostEstimate(
            flops=4 * rows * 128 * cols * 128 * 384, bytes_accessed=cols * 128 * 768, transcendentals=rows * cols * 128 * 128
        ),
        name="similarity_grads",
    )(ids, scal, tlive, rlive, rowsum, colsum, *texts, *images)


def write_halves(core, blocks, keep_ref, send_ref):
    half = len(blocks) // 2
    size = blocks[0].shape[0]

    def put(first, second):
        for at, (kept, sent) in enumerate(zip(first, second)):
            keep_ref[at * size : (at + 1) * size, :] = kept.astype(BF16)
            send_ref[at * size : (at + 1) * size, :] = sent.astype(BF16)

    @pl.when(core == 0)
    def _():
        put(blocks[:half], blocks[half:])

    @pl.when(core != 0)
    def _():
        put(blocks[half:], blocks[:half])


def back_kernel(
    cut, others, plan_ref, x_ref, qkv_ref, att_ref, y1_ref, slope_ref, recv_ref, lens_ref, got_ref,
    dun_ref, emb_ref, pooled_ref, hsum_ref, gain_ref, wqkv_ref, wout_ref, gain_two_ref, wup_ref, wdown_ref, wproj_ref, *refs,
):
    other_refs = refs[:others]
    stat_ref = refs[others]
    grad_ref, keep_a, send_a, keep_b, send_b, keep_c, send_c = refs[others + 1 : others + 8]
    dyp, dhp, dproj, ddown, dmix, dheads, acc_up, acc_out, acc_qkv, bias_ref, du_ref = refs[others + 8 :]
    step = pl.program_id(0)
    block = plan_ref[ORDER + step]
    active = step < plan_ref[ACTIVE]
    width = dun_ref.shape[1]
    ff = hsum_ref.shape[1]

    @pl.when(step == 0)
    def _():
        acc_up[...] = jnp.zeros_like(acc_up)
        acc_out[...] = jnp.zeros_like(acc_out)
        acc_qkv[...] = jnp.zeros_like(acc_qkv)
        g = dun_ref[...]
        for other in other_refs:
            g = g + other[...].astype(F32)
        e = emb_ref[...]
        inv = unit_scale(e)
        t = e * inv
        demb = (inv * (g - t * jnp.sum(g * t, axis=-1, keepdims=True))).astype(BF16)
        dproj[...] = mm_tn(pooled_ref[...], demb)
        back = mm_t(demb, wproj_ref[...]) * (1.0 / all_lengths(plan_ref, cut, lens_ref, got_ref))
        dyp[...] = back
        db = back.astype(BF16)
        dhp[...] = mm_t(db, wdown_ref[...])
        h = hsum_ref[...]
        hi = h.astype(BF16)
        lo = (h - hi.astype(F32)).astype(BF16)
        ddown[...] = mm_tn(hi, db) + mm_tn(lo, db)

    @pl.when(active)
    def _():
        x = text_tokens_of(plan_ref, cut, block, x_ref, recv_ref)
        lens = block_lengths(plan_ref, cut, block, lens_ref, got_ref)
        grad = back_block(
            block, x, lens, x_ref.shape[1], qkv_ref, att_ref, y1_ref, slope_ref, gain_ref, wqkv_ref, wout_ref,
            gain_two_ref, wup_ref, dyp, dhp, dmix, dheads, acc_up, acc_out, acc_qkv, bias_ref, du_ref,
        )
        grad_ref[...] = grad.astype(BF16).reshape(grad_ref.shape)

    @pl.when(jnp.logical_not(active))
    def _():
        grad_ref[...] = jnp.zeros_like(grad_ref)

    @pl.when(step == pl.num_programs(0) - 1)
    def _():
        core = plan_ref[0] & 1
        index = lax.broadcasted_iota(jnp.int32, (128, width), 0)
        stat = jnp.concatenate([stat_ref[:1, :]] * (width // 128), axis=1)
        by_qkv = jnp.sum(acc_qkv[...] * wqkv_ref[...].astype(F32), axis=1, keepdims=True)
        by_up = jnp.sum(acc_up[...] * wup_ref[...].astype(F32), axis=1, keepdims=True)
        first = as_row(by_qkv) / gain_ref[...]
        second = as_row(by_up) / gain_two_ref[...]
        small = jnp.where(index == 0, first, jnp.where(index == 1, second, jnp.where(index == 2, stat, 0.0)))
        blocks = [ddown[at : at + 128, :] for at in range(0, ff, 128)]
        blocks += [dproj[at : at + 128, :] for at in range(0, width, 128)]
        write_halves(core, blocks + [small], keep_a, send_a)
        write_halves(core, [acc_up[:, c : c + width] for c in range(0, ff, width)], keep_b, send_b)
        blocks = [acc_out[...]] + [acc_qkv[:, c * width : (c + 1) * width] for c in range(3)]
        write_halves(core, blocks, keep_c, send_c)


def back_block(
    block, x, lens, length, qkv_ref, att_ref, y1_ref, slope_ref, gain_ref, wqkv_ref, wout_ref,
    gain_two_ref, wup_ref, dyp, dhp, dmix, dheads, acc_up, acc_out, acc_qkv, bias_ref, du_ref,
):
    rows, width = x.shape
    ff = wup_ref.shape[1]
    pair = pl.ds(pl.multiple_of(block * NB, NB), NB)

    def spread(values):
        return jnp.broadcast_to(values[:, None, :], (NB, length, values.shape[1])).reshape(rows, values.shape[1])

    n2, inv = stats(y1_ref[...])
    n2_low = (n2 * gain_two_ref[...]).astype(BF16)
    for c in range(0, ff, width):
        at = slice(c, c + width)
        du_ref[:, at] = (spread(dhp[pair, at]) * slope_ref[:, at].astype(F32)).astype(BF16)
    dn2 = mm_t(du_ref[...], wup_ref[...])
    acc_up[...] += mm_tn(n2_low, du_ref[...])
    live = mm_tn(live_pick(lens, rows).astype(BF16), jnp.ones((NB, 128), BF16))
    dy1 = spread(dyp[pair, :]) * jnp.concatenate([live] * (width // 128), axis=1)
    dy1 = dy1 + norm_back(dn2 * gain_two_ref[...], n2, inv)
    da = dy1.astype(BF16)
    acc_out[...] += mm_tn(att_ref[...], da)
    dheads[...] = mm_t(da, wout_ref[...]).astype(BF16)
    attention_grads(length, live, qkv_ref, dmix, dheads, bias_ref)
    n1, inv = stats(x)
    n1_low = (n1 * gain_ref[...]).astype(BF16)
    dn1 = mm_t(dmix[...], wqkv_ref[...])
    acc_qkv[...] += mm_tn(n1_low, dmix[...])
    return dy1 + norm_back(dn1 * gain_ref[...], n1, inv)


def attention_grads(length, live, qkv_ref, dmix, dheads, bias_ref):
    rows, width = dheads.shape
    lane = lax.broadcasted_iota(jnp.int32, (128, 128), 1)
    first = lane < HEAD
    low = first[:1].astype(BF16)
    high = 1 - low
    eye = (lane == lax.broadcasted_iota(jnp.int32, (128, 128), 0)).astype(BF16)
    same = same_pair(length)
    for g in range(rows // 128):
        bias_ref[g] = jnp.where(same & (live[g * 128 : g * 128 + 128, :] > 0), 0.0, -1e30)

    zero = jnp.zeros((128, 128), BF16)

    def both_sides(one, two):
        return jnp.concatenate(
            [jnp.concatenate([one, zero], axis=1), jnp.concatenate([zero, two], axis=1)], axis=0
        )

    def pieces(unit, part):
        g, h = unit
        return qkv_ref[pl.ds(g * 128, 128), part * width + h : part * width + h + 128]

    def scores(unit):
        g, h = unit
        k = pieces(unit, 1)
        v = pieces(unit, 2)
        do = dheads[pl.ds(g * 128, 128), h : h + 128]
        left = jnp.concatenate(
            [jnp.concatenate([k * low, v * low], axis=1), jnp.concatenate([k * high, v * high], axis=1)], axis=0
        )
        made = mm_t(left, both_sides(pieces(unit, 0) * BF16(HEAD**-0.5), do))
        return made[:, :128], made[:, 128:]

    def soft(unit, made):
        g, _ = unit
        s, dp = made
        s = s.reshape(2, 128, 128) + bias_ref[g][None]
        e = jnp.exp(s - jnp.max(s, axis=1, keepdims=True))
        p = e * (1.0 / jnp.sum(e, axis=1, keepdims=True))
        dp = dp.reshape(2, 128, 128)
        ds = p * (dp - jnp.sum(p * dp, axis=1, keepdims=True))
        return p.reshape(256, 128).astype(BF16), ds.reshape(256, 128).astype(BF16)

    def products(unit, made):
        g, h = unit
        p, ds = made
        at = pl.ds(g * 128, 128)
        do = dheads[at, h : h + 128]
        made = mm(jnp.concatenate([p, ds], axis=1), both_sides(do, pieces(unit, 0) * BF16(HEAD**-0.5)))
        dv = made[:, :128]
        dk = made[:, 128:]
        dmix[at, 2 * width + h : 2 * width + h + 128] = jnp.where(first, dv[:128], dv[128:]).astype(BF16)
        dmix[at, width + h : width + h + 128] = jnp.where(first, dk[:128], dk[128:]).astype(BF16)
        return mm_t(eye, ds).astype(BF16)

    def query(unit, ds):
        g, h = unit
        k = pieces(unit, 1)
        kbd = jnp.concatenate([k * low, k * high], axis=0)
        dmix[pl.ds(g * 128, 128), h : h + 128] = (mm(ds, kbd) * HEAD**-0.5).astype(BF16)

    staggered([scores, soft, products, query], [(g, h) for g in range(rows // 128) for h in range(0, width, 128)], 3)


def text_backward(
    plan, x, qkv, att, y1, slopes, received, lens, got, cut, dun, emb, pooled, hsum,
    gain_one, wqkv, wout, gain_two, wup, wdown, wproj, others, stat,
):
    pairs, length, width = x.shape
    rows = NB * length
    tokens = pairs * length
    ff = wup.shape[1]
    rest = (received, lens, got, dun, emb, pooled, hsum, gain_one, wqkv, wout, gain_two, wup, wdown, wproj, *others, stat)
    halves = [(ff + width + 128) // 2, ff // 2, 2 * width]
    shapes = [(half, width) for half in halves for _ in range(2)]
    return pl.pallas_call(
        functools.partial(back_kernel, cut, len(others)),
        grid_spec=pltpu.PrefetchScalarGridSpec(
            num_scalar_prefetch=1,
            grid=(pairs // NB,),
            in_specs=[ordered_pairs(x.shape), ordered(3 * width, rows), ordered(width, rows), ordered(width, rows), ordered(ff, rows)]
            + [fixed(w.shape) for w in rest],
            out_specs=[ordered_pairs(x.shape, ORDER_ALL)] + [held(shape) for shape in shapes],
            scratch_shapes=[
                pltpu.VMEM((pairs, width), F32),
                pltpu.VMEM((pairs, ff), F32),
                pltpu.VMEM((width, width), F32),
                pltpu.VMEM((ff, width), F32),
                pltpu.VMEM((rows, 3 * width), BF16),
                pltpu.VMEM((rows, width), BF16),
                pltpu.VMEM((width, ff), F32),
                pltpu.VMEM((width, width), F32),
                pltpu.VMEM((width, 3 * width), F32),
                pltpu.VMEM((rows // 128, 128, 128), F32),
                pltpu.VMEM((rows, ff), BF16),
            ],
        ),
        out_shape=[pltpu.HBM(x.shape, BF16)] + [pltpu.HBM(shape, BF16) for shape in shapes],
        compiler_params=params(BACK_LIMIT),
        cost_estimate=pl.CostEstimate(
            flops=2 * tokens * width * (10 * width + 2 * ff), bytes_accessed=24 * 2**20, transcendentals=0
        ),
        name="text_backward",
    )(plan, x, qkv, att, y1, slopes, *rest)


def flip(values, axis, bits):
    size = lax.axis_size(axis)
    return lax.ppermute(values, axis, [(k, k ^ bits) for k in range(size)])


def reduce_round(kept, axis, unit, ways, split):
    if not split:
        low = kept.astype(BF16)
        others = [flip(low, axis, p * unit).astype(F32) for p in range(1, ways)]
        return tree_sum([low.astype(F32)] + others)
    me = (lax.axis_index(axis) // unit) % ways
    pieces = kept.reshape(ways, kept.shape[0] // ways, kept.shape[1])
    total = lax.dynamic_index_in_dim(pieces, me, 0, keepdims=False)
    for p in range(1, ways):
        piece = lax.dynamic_index_in_dim(pieces, me ^ p, 0, keepdims=False)
        total = total + flip(piece.astype(BF16), axis, p * unit).astype(F32)
    return total


def gather_round(piece, axis, unit, ways, split):
    if not split:
        return piece
    return jnp.concatenate([piece] + [flip(piece, axis, p * unit) for p in range(1, ways)], axis=0)


def exchange(keep, send, rounds, before_gather=None, before_last=None):
    kept = keep.astype(F32) + flip(send, "col", 1).astype(F32)
    for one in rounds:
        kept = reduce_round(kept, *one)
    piece = kept.astype(BF16)
    if before_gather is not None:
        piece = tie(piece, before_gather)
    for k, one in enumerate(reversed(rounds)):
        if before_last is not None and k == len(rounds) - 1:
            piece = tie(piece, before_last)
        piece = gather_round(piece, *one)
    return piece, flip(piece, "col", 1)


def tie(first, *others):
    return lax.optimization_barrier((first, *others))[0]


def tree_sum(parts):
    while len(parts) > 1:
        parts = [parts[k] + parts[k + 1] for k in range(0, len(parts), 2)]
    return parts[0]


def sum_over(values, axis, unit, ways):
    return tree_sum([values] + [flip(values, axis, p * unit) for p in range(1, ways)])


def place_kernel(targets, rounds, last, ids_ref, own_ref, other_ref, *outs):
    col = ids_ref[0]
    row = ids_ref[1]
    half, width = own_ref.shape
    steps = []
    size = half
    for axis, unit, ways, split in rounds:
        if split:
            size //= ways
            steps.append((axis, unit, ways, size))
    count = half // size
    places = outs[: len(targets) - 1] + outs[-1:] if last else outs
    for other, source in enumerate((own_ref, other_ref)):

        @pl.loop(0, count)
        def _(k):
            start = ((col & 1) ^ other) * half
            left = k
            weight = count
            for axis, unit, ways, step in steps:
                weight //= ways
                digit = left // weight
                left = left - digit * weight
                index = (col if axis == "col" else row) // unit % ways
                start = start + (index ^ digit) * step
            value = source[pl.ds(pl.multiple_of(k * size, 16), size), :].astype(F32)
            for first, past, by_row, ref in [target + (ref,) for target, ref in zip(targets, places)]:

                @pl.when((start >= first) & (start < past))
                def _():
                    inside = start - first
                    if by_row:
                        ref[pl.ds(pl.multiple_of(inside, 8), size), :] = value
                    else:
                        lane = pl.multiple_of((inside // width) * width, 128)
                        ref[pl.ds(pl.multiple_of(inside % width, 8), size), pl.ds(lane, width)] = value

    if last:
        first_gain, second_gain, loss, moved, small = outs[-5:]
        first_gain[...] = small[0, :]
        second_gain[...] = small[1, :]
        lane = lax.broadcasted_iota(jnp.int32, (1, 128), 1)
        stat = small[2:3, :128]
        loss[0] = jnp.sum(jnp.where(lane == 0, stat, 0.0))
        moved[0] = jnp.sum(jnp.where(lane == 1, stat, 0.0))


def place(ids, gathered, targets, rounds, shapes, last=False):
    width = gathered[0].shape[1]
    specs = [VMEM] * len(shapes)
    made = [jax.ShapeDtypeStruct(shape, F32) for shape in shapes]
    scratch = []
    if last:
        specs = specs + [VMEM, VMEM, SMEM, SMEM]
        made = made + [jax.ShapeDtypeStruct((size,), F32) for size in (width, width, 1, 1)]
        scratch = [pltpu.VMEM((128, width), F32)]
    return pl.pallas_call(
        functools.partial(place_kernel, targets, rounds, last),
        in_specs=[SMEM, VMEM, VMEM],
        out_specs=specs,
        out_shape=made,
        scratch_shapes=scratch,
        compiler_params=params(SIM_LIMIT),
        name="place_gradients",
    )(ids, *gathered)


def body(
    image_tokens, text_tokens, lengths, pair_count, img_qkv, img_out, img_up, img_down, img_proj,
    gain_one, txt_qkv, txt_out, gain_two, txt_up, txt_down, txt_proj, log_scale,
):
    pairs, _, width = image_tokens.shape
    ff = txt_up.shape[1]
    row_index = lax.axis_index("row")
    col_index = lax.axis_index("col")
    row_count = lax.axis_size("row")
    col_count = lax.axis_size("col")
    high = col_count // 4
    cut = pairs - NB
    across = row_count - 1

    by_token = jnp.transpose(image_tokens, (1, 0, 2))
    got_images = flip(by_token[:, cut:], "row", across)
    got_texts = flip(text_tokens[cut:], "row", across)
    lens = lengths.astype(F32).reshape(pairs // QB, QB)
    got_lens = flip(lens[cut // QB :], "row", across)
    plan, rlive, tlive, scal = prepare(pair_count, log_scale, cut)
    gain_one = gain_one.reshape(1, width)
    gain_two = gain_two.reshape(1, width)

    weights = (img_qkv, img_out, img_up, img_down, img_proj)
    first_unit = image_tower(plan, by_token, None, 0, cut, cut, IMAGE_NB, 1.0, *weights)
    last_unit = lax.cond(
        plan[IMAGE_BLOCKS + cut // GROUP] > 0,
        lambda: image_tower(plan, by_token, got_images, cut, NB, cut, GROUP, 0.01, *weights),
        lambda: jnp.zeros((NB, width), BF16),
    )
    unit = jnp.concatenate([first_unit, last_unit], axis=0)
    parts = [unit] + [flip(unit, "col", 4 * p) for p in range(1, high)]
    qkv, att, y1 = text_first(plan, text_tokens, got_texts, lens, got_lens, cut, gain_one, txt_qkv, txt_out)
    parts = lax.optimization_barrier((*parts, y1))
    y1 = parts[-1]
    near = jnp.concatenate(parts[:-1], axis=0)
    beside = flip(near, "col", 2)
    core_near = flip(near, "col", 1)
    slopes, hsum, pooled, emb, text_low = text_second(
        plan, y1, lens, got_lens, cut, gain_two, txt_up, txt_down, txt_proj
    )
    images = [near, core_near, beside, flip(tie(beside, text_low), "col", 1)]
    texts = [text_low] + [flip(text_low, "row", p) for p in range(1, row_count)]
    rowsum, colsum = sim_sums(plan, scal, texts, tlive, rlive, images)
    total_col = colsum
    for p in range(1, row_count):
        other = flip(colsum, "row", p)
        total_col = total_col + jnp.concatenate([other[k ^ p : (k ^ p) + 1] for k in range(row_count)], axis=0)
    for bit in range(2, (high * 4).bit_length() - 1):
        rowsum = rowsum + flip(rowsum, "col", 1 << bit)
    rowsum = sum_over(rowsum, "col", 1, 4)
    *duns, stat = sim_grads(plan, scal, texts, tlive, rlive, rowsum, total_col, images)
    others = [flip(duns[p], "row", p) for p in range(1, row_count)]
    split_row = width * 2 % (row_count * 2 * 2 * 16) == 0
    along_row = ("row", 1, row_count, split_row)
    along_y = ("col", 2, 2, True)
    along_z = ("col", 4, 2, high % 2 == 0)
    along_far = ("col", 8, high // 2, False)
    order_a = [along_row, along_y, along_z, along_far]
    order_b = [along_y, along_z, along_row, along_far]
    order_c = [along_z, along_row, along_y, along_far]
    qkv = pltpu.with_memory_space_constraint(qkv, pltpu.HBM)
    text_grad, keep_a, send_a, keep_b, send_b, keep_c, send_c = text_backward(
        plan, text_tokens, qkv, att, y1, slopes, got_texts, lens, got_lens, cut, duns[0], emb, pooled, hsum,
        gain_one, txt_qkv, txt_out, gain_two, txt_up, txt_down, txt_proj, others, stat,
    )
    back = flip(text_grad[cut:], "row", across)
    low_half = row_index < row_count // 2
    counts = pair_count[:, col_index]
    balanced = jnp.where(low_half, counts[row_index], counts[row_index ^ across]) <= cut
    last = jnp.where(balanced, jnp.where(low_half, jnp.zeros_like(back), back), text_grad[cut:])
    text_grad = lax.dynamic_update_slice_in_dim(text_grad, last, cut, 0)
    orders = [order_a, order_b, order_c]
    targets = [
        [(0, ff, True), (ff, ff + width, True), (ff + width, ff + width + 128, True)],
        [(0, ff, False)],
        [(0, width, True), (width, 4 * width, False)],
    ]
    shapes = [[(ff, width), (width, width)], [(width, ff)], [(width, width), (width, 3 * width)]]
    placed = []
    waits = [(back, None), (None, None), (None, None)]
    for keep, send, rounds, places, sizes in zip((keep_a, keep_b, keep_c), (send_a, send_b, send_c), orders, targets, shapes):
        gathered = exchange(keep, send, rounds, *waits.pop(0))
        placed += place(plan, gathered, places, rounds, sizes, not placed)
    sum_down, sum_proj, sum_one, sum_two, loss, sum_scale, sum_up, sum_out, sum_qkv = placed
    return (
        loss, text_grad, sum_one, sum_qkv, sum_out, sum_two, sum_up, sum_down, sum_proj, sum_scale,
    )


def solution(mesh):
    return jax.shard_map(
        body,
        mesh=mesh,
        in_specs=(
            P(("row", "col"), None, None),
            P(("row", "col"), None, None),
            P(("row", "col")),
            P(),
            P(),
            P(),
            P(),
            P(),
            P(),
            P(),
            P(),
            P(),
            P(),
            P(),
            P(),
            P(),
            P(),
        ),
        out_specs=(P(), P(("row", "col"), None, None), P(), P(), P(), P(), P(), P(), P(), P()),
        check_vma=False,
    )
```
